32 devices in a mesh: dp: 16 (over z, x, core), blk: 2 (over y).
Axes of the slice: x: 2, y: 2, z: 4, core: 2. Of those that a mesh axis runs over, the one named last changes fastest.
Arguments:
- patches: bfloat16 [16, 1024, 768], P('dp', 'blk'), may hold values from -6 to 6
- segments: int32 [16, 1024], P('dp'), may hold values from 0 to 34, as said below
- entry_gain: float32 [768], replicated, may hold values from 0.1 to 1.9
- entry_shift: float32 [768], replicated, may hold values from -3 to 3
- joint_weight: bfloat16 [768, 2304], replicated, may hold values from -0.21875 to 0.21875
- joint_bias: float32 [1536], replicated, may hold values from -3 to 3
- output_weight: bfloat16 [768, 768], replicated, may hold values from -0.625 to 0.625
- output_bias: float32 [768], replicated, may hold values from -3 to 3
- middle_gain: float32 [768], replicated, may hold values from 0.1 to 1.9
- middle_shift: float32 [768], replicated, may hold values from -3 to 3
- expand_weight: bfloat16 [768, 3072], replicated, may hold values from -0.21875 to 0.21875
- expand_bias: float32 [3072], replicated, may hold values from -3 to 3
- reduce_weight: bfloat16 [3072, 768], replicated, may hold values from -0.15625 to 0.15625
- reduce_bias: float32 [768], replicated, may hold values from -3 to 3
- cotangent: bfloat16 [16, 1024, 768], P('dp', 'blk'), may hold values from -6 to 6
Outputs:
- outputs: bfloat16 [16, 1024, 768], P('dp', 'blk')
- input_gradient: bfloat16 [16, 1024, 768], P('dp', 'blk')
- entry_gain_gradient: float32 [768], P('dp')
- entry_shift_gradient: float32 [768], P('dp')
- joint_weight_gradient: float32 [768, 2304], P('dp')
- joint_bias_gradient: float32 [1536], P('dp')
- output_weight_gradient: float32 [768, 768], P('dp')
- output_bias_gradient: float32 [768], P('dp')
- middle_gain_gradient: float32 [768], P('dp')
- middle_shift_gradient: float32 [768], P('dp')
- expand_weight_gradient: float32 [768, 3072], P('dp')
- expand_bias_gradient: float32 [3072], P('dp')
- reduce_weight_gradient: float32 [3072, 768], P('dp')
- reduce_bias_gradient: float32 [768], P('dp')
The draws below stay inside these ranges and needn't reach their ends.
Inputs may be any that keep to these rules, and one draw needn't show every extreme that they name: `segments`: images are numbered 1, 2, ... in order and lie contiguously from position 0, each of 30 to 98 positions; the padding, 0, fills the end of every row with 1 to 98 positions.
All inputs are finite; a program needn't handle non-finite values.
Results may differ from the reference program's by a relative error of at most 0.019.
Values may be sent and summed in bfloat16 or wider, within the bound.
A program may use at most 192 MiB of HBM per device.

```python
import math
import jax
import jax.numpy as jnp
from jax import lax

D = 768
HEADS = 12
HD = 64
FF = 3072
ROW = 1024
ROWS = 16


def draw_segments(key, part):
    count = ROW // 30 + 1
    lengths = jax.random.randint(jax.random.fold_in(key, 1), (ROWS, count), 30, 99)
    packed_row = jax.random.randint(jax.random.fold_in(key, 2), (), 0, ROWS)
    rows_index = jnp.arange(ROWS)[:, None]
    lengths = jnp.where(rows_index == packed_row, 30, lengths)
    bounds = jnp.cumsum(lengths, axis=1)
    placed = jnp.sum((bounds <= ROW - 1).astype(jnp.int32), axis=1)
    places = jnp.arange(ROW)
    images = jnp.sum((bounds[:, None, :] <= places[None, :, None]).astype(jnp.int32), axis=2)
    return jnp.where(images < placed[:, None], images + 1, 0).astype(jnp.int32)


def strengthened(array, stream_key, source, target, blocks, factor):
    owner, partner = [(jnp.arange(array.shape[dim]) // (array.shape[dim] // blocks)).reshape([-1 if axis == dim else 1 for axis in range(array.ndim)]) for dim in (source, target)]
    chosen = jax.random.permutation(stream_key, blocks)[partner]
    strong = (owner == chosen) | (owner == (partner + blocks // 2) % blocks)
    return jnp.where(strong, factor * array, array)


def levels(key, shape, split, least, high):
    def one(position, parts):
        heights = jax.random.uniform(jax.random.fold_in(jax.random.fold_in(key, 6), position), (parts,), jnp.float32, least / len(split), high / len(split))
        return jnp.repeat(jnp.exp(heights), shape[position] // parts).reshape((-1,) + (1,) * (len(shape) - position - 1))

    level = one(*split[0])
    for cut in split[1:]:
        level = level * one(*cut)
    return level


def noise(stream_key, dims, scale, bound, pieces=(), dtype=jnp.bfloat16):
    array = jax.random.normal(stream_key, dims, jnp.float32) * scale
    if len(pieces) > 0:
        array = levels(stream_key, dims, pieces, -0.22, 0.18) * array
    return jnp.clip(array, min=-bound, max=bound).astype(dtype)


def noise_with(stream_key, dims, deviation, most, split, heavy, held_as=jnp.bfloat16):
    drawn = deviation * jax.random.normal(stream_key, dims, jnp.float32)
    if split:
        drawn = drawn * levels(stream_key, dims, split, -0.22, 0.18)
    return jnp.clip(strengthened(drawn, jax.random.fold_in(stream_key, 3), *heavy), -most, most).astype(held_as)


def setup_inputs(seed: int = 0) -> dict:
    arg_keys = jax.random.split(jax.random.key(seed), 16)
    patches = noise(arg_keys[0], (ROWS, ROW, D), 1.0, 6.0, ((0, 16), (1, 2)))
    segments = draw_segments(jax.random.fold_in(arg_keys[15], 71), 0)
    entry_gain = jnp.clip(1.0 + 0.18 * jax.random.normal(arg_keys[2], (D,), jnp.float32), 0.1, 1.9)
    entry_shift = noise(arg_keys[3], (D,), 0.5, 3.0, (), jnp.float32)
    joint_weight = noise(arg_keys[4], (D, 3 * D), D ** -0.5, 0.21875)
    joint_bias = noise(arg_keys[5], (2 * D,), 0.5, 3.0, (), jnp.float32)
    output_weight = noise(arg_keys[6], (D, D), (D // 8) ** -0.5, 0.625)
    output_bias = noise(arg_keys[7], (D,), 0.5, 3.0, (), jnp.float32)
    middle_gain = jnp.clip(1.0 + 0.18 * jax.random.normal(arg_keys[8], (D,), jnp.float32), 0.1, 1.9)
    middle_shift = noise(arg_keys[9], (D,), 0.5, 3.0, (), jnp.float32)
    expand_weight = noise(arg_keys[10], (D, FF), D ** -0.5, 0.21875)
    expand_bias = noise(arg_keys[11], (FF,), 0.5, 3.0, (), jnp.float32)
    reduce_weight = noise(arg_keys[12], (FF, D), (FF // 2) ** -0.5, 0.15625)
    reduce_bias = noise(arg_keys[13], (D,), 0.5, 3.0, (), jnp.float32)
    cotangent = noise_with(arg_keys[14], (ROWS, ROW, D), 1.0, 6.0, ((0, 16), (1, 2)), (0, 2, 16, 2.0))
    return dict(patches=patches, segments=segments, entry_gain=entry_gain, entry_shift=entry_shift, joint_weight=joint_weight, joint_bias=joint_bias, output_weight=output_weight, output_bias=output_bias, middle_gain=middle_gain, middle_shift=middle_shift, expand_weight=expand_weight, expand_bias=expand_bias, reduce_weight=reduce_weight, reduce_bias=reduce_bias, cotangent=cotangent)


@jax.custom_vjp
def low(v):
    return lax.optimization_barrier(v.astype(jnp.bfloat16)).astype(jnp.float32)

@jax.custom_vjp
def low_back(v):
    return v

def low_keep(v):
    return (low(v), None)

def low_pass(kept, grad):
    return (grad,)

def back_keep(v):
    return (v, None)

def back_low(kept, grad):
    return (low(grad),)
low.defvjp(low_keep, low_pass)
low_back.defvjp(back_keep, back_low)
highest = lax.Precision.HIGHEST

def normalize(values, gain, shift):
    average = lax.optimization_barrier(jnp.mean(values, axis=-1, keepdims=True))
    centred = values - average
    spread = lax.optimization_barrier(jnp.mean(centred * centred, axis=-1, keepdims=True))
    return centred * lax.rsqrt(spread + 1e-06) * gain + shift

def attend_rows(query_block, query_segments, key_heads, value_heads, key_segments):
    raw_scores = low_back(jnp.einsum('qhd,khd->hqk', query_block, key_heads, precision=highest))
    scores = raw_scores * HD ** (-0.5)
    allowed = query_segments[:, None] == key_segments[None, :]
    scores = jnp.where(allowed[None], scores, -1e+30)
    shares = low(jax.nn.softmax(scores, axis=-1))
    return jnp.einsum('hqk,khd->qhd', shares, value_heads, precision=highest)

def row_forward(row_input, row_segments, params):
    entry_gain, entry_shift, joint_weight, joint_bias, output_weight, output_bias, middle_gain, middle_shift, expand_weight, expand_bias, reduce_weight, reduce_bias = params
    length = row_input.shape[0]
    width = row_input.shape[1]
    normed = low(normalize(row_input, entry_gain, entry_shift))
    joined = low_back(jnp.dot(normed, joint_weight, precision=highest))
    queries = low(joined[:, :width] + joint_bias[:width]).reshape(length, HEADS, HD)
    key_heads = low(joined[:, width:2 * width]).reshape(length, HEADS, HD)
    value_heads = low(joined[:, 2 * width:] + joint_bias[width:]).reshape(length, HEADS, HD)
    block = math.gcd(length, 512)
    blocks = length // block

    def one_block(paired):
        return attend_rows(paired[0], paired[1], key_heads, value_heads, row_segments)
    attended = lax.map(jax.checkpoint(one_block), (queries.reshape(blocks, block, HEADS, HD), row_segments.reshape(blocks, block)))
    mixed = low_back(low(attended.reshape(length, width)))
    middle = row_input + low_back(jnp.dot(mixed, output_weight, precision=highest)) + output_bias
    normed_two = low(normalize(middle, middle_gain, middle_shift))
    hidden = low_back(jnp.dot(normed_two, expand_weight, precision=highest)) + expand_bias
    activated = low(jax.nn.gelu(hidden, approximate=False))
    return middle + jnp.dot(activated, reduce_weight, precision=highest) + reduce_bias

def reference(patches, segments, entry_gain, entry_shift, joint_weight, joint_bias, output_weight, output_bias, middle_gain, middle_shift, expand_weight, expand_bias, reduce_weight, reduce_bias, cotangent):
    params = tuple((weight.astype(jnp.float32) for weight in (entry_gain, entry_shift, joint_weight, joint_bias, output_weight, output_bias, middle_gain, middle_shift, expand_weight, expand_bias, reduce_weight, reduce_bias)))

    def per_row(totals, row_items):
        row_input, row_segments, row_cotangent = row_items

        def forward(inputs, weights):
            return row_forward(inputs, row_segments, weights)
        result, pullback = jax.vjp(forward, row_input.astype(jnp.float32), params)
        input_grads, param_grads = pullback(row_cotangent.astype(jnp.float32))
        totals = jax.tree.map(lambda first, second: first + second, totals, param_grads)
        return (totals, (result.astype(jnp.bfloat16), input_grads.astype(jnp.bfloat16)))
    zeroed = jax.tree.map(jnp.zeros_like, params)
    totals, (outputs, input_gradient) = lax.scan(per_row, zeroed, (patches, segments, cotangent))
    return (outputs, input_gradient, totals[0], totals[1], totals[2], totals[3], totals[4], totals[5], totals[6], totals[7], totals[8], totals[9], totals[10], totals[11])
```

```python
import functools
import jax
import jax.numpy as jnp
from jax import lax
from jax.experimental import pallas as pl
from jax.experimental.pallas import tpu as pltpu
from jax.sharding import PartitionSpec as P

MESH = pl.DeviceIdType.MESH
CHUNKS = 18
BF = jnp.bfloat16
F32 = jnp.float32


class Grid:
    def __init__(self, dp, blk, width):
        self.A = 4
        self.B = dp // 8
        self.Y = blk
        self.dp = dp
        self.R = width // dp
        self.ny = 2 if blk == 2 else 0
        self.nx = 4 - self.ny


def comm_scratch(g):
    A, B, Y, R, nx, ny = g.A, g.B, g.Y, g.R, g.nx, g.ny
    shapes = dict(
        r0=pltpu.VMEM((CHUNKS, 4, B, A, R, 128), BF),
        rx=pltpu.VMEM((CHUNKS, B - 1, nx, A, R, 128), BF),
        rz=pltpu.VMEM((CHUNKS, A - 1, nx, R, 128), BF),
        ryx=pltpu.VMEM((CHUNKS, Y, nx, R, 128), BF),
        s_core=pltpu.SemaphoreType.DMA((2, CHUNKS)),
        s_x=pltpu.SemaphoreType.DMA((2, CHUNKS, B - 1)),
        s_z=pltpu.SemaphoreType.DMA((2, CHUNKS, A - 1)),
        s_yx=pltpu.SemaphoreType.DMA((2, CHUNKS, Y - 1)),
    )
    if ny:
        shapes.update(
            ry=pltpu.VMEM((CHUNKS, B, A, R, 128), BF),
            rx2=pltpu.VMEM((CHUNKS, B - 1, A, R, 128), BF),
            rz2=pltpu.VMEM((CHUNKS, A - 1, R, 128), BF),
            rag=pltpu.VMEM((CHUNKS, 2, R, 128), BF),
            s_y=pltpu.SemaphoreType.DMA((2, CHUNKS)),
            s_x2=pltpu.SemaphoreType.DMA((2, CHUNKS, B - 1)),
            s_z2=pltpu.SemaphoreType.DMA((2, CHUNKS, A - 1)),
            s_ag=pltpu.SemaphoreType.DMA((2, CHUNKS)),
        )
    return shapes


class Comm:
    def __init__(self, g, G, slots, refs, emit):
        self.g, self.G, self.slots, self.emit = g, G, slots, emit
        self.__dict__.update(refs)
        dp = lax.axis_index("dp")
        self.y = lax.axis_index("blk")
        self.c = dp % 2
        self.b = (dp // 2) % g.B
        self.a = dp // (2 * g.B)

    def dev(self, a=None, b=None, c=None, y=None):
        a = self.a if a is None else a
        b = self.b if b is None else b
        c = self.c if c is None else c
        y = self.y if y is None else y
        return ((a * self.g.B + b) * 2 + c, y)

    def partners(self):
        g = self.g
        return (
            [self.dev(c=1 - self.c)]
            + [self.dev(b=(self.b + k) % g.B) for k in range(1, g.B)]
            + [self.dev(a=(self.a + k) % g.A) for k in range(1, g.A)]
            + [self.dev(y=(self.y + k) % g.Y) for k in range(1, g.Y)]
        )

    def barrier(self):
        sem = pltpu.get_barrier_semaphore()
        others = self.partners()
        for other in others:
            pl.semaphore_signal(sem, inc=1, device_id=other, device_id_type=MESH)
        pl.semaphore_wait(sem, len(others))

    def copy(self, src, dst, sems, index, device):
        return pltpu.make_async_remote_copy(
            src_ref=src,
            dst_ref=dst,
            send_sem=sems.at[(0,) + index],
            recv_sem=sems.at[(1,) + index],
            device_id=device,
            device_id_type=MESH,
        )

    def stage0(self, j):
        s = j % self.slots
        return [self.copy(self.G.at[s, 1 - self.c], self.r0.at[j], self.s_core, (j,), self.dev(c=1 - self.c))]

    def stage1(self, j):
        g, s = self.g, j % self.slots
        out = []
        for k in range(1, g.B):
            other = (self.b + k) % g.B
            out.append(
                self.copy(
                    self.G.at[s, self.c, pl.ds(0, g.nx), other],
                    self.rx.at[j, k - 1],
                    self.s_x,
                    (j, k - 1),
                    self.dev(b=other),
                )
            )
        if g.ny:
            out.append(
                self.copy(
                    self.G.at[s, self.c, g.nx + 1 - self.y], self.ry.at[j], self.s_y, (j,), self.dev(y=1 - self.y)
                )
            )
        return out

    def stage2(self, j):
        g, s = self.g, j % self.slots
        out = []
        for k in range(1, g.A):
            other = (self.a + k) % g.A
            out.append(
                self.copy(
                    self.G.at[s, self.c, pl.ds(0, g.nx), self.b, other],
                    self.rz.at[j, k - 1],
                    self.s_z,
                    (j, k - 1),
                    self.dev(a=other),
                )
            )
        if g.ny:
            for k in range(1, g.B):
                other = (self.b + k) % g.B
                out.append(
                    self.copy(
                        self.G.at[s, self.c, g.nx + self.y, other],
                        self.rx2.at[j, k - 1],
                        self.s_x2,
                        (j, k - 1),
                        self.dev(b=other),
                    )
                )
        return out

    def stage3(self, j):
        g, s = self.g, j % self.slots
        out = []
        for k in range(1, g.Y):
            other = (self.y + k) % g.Y
            out.append(
                self.copy(
                    self.ryx.at[j, self.y], self.ryx.at[j, self.y], self.s_yx, (j, k - 1), self.dev(y=other)
                )
            )
        if g.ny:
            for k in range(1, g.A):
                other = (self.a + k) % g.A
                out.append(
                    self.copy(
                        self.G.at[s, self.c, g.nx + self.y, self.b, other],
                        self.rz2.at[j, k - 1],
                        self.s_z2,
                        (j, k - 1),
                        self.dev(a=other),
                    )
                )
        return out

    def stage4(self, j):
        if not self.g.ny:
            return []
        return [self.copy(self.rag.at[j, self.y], self.rag.at[j, self.y], self.s_ag, (j,), self.dev(y=1 - self.y))]

    def after0(self, j):
        s = j % self.slots
        g = self.g

        def add(i, _):
            col, b = i // g.B, i % g.B
            mine = self.G.at[s, self.c, col, b]
            mine[...] = mine[...] + self.r0[j, col, b]
            return 0

        lax.fori_loop(0, 4 * g.B, add, 0)

    def sum_into(self, mine, parts):
        total = mine[...].astype(F32)
        for part in parts:
            total = total + part.astype(F32)
        mine[...] = total.astype(BF)

    def after1(self, j):
        g, s = self.g, j % self.slots
        for col in range(g.nx):
            self.sum_into(
                self.G.at[s, self.c, col, self.b], [self.rx[j, k, col] for k in range(g.B - 1)]
            )
        if g.ny:
            for b in range(g.B):
                self.sum_into(self.G.at[s, self.c, g.nx + self.y, b], [self.ry[j, b]])

    def after2(self, j):
        g, s = self.g, j % self.slots
        total = self.G[s, self.c, pl.ds(0, g.nx), self.b, self.a].astype(F32)
        for k in range(g.A - 1):
            total = total + self.rz[j, k].astype(F32)
        self.ryx[j, self.y] = total.astype(BF)
        if g.ny:
            self.sum_into(
                self.G.at[s, self.c, g.nx + self.y, self.b], [self.rx2[j, k] for k in range(g.B - 1)]
            )

    def after3(self, j):
        g, s = self.g, j % self.slots
        total = self.ryx[j, 0].astype(F32)
        for k in range(1, g.Y):
            total = total + self.ryx[j, k].astype(F32)
        for col in range(g.nx):
            self.emit(j, col, total[col])
        if g.ny:
            total = self.G[s, self.c, g.nx + self.y, self.b, self.a].astype(F32)
            for k in range(g.A - 1):
                total = total + self.rz2[j, k].astype(F32)
            self.rag[j, self.y] = total.astype(BF)

    def after4(self, j):
        for k in range(self.g.ny):
            self.emit(j, self.g.nx + k, self.rag[j, k].astype(F32))

    def start(self, stage, j):
        for copy in (self.stage0, self.stage1, self.stage2, self.stage3, self.stage4)[stage](j):
            copy.start()

    def finish(self, stage, j):
        for copy in (self.stage0, self.stage1, self.stage2, self.stage3, self.stage4)[stage](j):
            copy.wait()
        (self.after0, self.after1, self.after2, self.after3, self.after4)[stage](j)
        if stage < 4:
            self.start(stage + 1, j)

    def advance(self, t, first=0, last=CHUNKS):
        for stage in range(4, -1, -1):
            j = t - stage
            if isinstance(j, int):
                if first <= j < last:
                    self.finish(stage, j)
            else:

                @pl.when((j >= first) & (j < last))
                def _(stage=stage, j=j):
                    self.finish(stage, j)


HEADS = 12
HD = 64


def emit_to(g, j_ref, o_ref, e_ref, r_ref):
    R = g.R

    def emit(j, col, value):
        @pl.when(j < 6)
        def _():
            e_ref[:, pl.ds(pl.multiple_of(j * 512 + col * 128, 128), 128)] = value

        @pl.when((j >= 6) & (j < 12))
        def _():
            r_ref[pl.ds(col * R, R), pl.ds(pl.multiple_of((j - 6) * 128, 128), 128)] = value

        @pl.when(j >= 12)
        def _():
            at = pl.multiple_of((j - 12) * 128, 128)
            if col < 3:
                j_ref[:, pl.ds(pl.multiple_of(col * 768 + at, 128), 128)] = value
            else:
                o_ref[:, pl.ds(at, 128)] = value

    return emit


def reduce_kernel(g, names, chunks, j_ref, o_ref, e_ref, r_ref, G, load, *scratch):
    refs = dict(zip(names, scratch))
    comm = Comm(g, G, CHUNKS, refs, emit_to(g, j_ref, o_ref, e_ref, r_ref))

    def fetch(j):
        return pltpu.make_async_copy(chunks.at[j], G.at[j], load.at[j])

    def start_fetch(j, _):
        fetch(j).start()
        return 0

    lax.fori_loop(0, CHUNKS, start_fetch, 0)
    comm.barrier()

    def feed(j, _):
        fetch(j).wait()
        comm.start(0, j)
        return 0

    lax.fori_loop(0, 2, feed, 0)

    def step(t, _):
        @pl.when(t + 2 < CHUNKS)
        def _():
            feed(t + 2, 0)

        comm.advance(t)
        return 0

    lax.fori_loop(0, CHUNKS + 4, step, 0)


def reduce_weights(g, chunks):
    shapes = comm_scratch(g)
    names = tuple(shapes)
    R = g.R
    return pl.pallas_call(
        functools.partial(reduce_kernel, g, names),
        out_shape=(
            jax.ShapeDtypeStruct((R, 2304), F32),
            jax.ShapeDtypeStruct((R, 768), F32),
            jax.ShapeDtypeStruct((R, 3072), F32),
            jax.ShapeDtypeStruct((4 * R, 768), F32),
        ),
        in_specs=[pl.BlockSpec(memory_space=pl.ANY)],
        out_specs=[pl.BlockSpec(memory_space=pltpu.VMEM)] * 4,
        scratch_shapes=[
            pltpu.VMEM((CHUNKS, 2, 4, g.B, g.A, R, 128), BF),
            pltpu.SemaphoreType.DMA((CHUNKS,)),
            *shapes.values(),
        ],
        compiler_params=pltpu.CompilerParams(
            collective_id=0, has_side_effects=True, vmem_limit_bytes=60 << 20
        ),
    )(chunks)


def with_halo(cells, sides, width):
    for axis, dim in sides:
        count = lax.axis_size(axis)
        ends = count - 1
        head = lax.slice_in_dim(cells, 0, width, axis=dim)
        tail = lax.slice_in_dim(cells, cells.shape[dim] - width, cells.shape[dim], axis=dim)
        cells = jnp.concatenate(
            [
                lax.ppermute(tail, axis, [(i, (i + 1) % count) for i in range(ends)]),
                cells,
                lax.ppermute(head, axis, [((i + 1) % count, i) for i in range(ends)]),
            ],
            axis=dim,
        )
    return cells


def from_behind(block, axis, distance):
    devices = range(lax.axis_size(axis))
    route = [(i - distance, i) for i in devices if i - distance in devices]
    return lax.ppermute(block, axis, route)


def normalize(values, gain, shift):
    average = jnp.mean(values, axis=-1, keepdims=True)
    centred = values - average
    spread = jnp.mean(centred * centred, axis=-1, keepdims=True)
    return centred * lax.rsqrt(spread + 1e-06) * gain + shift


def exact_gelu(inner):
    return jax.nn.gelu(inner, approximate=False)


def local(
    patches,
    segments,
    entry_gain,
    entry_shift,
    joint_weight,
    joint_bias,
    output_weight,
    output_bias,
    middle_gain,
    middle_shift,
    expand_weight,
    expand_bias,
    reduce_weight,
    reduce_bias,
    cotangent,
):
    row_input = patches[0].astype(jnp.float32)
    length = row_input.shape[0]
    width = row_input.shape[1]
    reach = 97
    extent = length + 2 * reach
    factor = HD ** (-0.5)
    start = lax.axis_index("blk") * length
    own_segments = lax.dynamic_slice_in_dim(segments[0], start, length)
    padded_segments = jnp.pad(segments[0], (reach, reach), constant_values=-1)
    near_segments = lax.dynamic_slice_in_dim(padded_segments, start, extent)
    allowed = (own_segments[:, None] == near_segments[None, :])[None]
    normed, entry_back = jax.vjp(normalize, row_input, entry_gain, entry_shift)
    normed_low = normed.astype(jnp.bfloat16)
    joined = jnp.dot(normed_low, joint_weight, preferred_element_type=jnp.float32)
    queries = (joined[:, :width] + joint_bias[:width]).astype(jnp.bfloat16)
    key_rows = joined[:, width : 2 * width].astype(jnp.bfloat16)
    value_rows = (joined[:, 2 * width :] + joint_bias[width:]).astype(jnp.bfloat16)
    query_heads = queries.reshape(length, HEADS, HD)
    stacked = jnp.concatenate([key_rows, value_rows], axis=1)
    extended = with_halo(stacked, (("blk", 0),), reach)

    def scores_for(near):
        near_keys = near[:, :width].reshape(extent, HEADS, HD)
        raw_scores = (
            jnp.einsum("qhd,khd->hqk", query_heads, near_keys, preferred_element_type=jnp.float32)
            * factor
        )
        return jnp.where(allowed, raw_scores, -1e30)

    scores = scores_for(extended)
    peak = jnp.max(scores, axis=-1)
    total = jnp.sum(jnp.exp(scores - peak[:, :, None]), axis=-1)
    logsum = peak + jnp.log(total)
    probs = jnp.exp(scores - logsum[:, :, None]).astype(jnp.bfloat16)
    near_values = extended[:, width:].reshape(extent, HEADS, HD)
    attended = jnp.einsum("hqk,khd->qhd", probs, near_values, preferred_element_type=jnp.float32)
    mixed = attended.reshape(length, width).astype(jnp.bfloat16)
    middle = (
        row_input + jnp.dot(mixed, output_weight, preferred_element_type=jnp.float32) + output_bias
    )
    normed_two, middle_back = jax.vjp(normalize, middle, middle_gain, middle_shift)
    normed_two_low = normed_two.astype(jnp.bfloat16)
    hidden = (
        jnp.dot(normed_two_low, expand_weight, preferred_element_type=jnp.float32) + expand_bias
    )
    activated, gelu_back = jax.vjp(exact_gelu, hidden)
    activated_low = activated.astype(jnp.bfloat16)
    result = (
        middle
        + jnp.dot(activated_low, reduce_weight, preferred_element_type=jnp.float32)
        + reduce_bias
    )
    incoming = cotangent[0]
    incoming_wide = incoming.astype(jnp.float32)
    reduce_bias_gradient = jnp.sum(incoming_wide, axis=0)
    reduce_weight_gradient = jnp.einsum(
        "sf,sd->fd", activated_low, incoming, preferred_element_type=jnp.float32
    )
    activated_gradient = jnp.einsum(
        "sd,fd->sf", incoming, reduce_weight, preferred_element_type=jnp.float32
    )
    (hidden_gradient,) = gelu_back(activated_gradient)
    expand_bias_gradient = jnp.sum(hidden_gradient, axis=0)
    hidden_low = hidden_gradient.astype(jnp.bfloat16)
    expand_weight_gradient = jnp.einsum(
        "sd,sf->df", normed_two_low, hidden_low, preferred_element_type=jnp.float32
    )
    normed_two_gradient = jnp.einsum(
        "sf,df->sd", hidden_low, expand_weight, preferred_element_type=jnp.float32
    )
    middle_part, middle_gain_gradient, middle_shift_gradient = middle_back(normed_two_gradient)
    middle_gradient = incoming_wide + middle_part
    output_bias_gradient = jnp.sum(middle_gradient, axis=0)
    middle_low = middle_gradient.astype(jnp.bfloat16)
    output_weight_gradient = jnp.einsum(
        "sd,se->de", mixed, middle_low, preferred_element_type=jnp.float32
    )
    attended_gradient = jnp.einsum(
        "se,de->sd", middle_low, output_weight, preferred_element_type=jnp.float32
    ).astype(jnp.bfloat16)
    back_near = with_halo(stacked, (("blk", 0),), reach)
    back_keys = back_near[:, :width].reshape(extent, HEADS, HD)
    back_values = back_near[:, width:].reshape(extent, HEADS, HD)
    gradient_heads = attended_gradient.reshape(length, HEADS, HD)
    shares = jnp.exp(scores_for(back_near) - logsum[:, :, None])
    share_gradient = jnp.einsum(
        "qhd,khd->hqk", gradient_heads, back_values, preferred_element_type=jnp.float32
    )
    delta = jnp.sum(shares * share_gradient, axis=-1)
    score_gradient = (shares * (share_gradient - delta[:, :, None]) * factor).astype(jnp.bfloat16)
    query_gradient = jnp.einsum(
        "hqk,khd->qhd", score_gradient, back_keys, preferred_element_type=jnp.float32
    )
    key_part = jnp.einsum(
        "hqk,qhd->khd", score_gradient, query_heads, preferred_element_type=jnp.float32
    )
    value_part = jnp.einsum(
        "hqk,qhd->khd",
        shares.astype(jnp.bfloat16),
        gradient_heads,
        preferred_element_type=jnp.float32,
    )
    partials = jnp.concatenate(
        [key_part.reshape(extent, width), value_part.reshape(extent, width)], axis=1
    )
    from_above = from_behind(partials[:reach].astype(jnp.bfloat16), "blk", -1).astype(jnp.float32)
    from_below = from_behind(partials[length + reach :].astype(jnp.bfloat16), "blk", 1).astype(
        jnp.float32
    )
    own_part = (
        partials[reach : reach + length]
        + jnp.pad(from_above, ((length - reach, 0), (0, 0)))
        + jnp.pad(from_below, ((0, length - reach), (0, 0)))
    )
    key_gradient = own_part[:, :width]
    value_gradient = own_part[:, width:]
    query_gradient = query_gradient.reshape(length, width)
    joint_bias_gradient = jnp.concatenate(
        [jnp.sum(query_gradient, axis=0), jnp.sum(value_gradient, axis=0)]
    )
    joined_low = jnp.concatenate([query_gradient, key_gradient, value_gradient], axis=1).astype(
        jnp.bfloat16
    )
    joint_weight_gradient = jnp.einsum(
        "sd,se->de", normed_low, joined_low, preferred_element_type=jnp.float32
    )
    normed_gradient = jnp.einsum(
        "se,de->sd", joined_low, joint_weight, preferred_element_type=jnp.float32
    )
    entry_part, entry_gain_gradient, entry_shift_gradient = entry_back(normed_gradient)
    input_gradient = (middle_gradient + entry_part).astype(jnp.bfloat16)
    g = Grid(lax.axis_size("dp"), lax.axis_size("blk"), width)
    A, B, R = g.A, g.B, g.R
    we = expand_weight_gradient.astype(BF).reshape(A, B, 2, R, 6, 4, 128).transpose(4, 2, 5, 1, 0, 3, 6)
    wr = reduce_weight_gradient.astype(BF).reshape(A, B, 2, 4, R, 6, 128).transpose(5, 2, 3, 1, 0, 4, 6)
    wj = joint_weight_gradient.astype(BF).reshape(A, B, 2, R, 3, 6, 128).transpose(5, 2, 4, 1, 0, 3, 6)
    wo = output_weight_gradient.astype(BF).reshape(A, B, 2, R, 1, 6, 128).transpose(5, 2, 4, 1, 0, 3, 6)
    chunks = jnp.concatenate([we, wr, jnp.concatenate([wj, wo], axis=2)], axis=0)
    sum_joint, sum_output, sum_expand, sum_reduce = reduce_weights(g, chunks)
    vectors = [
        entry_gain_gradient,
        entry_shift_gradient,
        joint_bias_gradient,
        output_bias_gradient,
        middle_gain_gradient,
        middle_shift_gradient,
        expand_bias_gradient,
        reduce_bias_gradient,
    ]
    packed = jnp.concatenate([v.reshape(2 * A * B, -1) for v in vectors], axis=1)
    mine = lax.psum(packed, ("dp", "blk"))[lax.axis_index("dp")]
    parts = []
    at = 0
    for v in vectors:
        size = v.shape[0] // (2 * A * B)
        parts.append(mine[at : at + size])
        at += size
    summed = (
        parts[0], parts[1], sum_joint, parts[2], sum_output, parts[3], parts[4], parts[5],
        sum_expand, parts[6], sum_reduce, parts[7],
    )
    return (
        result.astype(jnp.bfloat16)[None],
        input_gradient[None],
        summed[0],
        summed[1],
        summed[2],
        summed[3],
        summed[4],
        summed[5],
        summed[6],
        summed[7],
        summed[8],
        summed[9],
        summed[10],
        summed[11],
    )


def solution(mesh):
    return jax.shard_map(
        local,
        mesh=mesh,
        in_specs=(
            P("dp", "blk", None),
            P("dp", None),
            P(),
            P(),
            P(),
            P(),
            P(),
            P(),
            P(),
            P(),
            P(),
            P(),
            P(),
            P(),
            P("dp", "blk", None),
        ),
        out_specs=(
            P("dp", "blk", None),
            P("dp", "blk", None),
            P("dp"),
            P("dp"),
            P("dp", None),
            P("dp"),
            P("dp", None),
            P("dp"),
            P("dp"),
            P("dp"),
            P("dp", None),
            P("dp"),
            P("dp", None),
            P("dp"),
        ),
        check_vma=False,
    )
```

```python
import functools
import jax
import jax.numpy as jnp
from jax import lax
from jax.experimental import pallas as pl
from jax.experimental.pallas import tpu as pltpu
from jax.sharding import PartitionSpec as P

MESH = pl.DeviceIdType.MESH
CHUNKS = 18
BF = jnp.bfloat16
F32 = jnp.float32


class Grid:
    def __init__(self, dp, blk, width):
        self.A = 4
        self.B = dp // 8
        self.Y = blk
        self.dp = dp
        self.R = width // dp
        self.ny = 2 if blk == 2 else 0
        self.nx = 4 - self.ny


def comm_scratch(g):
    A, B, Y, R, nx, ny = g.A, g.B, g.Y, g.R, g.nx, g.ny
    shapes = dict(
        r0=pltpu.VMEM((CHUNKS, 4, B, A, R, 128), BF),
        rx=pltpu.VMEM((CHUNKS, B - 1, nx, A, R, 128), BF),
        rz=pltpu.VMEM((CHUNKS, A - 1, nx, R, 128), BF),
        ryx=pltpu.VMEM((CHUNKS, Y, nx, R, 128), BF),
        s_core=pltpu.SemaphoreType.DMA((2, CHUNKS)),
        s_x=pltpu.SemaphoreType.DMA((2, CHUNKS, B - 1)),
        s_z=pltpu.SemaphoreType.DMA((2, CHUNKS, A - 1)),
        s_yx=pltpu.SemaphoreType.DMA((2, CHUNKS, Y - 1)),
    )
    if ny:
        shapes.update(
            ry=pltpu.VMEM((CHUNKS, B, A, R, 128), BF),
            rx2=pltpu.VMEM((CHUNKS, B - 1, A, R, 128), BF),
            rz2=pltpu.VMEM((CHUNKS, A - 1, R, 128), BF),
            rag=pltpu.VMEM((CHUNKS, 2, R, 128), BF),
            s_y=pltpu.SemaphoreType.DMA((2, CHUNKS)),
            s_x2=pltpu.SemaphoreType.DMA((2, CHUNKS, B - 1)),
            s_z2=pltpu.SemaphoreType.DMA((2, CHUNKS, A - 1)),
            s_ag=pltpu.SemaphoreType.DMA((2, CHUNKS)),
        )
    return shapes


class Comm:
    def __init__(self, g, G, slots, refs, emit):
        self.g, self.G, self.slots, self.emit = g, G, slots, emit
        self.__dict__.update(refs)
        dp = lax.axis_index("dp")
        self.y = lax.axis_index("blk")
        self.c = dp % 2
        self.b = (dp // 2) % g.B
        self.a = dp // (2 * g.B)

    def dev(self, a=None, b=None, c=None, y=None):
        a = self.a if a is None else a
        b = self.b if b is None else b
        c = self.c if c is None else c
        y = self.y if y is None else y
        return ((a * self.g.B + b) * 2 + c, y)

    def partners(self):
        g = self.g
        return (
            [self.dev(c=1 - self.c)]
            + [self.dev(b=(self.b + k) % g.B) for k in range(1, g.B)]
            + [self.dev(a=(self.a + k) % g.A) for k in range(1, g.A)]
            + [self.dev(y=(self.y + k) % g.Y) for k in range(1, g.Y)]
        )

    def barrier(self):
        sem = pltpu.get_barrier_semaphore()
        others = self.partners()
        for other in others:
            pl.semaphore_signal(sem, inc=1, device_id=other, device_id_type=MESH)
        pl.semaphore_wait(sem, len(others))

    def copy(self, src, dst, sems, index, device):
        return pltpu.make_async_remote_copy(
            src_ref=src,
            dst_ref=dst,
            send_sem=sems.at[(0,) + index],
            recv_sem=sems.at[(1,) + index],
            device_id=device,
            device_id_type=MESH,
        )

    def stage0(self, j):
        s = j % self.slots
        return [self.copy(self.G.at[s, 1 - self.c], self.r0.at[j], self.s_core, (j,), self.dev(c=1 - self.c))]

    def stage1(self, j):
        g, s = self.g, j % self.slots
        out = []
        for k in range(1, g.B):
            other = (self.b + k) % g.B
            out.append(
                self.copy(
                    self.G.at[s, self.c, pl.ds(0, g.nx), other],
                    self.rx.at[j, k - 1],
                    self.s_x,
                    (j, k - 1),
                    self.dev(b=other),
                )
            )
        if g.ny:
            out.append(
                self.copy(
                    self.G.at[s, self.c, g.nx + 1 - self.y], self.ry.at[j], self.s_y, (j,), self.dev(y=1 - self.y)
                )
            )
        return out

    def stage2(self, j):
        g, s = self.g, j % self.slots
        out = []
        for k in range(1, g.A):
            other = (self.a + k) % g.A
            out.append(
                self.copy(
                    self.G.at[s, self.c, pl.ds(0, g.nx), self.b, other],
                    self.rz.at[j, k - 1],
                    self.s_z,
                    (j, k - 1),
                    self.dev(a=other),
                )
            )
        if g.ny:
            for k in range(1, g.B):
                other = (self.b + k) % g.B
                out.append(
                    self.copy(
                        self.G.at[s, self.c, g.nx + self.y, other],
                        self.rx2.at[j, k - 1],
                        self.s_x2,
                        (j, k - 1),
                        self.dev(b=other),
                    )
                )
        return out

    def stage3(self, j):
        g, s = self.g, j % self.slots
        out = []
        for k in range(1, g.Y):
            other = (self.y + k) % g.Y
            out.append(
                self.copy(
                    self.ryx.at[j, self.y], self.ryx.at[j, self.y], self.s_yx, (j, k - 1), self.dev(y=other)
                )
            )
        if g.ny:
            for k in range(1, g.A):
                other = (self.a + k) % g.A
                out.append(
                    self.copy(
                        self.G.at[s, self.c, g.nx + self.y, self.b, other],
                        self.rz2.at[j, k - 1],
                        self.s_z2,
                        (j, k - 1),
                        self.dev(a=other),
                    )
                )
        return out

    def stage4(self, j):
        if not self.g.ny:
            return []
        return [self.copy(self.rag.at[j, self.y], self.rag.at[j, self.y], self.s_ag, (j,), self.dev(y=1 - self.y))]

    def after0(self, j):
        s = j % self.slots
        g = self.g

        def add(i, _):
            col, b = i // g.B, i % g.B
            mine = self.G.at[s, self.c, col, b]
            mine[...] = mine[...] + self.r0[j, col, b]
            return 0

        lax.fori_loop(0, 4 * g.B, add, 0)

    def sum_into(self, mine, parts):
        total = mine[...].astype(F32)
        for part in parts:
            total = total + part.astype(F32)
        mine[...] = total.astype(BF)

    def after1(self, j):
        g, s = self.g, j % self.slots
        for col in range(g.nx):
            self.sum_into(
                self.G.at[s, self.c, col, self.b], [self.rx[j, k, col] for k in range(g.B - 1)]
            )
        if g.ny:
            for b in range(g.B):
                self.sum_into(self.G.at[s, self.c, g.nx + self.y, b], [self.ry[j, b]])

    def after2(self, j):
        g, s = self.g, j % self.slots
        total = self.G[s, self.c, pl.ds(0, g.nx), self.b, self.a].astype(F32)
        for k in range(g.A - 1):
            total = total + self.rz[j, k].astype(F32)
        self.ryx[j, self.y] = total.astype(BF)
        if g.ny:
            self.sum_into(
                self.G.at[s, self.c, g.nx + self.y, self.b], [self.rx2[j, k] for k in range(g.B - 1)]
            )

    def after3(self, j):
        g, s = self.g, j % self.slots
        total = self.ryx[j, 0].astype(F32)
        for k in range(1, g.Y):
            total = total + self.ryx[j, k].astype(F32)
        for col in range(g.nx):
            self.emit(j, col, total[col])
        if g.ny:
            total = self.G[s, self.c, g.nx + self.y, self.b, self.a].astype(F32)
            for k in range(g.A - 1):
                total = total + self.rz2[j, k].astype(F32)
            self.rag[j, self.y] = total.astype(BF)

    def after4(self, j):
        for k in range(self.g.ny):
            self.emit(j, self.g.nx + k, self.rag[j, k].astype(F32))

    def start(self, stage, j):
        for copy in (self.stage0, self.stage1, self.stage2, self.stage3, self.stage4)[stage](j):
            copy.start()

    def finish(self, stage, j):
        for copy in (self.stage0, self.stage1, self.stage2, self.stage3, self.stage4)[stage](j):
            copy.wait()
        (self.after0, self.after1, self.after2, self.after3, self.after4)[stage](j)
        if stage < 4:
            self.start(stage + 1, j)

    def advance(self, t, first=0, last=CHUNKS):
        for stage in range(4, -1, -1):
            j = t - stage
            if isinstance(j, int):
                if first <= j < last:
                    self.finish(stage, j)
            else:

                @pl.when((j >= first) & (j < last))
                def _(stage=stage, j=j):
                    self.finish(stage, j)


def emit_to(g, j_ref, o_ref, e_ref, r_ref):
    R = g.R

    def emit(j, col, value):
        @pl.when(j < 6)
        def _():
            e_ref[:, pl.ds(pl.multiple_of(j * 512 + col * 128, 128), 128)] = value

        @pl.when((j >= 6) & (j < 12))
        def _():
            r_ref[pl.ds(col * R, R), pl.ds(pl.multiple_of((j - 6) * 128, 128), 128)] = value

        @pl.when(j >= 12)
        def _():
            at = pl.multiple_of((j - 12) * 128, 128)
            if col < 3:
                j_ref[:, pl.ds(pl.multiple_of(col * 768 + at, 128), 128)] = value
            else:
                o_ref[:, pl.ds(at, 128)] = value

    return emit


HEADS = 12
HD = 64
D = 768
FF = 3072
ROWS = 512
EDGE = 128
SPAN = 3 * EDGE
PAIRS = HEADS // 2
SLOTS = 8
TICK = 512
TICKS = FF // TICK


def nn(left, right):
    return jnp.dot(left, right, preferred_element_type=F32)


def nt(left, right):
    return lax.dot_general(left, right, (((1,), (1,)), ((), ())), preferred_element_type=F32)


def stats(values):
    average = jnp.mean(values, axis=-1, keepdims=True)
    centred = values - average
    spread = jnp.mean(centred * centred, axis=-1, keepdims=True)
    inverse = lax.rsqrt(spread + 1e-06)
    return centred * inverse, inverse


def normal_parts(hidden):
    half = hidden * (0.5**0.5)
    size = jnp.abs(half)
    ratio = 1.0 / (1.0 + 0.3275911 * size)
    bell = jnp.exp(-half * half)
    tail = ((((1.061405429 * ratio - 1.453152027) * ratio + 1.421413741) * ratio - 0.284496736) * ratio + 0.254829592) * ratio
    tail = 0.5 * tail * bell
    share = jnp.where(hidden >= 0, 1.0 - tail, tail)
    return share, hidden * bell * 0.3989422804014327


def column_sum(values):
    return jnp.sum(values, axis=0, keepdims=True)


def layer_kernel(g, names, *refs):
    r = dict(zip(names, refs))
    A, B, R, Y = g.A, g.B, g.R, g.Y
    (patches, cotangent, segments, w_joint, w_output, w_expand, w_reduce) = (
        r[n] for n in ("patches", "cotangent", "segments", "w_joint", "w_output", "w_expand", "w_reduce")
    )
    G, vec = r["G"], r["vec"]
    r["oe"], r["oo"] = r["vT"], r["n2"]
    out_rows, dx_rows = r["k"].at[pl.ds(0, ROWS)], r["ml"]
    x, xh, dy = r["x"], r["xh"], r["dy"]
    comm = Comm(g, G, SLOTS, r, emit_to(g, r["j_out"], r["o_out"], r["e_out"], r["r_out"]))
    y = comm.y
    has_left, has_right = y > 0, y < Y - 1

    def load(src, dst, k):
        return pltpu.make_async_copy(src, dst, r["load"].at[k])

    load_x = load(patches, x, 0)
    load_wj = load(w_joint, r["wj"], 1)
    load_wo = load(w_output, r["wo"], 2)
    load_dy = load(cotangent, dy, 3)

    def ffn_loads(i):
        s = i % 3
        at = pl.ds(pl.multiple_of(i * TICK, TICK), TICK)
        return (
            pltpu.make_async_copy(w_expand.at[:, at], r["we"].at[s], r["stream"].at[0, s]),
            pltpu.make_async_copy(w_reduce.at[at], r["wr"].at[s], r["stream"].at[1, s]),
        )

    load_x.start()
    load_wj.start()
    load_wo.start()
    load_dy.start()
    for i in range(3):
        for copy in ffn_loads(i):
            copy.start()
    comm.barrier()

    def edge(k, side, src, dst, sems):
        other = comm.dev(y=(y + Y - 1) % Y) if side == 0 else comm.dev(y=(y + 1) % Y)
        return pltpu.make_async_remote_copy(
            src_ref=src, dst_ref=dst, send_sem=sems.at[(0,) + k + (side,)], recv_sem=sems.at[(1,) + k + (1 - side,)],
            device_id=other, device_id_type=MESH,
        )

    def x_edges():
        return (
            edge((), 0, patches.at[pl.ds(0, EDGE)], xh.at[1], r["s_edge"]),
            edge((), 1, patches.at[pl.ds(ROWS - EDGE, EDGE)], xh.at[0], r["s_edge"]),
        )

    to_left, to_right = x_edges()

    @pl.when(has_left)
    def _():
        to_left.start()

    @pl.when(has_right)
    def _():
        to_right.start()

    @pl.when(jnp.logical_not(has_left))
    def _():
        xh[0] = jnp.zeros((EDGE, D), BF)

    @pl.when(jnp.logical_not(has_right))
    def _():
        xh[1] = jnp.zeros((EDGE, D), BF)

    first_block = y * (ROWS // EDGE)
    count = segments.shape[0]
    columns = []
    for k in range(6):
        index = first_block + k - 1
        inside = (index >= 0) & (index < count)
        row = segments[pl.ds(jnp.clip(index, 0, count - 1), 1), :]
        row = jnp.where(inside, row, -1)
        columns.append(row)
    for b in range(4):
        for k in range(3):
            keys = jnp.broadcast_to(columns[b + k].astype(F32), (EDGE, EDGE)).T
            own = columns[b + 1].astype(F32)
            r["bias"][b, k * EDGE : (k + 1) * EDGE, :] = jnp.where(keys == own, 0.0, -1e30)

    vec[...] = jnp.zeros_like(vec)
    entry_gain, entry_shift = r["entry_gain"][...], r["entry_shift"][...]
    lanes = lax.broadcasted_iota(jnp.int32, (1, D), 1) % 128
    even = lanes < HD

    def project(rows, at, own, row_at):
        count = rows.shape[0]
        normal, _ = stats(rows.astype(F32))
        low = (normal * entry_gain + entry_shift).astype(BF)
        wj = r["wj"]
        key_rows = nn(low, wj[:, D : 2 * D]).astype(BF)
        r["k"][pl.ds(at, count), :] = key_rows
        r["kT"][:, pl.ds(at, count)] = key_rows.T
        value_rows = (nn(low, wj[:, 2 * D :]) + r["joint_bias"][:, D:]).astype(BF)
        r["v"][pl.ds(at, count), :] = value_rows
        r["vT"][:, pl.ds(at, count)] = value_rows.T
        if own:
            r["n1T"][:, pl.ds(row_at, count)] = low.T
            queries = (nn(low, wj[:, :D]) + r["joint_bias"][:, :D]).astype(BF) * BF(HD**-0.5)
            r["qe"][pl.ds(row_at, count), :] = jnp.where(even, queries, BF(0))
            r["qo"][pl.ds(row_at, count), :] = jnp.where(even, BF(0), queries)

    load_x.wait()
    load_wj.wait()

    def own_rows(i, _):
        at = pl.multiple_of(i * 256, 256)
        project(x[pl.ds(at, 256), :], pl.multiple_of(at + EDGE, EDGE), True, at)
        return 0

    lax.fori_loop(0, 2, own_rows, 0)

    @pl.when(has_left)
    def _():
        to_left.wait_send()
        to_right.wait_recv() if Y == 1 else edge((), 1, patches.at[pl.ds(0, EDGE)], xh.at[0], r["s_edge"]).wait_recv()

    @pl.when(has_right)
    def _():
        to_right.wait_send()
        edge((), 0, patches.at[pl.ds(0, EDGE)], xh.at[1], r["s_edge"]).wait_recv()

    def edge_rows(i, _):
        project(xh[i], pl.multiple_of(i * (ROWS + EDGE), EDGE), False, 0)
        return 0

    lax.fori_loop(0, 2, edge_rows, 0)

    top = lax.broadcasted_iota(jnp.int32, (EDGE, 1), 0) < HD

    def attend(p, _):
        at = pl.ds(pl.multiple_of(p * 128, 128), 128)
        for b in range(4):
            keys, own = pl.ds(b * EDGE, SPAN), pl.ds(b * EDGE, EDGE)
            both = jnp.concatenate([r["qe"][own, at], r["qo"][own, at]], axis=0)
            scores = nt(r["k"][keys, at], both)
            bias = r["bias"][b]
            scores = scores + jnp.concatenate([bias, bias], axis=1)
            powers = jnp.exp(scores - jnp.max(scores, axis=0, keepdims=True))
            probs = (powers * (1.0 / column_sum(powers))).astype(BF)
            r["probs"][p, b] = probs
            mixed = nn(r["vT"][at, keys], probs)
            r["attT"][at, own] = jnp.where(top, mixed[:, :128], mixed[:, 128:]).astype(BF)
        return 0

    lax.fori_loop(0, PAIRS, attend, 0)

    load_wo.wait()
    mid, total, n2, n2T = r["mid"], r["total"], r["n2"], r["n2T"]
    middle_gain, middle_shift = r["middle_gain"][...], r["middle_shift"][...]

    def finish_attention(i, _):
        at = pl.ds(pl.multiple_of(i * 256, 256), 256)
        mixed = r["attT"][:, at].T
        middle = x[at, :].astype(F32) + nn(mixed, r["wo"][...]) + r["output_bias"][...]
        mid[at, :] = middle
        total[at, :] = middle + r["reduce_bias"][...]
        normal, _ = stats(middle)
        low = (normal * middle_gain + middle_shift).astype(BF)
        n2[at, :] = low
        n2T[:, at] = low.T
        r["dn"][at, :] = jnp.zeros((256, D), F32)
        return 0

    lax.fori_loop(0, 2, finish_attention, 0)
    load_dy.wait()

    def feed_forward(i, _):
        s = i % 3
        for copy in ffn_loads(i):
            copy.wait()
        we, wr = r["we"].at[s], r["wr"].at[s]
        at = pl.ds(pl.multiple_of(i * TICK, TICK), TICK)
        bias = r["expand_bias"][:, at]
        bias_sum = jnp.zeros((1, TICK), F32)
        for half in range(2):
            rows = pl.ds(half * 256, 256)
            hidden = nn(n2[rows, :], we[...]) + bias
            back = nt(dy[rows, :], wr[...])
            share, slope = normal_parts(hidden)
            active = (hidden * share).astype(BF)
            hidden_gradient = back * (share + slope)
            bias_sum = bias_sum + column_sum(hidden_gradient)
            low = hidden_gradient.astype(BF)
            r["hl"][rows, :] = low
            r["actT"][at, rows] = active.T
            total[rows, :] += nn(active, wr[...])
            r["dn"][rows, :] += nt(low, we[...])
        r["eb"][:, at] = bias_sum
        for part in range(2):
            block = nn(n2T[part * 384 : (part + 1) * 384, :], r["hl"][...]).astype(BF)
            store_rows(block, i, part * 2, 2)
        comm.start(0, i)

        @pl.when(i + 3 < TICKS)
        def _():
            for copy in ffn_loads(i + 3):
                copy.start()

        comm.advance(i - 1)
        return 0

    def store_rows(block, chunk, a0, na):
        slot = chunk % SLOTS
        for a in range(na):
            for b in range(B):
                for c in range(2):
                    row = ((a * B + b) * 2 + c) * R
                    for col in range(block.shape[1] // 128):
                        G[slot, c, col, b, a0 + a] = block[row : row + R, col * 128 : (col + 1) * 128]

    lax.fori_loop(0, TICKS, feed_forward, 0)

    def reduce_gradient(p, _):
        at = pl.ds(pl.multiple_of(p * 256, 256), 256)
        chunk = 6 + 2 * p

        def part(a, _):
            block = nn(r["actT"][pl.ds(pl.multiple_of(a * D, D), D), :], dy[:, at]).astype(BF)
            for h in range(2):
                slot = (chunk + h) % SLOTS
                for b in range(B):
                    for c in range(2):
                        for k in range(4):
                            row = ((b * 2 + c) * 4 + k) * R
                            G[slot, c, k, b, a] = block[row : row + R, h * 128 : (h + 1) * 128]
            return 0

        lax.fori_loop(0, A, part, 0)
        comm.start(0, chunk)
        comm.start(0, chunk + 1)
        comm.advance(5 + p)
        return 0

    lax.fori_loop(0, 3, reduce_gradient, 0)

    def middle_back(i, _):
        at = pl.ds(pl.multiple_of(i * 256, 256), 256)
        out_rows[at, :] = total[at, :].astype(BF)
        error = r["dn"][at, :]
        normal, inverse = stats(mid[at, :])
        scaled = error * middle_gain
        part = inverse * (
            scaled
            - jnp.mean(scaled, axis=-1, keepdims=True)
            - normal * jnp.mean(scaled * normal, axis=-1, keepdims=True)
        )
        incoming = dy[at, :].astype(F32)
        gradient = incoming + part
        vec[5:6, :] += column_sum(error * normal)
        vec[6:7, :] += column_sum(error)
        vec[4:5, :] += column_sum(gradient)
        vec[11:12, :] += column_sum(incoming)
        mid[at, :] = gradient
        low = gradient.astype(BF)
        r["ml"][at, :] = low
        back = nt(low, r["wo"][...]).astype(BF)
        r["oe"][at, :] = jnp.where(even, back, BF(0))
        r["oo"][at, :] = jnp.where(even, BF(0), back)
        total[at, :] = jnp.zeros((256, D), F32)
        return 0

    lax.fori_loop(0, 2, middle_back, 0)
    save_out = pltpu.make_async_copy(out_rows, r["out"], r["save"].at[0])
    save_out.start()
    for k in range(4):
        vec[7 + k : 8 + k, :] = r["eb"][:, k * D : (k + 1) * D]
    comm.advance(8)

    parts, jq, sent, got, s_part = r["parts"], r["jq"], r["sent"], r["got"], r["s_part"]

    def part_copies(p):
        return (
            edge((p,), 0, sent.at[p % 2, 0], got.at[p, 1], s_part),
            edge((p,), 1, sent.at[p % 2, 1], got.at[p, 0], s_part),
        )

    def attend_back(p):
        at = pl.ds(pl.multiple_of(p * 128, 128), 128)
        slot = p % 2
        own_sum = jnp.zeros((1, 128), F32)
        parts[slot] = jnp.zeros((ROWS + 2 * EDGE, 256), F32)
        for b in range(4):
            keys, own = pl.ds(b * EDGE, SPAN), pl.ds(b * EDGE, EDGE)
            queries = jnp.concatenate([r["qe"][own, at], r["qo"][own, at]], axis=0)
            errors = jnp.concatenate([r["oe"][own, at], r["oo"][own, at]], axis=0)
            shares = nt(r["v"][keys, at], errors)
            probs = r["probs"][p, b]
            wide = probs.astype(F32)
            product = wide * shares
            delta = column_sum(product)
            low = (product - wide * delta).astype(BF)
            parts[slot, keys, 0:128] += nn(low, queries)
            parts[slot, keys, 128:256] += nn(probs, errors)
            turned = nn(r["kT"][at, keys], low)
            mine = (jnp.where(top, turned[:, :128], turned[:, 128:]) * HD**-0.5).T
            own_sum = own_sum + column_sum(mine)
            jq[slot, own, :] = mine.astype(BF)
        vec[2:3, at] = own_sum
        to_left, to_right = part_copies(p)

        @pl.when(has_left)
        def _():
            sent[slot, 0] = parts[slot, 0:EDGE, :].astype(BF)
            to_left.start()

        @pl.when(has_right)
        def _():
            sent[slot, 1] = parts[slot, ROWS + EDGE :, :].astype(BF)
            to_right.start()

    def joint_gradient(p):
        at = pl.ds(pl.multiple_of(p * 128, 128), 128)
        slot = p % 2
        to_left, to_right = part_copies(p)

        @pl.when(has_left)
        def _():
            to_left.wait_send()
            to_right.wait_recv()
            parts[slot, EDGE : 2 * EDGE, :] += got[p, 0].astype(F32)

        @pl.when(has_right)
        def _():
            to_right.wait_send()
            to_left.wait_recv()
            parts[slot, ROWS : ROWS + EDGE, :] += got[p, 1].astype(F32)

        sums = parts[slot, EDGE : ROWS + EDGE, :]
        vec[3:4, at] = column_sum(sums[:, 128:])
        low = jnp.concatenate([jq[slot], sums.astype(BF)], axis=1)
        wj = r["wj"]
        weights = jnp.concatenate([wj[:, pl.ds(pl.multiple_of(k * D + p * 128, 128), 128)] for k in range(3)], axis=1)
        total[...] += nt(low, weights)
        low_out = r["ml"][:, at]
        for part in range(2):
            rows = pl.ds(part * 384, 384)
            block = nn(r["n1T"][rows, :], low).astype(BF)
            block_out = nn(r["attT"][rows, :], low_out).astype(BF)
            store_rows(jnp.concatenate([block, block_out], axis=1), 12 + p, part * 2, 2)
        comm.start(0, 12 + p)

    def pair_step(i, _):
        @pl.when(i < PAIRS)
        def _():
            attend_back(i)

        @pl.when(i > 0)
        def _():
            joint_gradient(i - 1)

        comm.advance(9 + i)
        return 0

    lax.fori_loop(0, PAIRS + 1, pair_step, 0)

    def entry_back(i, _):
        at = pl.ds(pl.multiple_of(i * 256, 256), 256)
        error = total[at, :]
        normal, inverse = stats(x[at, :].astype(F32))
        scaled = error * entry_gain
        part = inverse * (
            scaled
            - jnp.mean(scaled, axis=-1, keepdims=True)
            - normal * jnp.mean(scaled * normal, axis=-1, keepdims=True)
        )
        vec[0:1, :] += column_sum(error * normal)
        vec[1:2, :] += column_sum(error)
        dx_rows[at, :] = (mid[at, :] + part).astype(BF)
        return 0

    lax.fori_loop(0, 2, entry_back, 0)
    save_dx = pltpu.make_async_copy(dx_rows, r["dx"], r["save"].at[1])
    save_dx.start()

    rv, s_vec = r["rv"], r["s_vec"]

    def vector_copies(step):
        groups = (
            [comm.dev(c=1 - comm.c)],
            [comm.dev(b=(comm.b + k) % B) for k in range(1, B)],
            [comm.dev(a=(comm.a + k) % A) for k in range(1, A)],
            [comm.dev(y=(comm.y + k) % Y) for k in range(1, Y)],
        )
        ids = (comm.c, comm.b, comm.a, comm.y)
        base = (0, 2, 2 + B, 2 + B + A)[step]
        here = rv.at[base + ids[step]]
        return here, [
            comm.copy(here, here, s_vec, (base + k,), other) for k, other in enumerate(groups[step])
        ]

    def vector_sum(step):
        base, size = ((0, 2), (2, B), (2 + B, A), (2 + B + A, Y))[step]
        value = rv[base]
        for k in range(1, size):
            value = value + rv[base + k]
        return value

    def vector_start(step, value):
        here, copies = vector_copies(step)
        here[...] = value
        for copy in copies:
            copy.start()

    def vector_wait(step):
        for copy in vector_copies(step)[1]:
            copy.wait()

    vector_start(0, vec[...])
    for step in range(4):
        comm.advance(16 + step)
        vector_wait(step)
        if step < 3:
            vector_start(step + 1, vector_sum(step))
    summed = vector_sum(3)
    place = lax.axis_index("dp")
    spot = lax.broadcasted_iota(jnp.int32, (D, 512), 0)
    lane = lax.broadcasted_iota(jnp.int32, (D, 512), 1)
    n2v, n4v = g.dp // 2, g.dp // 4
    want = jnp.where(
        lane < 128,
        lane + place * R,
        jnp.where(lane < 256, lane - 128 + (place % n2v) * (2 * R), lane - 256 + (place % n4v) * (4 * R)),
    )
    pick = jnp.where(spot == want, 1.0, 0.0).astype(F32)
    picked = jnp.dot(summed, pick, precision=lax.Precision.HIGHEST, preferred_element_type=F32)
    kind = lax.broadcasted_iota(jnp.int32, (16, 1), 0)
    r["v_out"][...] = picked[:, 0:128]
    r["jb_out"][...] = column_sum(jnp.where(kind == 2 + place // n2v, picked[:, 128:256], 0.0))
    r["eb_out"][...] = column_sum(jnp.where(kind == 7 + place // n4v, picked[:, 256:512], 0.0))
    for t in range(20, CHUNKS + 4):
        comm.advance(t)
    save_out.wait()
    save_dx.wait()


def layer(g, patches, segments, vectors, weights, cotangent):
    A, B, R, Y = g.A, g.B, g.R, g.Y
    comm_shapes = comm_scratch(g)
    V = pl.BlockSpec(memory_space=pltpu.VMEM)
    H = pl.BlockSpec(memory_space=pl.ANY)
    inputs = dict(
        patches=(patches, H),
        cotangent=(cotangent, H),
        segments=(segments, V),
        w_joint=(weights[0], H),
        w_output=(weights[1], H),
        w_expand=(weights[2], H),
        w_reduce=(weights[3], H),
        **{name: (value, V) for name, value in vectors.items()},
    )
    outputs = dict(
        out=((ROWS, D), BF),
        dx=((ROWS, D), BF),
        j_out=((R, 3 * D), F32),
        o_out=((R, D), F32),
        e_out=((R, FF), F32),
        r_out=((4 * R, D), F32),
        v_out=((16, 128), F32),
        jb_out=((1, 128), F32),
        eb_out=((1, 256), F32),
    )
    ext = ROWS + 2 * EDGE
    scratch = dict(
        x=pltpu.VMEM((ROWS, D), BF),
        xh=pltpu.VMEM((2, EDGE, D), BF),
        dy=pltpu.VMEM((ROWS, D), BF),
        wj=pltpu.VMEM((D, 3 * D), BF),
        wo=pltpu.VMEM((D, D), BF),
        we=pltpu.VMEM((3, D, TICK), BF),
        wr=pltpu.VMEM((3, TICK, D), BF),
        n1T=pltpu.VMEM((D, ROWS), BF),
        qe=pltpu.VMEM((ROWS, D), BF),
        qo=pltpu.VMEM((ROWS, D), BF),
        k=pltpu.VMEM((ext, D), BF),
        v=pltpu.VMEM((ext, D), BF),
        kT=pltpu.VMEM((D, ext), BF),
        vT=pltpu.VMEM((D, ext), BF),
        bias=pltpu.VMEM((4, SPAN, EDGE), F32),
        probs=pltpu.VMEM((PAIRS, 4, SPAN, 2 * EDGE), BF),
        attT=pltpu.VMEM((D, ROWS), BF),
        mid=pltpu.VMEM((ROWS, D), F32),
        total=pltpu.VMEM((ROWS, D), F32),
        dn=pltpu.VMEM((ROWS, D), F32),
        n2=pltpu.VMEM((ROWS, D), BF),
        n2T=pltpu.VMEM((D, ROWS), BF),
        hl=pltpu.VMEM((ROWS, TICK), BF),
        actT=pltpu.VMEM((FF, ROWS), BF),
        eb=pltpu.VMEM((1, FF), F32),
        ml=pltpu.VMEM((ROWS, D), BF),
        parts=pltpu.VMEM((2, ext, 256), F32),
        jq=pltpu.VMEM((2, ROWS, 128), BF),
        sent=pltpu.VMEM((2, 2, EDGE, 256), BF),
        got=pltpu.VMEM((PAIRS, 2, EDGE, 256), BF),
        vec=pltpu.VMEM((16, D), F32),
        rv=pltpu.VMEM((2 + B + A + Y, 16, D), F32),
        G=pltpu.VMEM((SLOTS, 2, 4, B, A, R, 128), BF),
        load=pltpu.SemaphoreType.DMA((4,)),
        save=pltpu.SemaphoreType.DMA((2,)),
        stream=pltpu.SemaphoreType.DMA((2, 3)),
        s_edge=pltpu.SemaphoreType.DMA((2, 2)),
        s_part=pltpu.SemaphoreType.DMA((2, PAIRS, 2)),
        s_vec=pltpu.SemaphoreType.DMA((2, 2 + B + A + Y)),
        **comm_shapes,
    )
    names = (*inputs, *outputs, *scratch)
    results = pl.pallas_call(
        functools.partial(layer_kernel, g, names),
        out_shape=tuple(jax.ShapeDtypeStruct(*shape) for shape in outputs.values()),
        in_specs=[spec for _, spec in inputs.values()],
        out_specs=[H, H] + [V] * (len(outputs) - 2),
        scratch_shapes=list(scratch.values()),
        compiler_params=pltpu.CompilerParams(
            collective_id=0, has_side_effects=True, vmem_limit_bytes=64 << 20
        ),
    )(*(value for value, _ in inputs.values()))
    return dict(zip(outputs, results))


def local(
    patches,
    segments,
    entry_gain,
    entry_shift,
    joint_weight,
    joint_bias,
    output_weight,
    output_bias,
    middle_gain,
    middle_shift,
    expand_weight,
    expand_bias,
    reduce_weight,
    reduce_bias,
    cotangent,
):
    g = Grid(lax.axis_size("dp"), lax.axis_size("blk"), D)
    R = g.R
    vectors = dict(
        entry_gain=entry_gain,
        entry_shift=entry_shift,
        joint_bias=joint_bias,
        output_bias=output_bias,
        middle_gain=middle_gain,
        middle_shift=middle_shift,
        expand_bias=expand_bias,
        reduce_bias=reduce_bias,
    )
    o = layer(
        g,
        patches[0],
        segments.reshape(-1, EDGE),
        {name: value.reshape(1, -1) for name, value in vectors.items()},
        (joint_weight, output_weight, expand_weight, reduce_weight),
        cotangent[0],
    )
    v = o["v_out"]
    return (
        o["out"][None],
        o["dx"][None],
        v[0, :R],
        v[1, :R],
        o["j_out"],
        o["jb_out"][0, : 2 * R],
        o["o_out"],
        v[4, :R],
        v[5, :R],
        v[6, :R],
        o["e_out"],
        o["eb_out"][0, : 4 * R],
        o["r_out"],
        v[11, :R],
    )


def solution(mesh):
    return jax.shard_map(
        local,
        mesh=mesh,
        in_specs=(
            P("dp", "blk", None),
            P("dp", None),
            P(),
            P(),
            P(),
            P(),
            P(),
            P(),
            P(),
            P(),
            P(),
            P(),
            P(),
            P(),
            P("dp", "blk", None),
        ),
        out_specs=(
            P("dp", "blk", None),
            P("dp", "blk", None),
            P("dp"),
            P("dp"),
            P("dp", None),
            P("dp"),
            P("dp", None),
            P("dp"),
            P("dp"),
            P("dp"),
            P("dp", None),
            P("dp"),
            P("dp", None),
            P("dp"),
        ),
        check_vma=False,
    )
```

```python
import functools
import jax
import jax.numpy as jnp
from jax import lax
from jax.experimental import pallas as pl
from jax.experimental.pallas import tpu as pltpu
from jax.sharding import PartitionSpec as P

MESH = pl.DeviceIdType.MESH
CHUNKS = 18
LAG = 2
RING = 9
BF = jnp.bfloat16
F32 = jnp.float32


class Grid:
    def __init__(self, dp, blk, width):
        self.A = 4
        self.B = dp // 8
        self.Y = blk
        self.dp = dp
        self.R = width // dp
        self.ny = 2 if blk == 2 else 0
        self.nx = 4 - self.ny


def comm_scratch(g):
    A, B, Y, R, nx, ny = g.A, g.B, g.Y, g.R, g.nx, g.ny
    shapes = dict(
        r0=pltpu.VMEM((RING, 4, B, A, R, 128), BF),
        rx=pltpu.VMEM((CHUNKS, B - 1, nx, A, R, 128), BF),
        rz=pltpu.VMEM((CHUNKS, A - 1, nx, R, 128), BF),
        ryx=pltpu.VMEM((CHUNKS, Y, nx, R, 128), BF),
        s_core=pltpu.SemaphoreType.DMA((2, CHUNKS)),
        s_x=pltpu.SemaphoreType.DMA((2, CHUNKS, B - 1)),
        s_z=pltpu.SemaphoreType.DMA((2, CHUNKS, A - 1)),
        s_yx=pltpu.SemaphoreType.DMA((2, CHUNKS, Y - 1)),
    )
    if ny:
        shapes.update(
            ry=pltpu.VMEM((CHUNKS, B, A, R, 128), BF),
            rx2=pltpu.VMEM((CHUNKS, B - 1, A, R, 128), BF),
            rz2=pltpu.VMEM((CHUNKS, A - 1, R, 128), BF),
            rag=pltpu.VMEM((CHUNKS, 2, R, 128), BF),
            s_y=pltpu.SemaphoreType.DMA((2, CHUNKS)),
            s_x2=pltpu.SemaphoreType.DMA((2, CHUNKS, B - 1)),
            s_z2=pltpu.SemaphoreType.DMA((2, CHUNKS, A - 1)),
            s_ag=pltpu.SemaphoreType.DMA((2, CHUNKS)),
        )
    return shapes


class Comm:
    def __init__(self, g, G, slots, refs, emit):
        self.g, self.G, self.slots, self.emit = g, G, slots, emit
        self.__dict__.update(refs)
        dp = lax.axis_index("dp")
        self.y = lax.axis_index("blk")
        self.c = dp % 2
        self.b = (dp // 2) % g.B
        self.a = dp // (2 * g.B)

    def dev(self, a=None, b=None, c=None, y=None):
        a = self.a if a is None else a
        b = self.b if b is None else b
        c = self.c if c is None else c
        y = self.y if y is None else y
        return ((a * self.g.B + b) * 2 + c, y)

    def partners(self):
        g = self.g
        return (
            [self.dev(c=1 - self.c)]
            + [self.dev(b=(self.b + k) % g.B) for k in range(1, g.B)]
            + [self.dev(a=(self.a + k) % g.A) for k in range(1, g.A)]
            + [self.dev(y=(self.y + k) % g.Y) for k in range(1, g.Y)]
        )

    def barrier(self):
        sem = pltpu.get_barrier_semaphore()
        others = self.partners()
        for other in others:
            pl.semaphore_signal(sem, inc=1, device_id=other, device_id_type=MESH)
        pl.semaphore_wait(sem, len(others))

    def copy(self, src, dst, sems, index, device):
        return pltpu.make_async_remote_copy(
            src_ref=src,
            dst_ref=dst,
            send_sem=sems.at[(0,) + index],
            recv_sem=sems.at[(1,) + index],
            device_id=device,
            device_id_type=MESH,
        )

    def stage0(self, j):
        s = j % self.slots
        return [self.copy(self.G.at[s, 1 - self.c], self.r0.at[j % RING], self.s_core, (j,), self.dev(c=1 - self.c))]

    def stage1(self, j):
        g, s = self.g, j % self.slots
        out = []
        for k in range(1, g.B):
            other = (self.b + k) % g.B
            out.append(
                self.copy(
                    self.G.at[s, self.c, pl.ds(0, g.nx), other],
                    self.rx.at[j, k - 1],
                    self.s_x,
                    (j, k - 1),
                    self.dev(b=other),
                )
            )
        if g.ny:
            out.append(
                self.copy(
                    self.G.at[s, self.c, g.nx + 1 - self.y], self.ry.at[j], self.s_y, (j,), self.dev(y=1 - self.y)
                )
            )
        return out

    def stage2(self, j):
        g, s = self.g, j % self.slots
        out = []
        for k in range(1, g.A):
            other = (self.a + k) % g.A
            out.append(
                self.copy(
                    self.G.at[s, self.c, pl.ds(0, g.nx), self.b, other],
                    self.rz.at[j, k - 1],
                    self.s_z,
                    (j, k - 1),
                    self.dev(a=other),
                )
            )
        if g.ny:
            for k in range(1, g.B):
                other = (self.b + k) % g.B
                out.append(
                    self.copy(
                        self.G.at[s, self.c, g.nx + self.y, other],
                        self.rx2.at[j, k - 1],
                        self.s_x2,
                        (j, k - 1),
                        self.dev(b=other),
                    )
                )
        return out

    def stage3(self, j):
        g, s = self.g, j % self.slots
        out = []
        for k in range(1, g.Y):
            other = (self.y + k) % g.Y
            out.append(
                self.copy(
                    self.ryx.at[j, self.y], self.ryx.at[j, self.y], self.s_yx, (j, k - 1), self.dev(y=other)
                )
            )
        if g.ny:
            for k in range(1, g.A):
                other = (self.a + k) % g.A
                out.append(
                    self.copy(
                        self.G.at[s, self.c, g.nx + self.y, self.b, other],
                        self.rz2.at[j, k - 1],
                        self.s_z2,
                        (j, k - 1),
                        self.dev(a=other),
                    )
                )
        return out

    def stage4(self, j):
        if not self.g.ny:
            return []
        return [self.copy(self.rag.at[j, self.y], self.rag.at[j, self.y], self.s_ag, (j,), self.dev(y=1 - self.y))]

    def after0(self, j):
        s = j % self.slots
        g = self.g

        def add(i, _):
            col, b = i // g.B, i % g.B
            mine = self.G.at[s, self.c, col, b]
            mine[...] = mine[...] + self.r0[j % RING, col, b]
            return 0

        lax.fori_loop(0, 4 * g.B, add, 0)

    def sum_into(self, mine, parts):
        total = mine[...].astype(F32)
        for part in parts:
            total = total + part.astype(F32)
        mine[...] = total.astype(BF)

    def after1(self, j):
        g, s = self.g, j % self.slots
        for col in range(g.nx):
            self.sum_into(
                self.G.at[s, self.c, col, self.b], [self.rx[j, k, col] for k in range(g.B - 1)]
            )
        if g.ny:
            for b in range(g.B):
                self.sum_into(self.G.at[s, self.c, g.nx + self.y, b], [self.ry[j, b]])

    def after2(self, j):
        g, s = self.g, j % self.slots
        total = self.G[s, self.c, pl.ds(0, g.nx), self.b, self.a].astype(F32)
        for k in range(g.A - 1):
            total = total + self.rz[j, k].astype(F32)
        self.ryx[j, self.y] = total.astype(BF)
        if g.ny:
            self.sum_into(
                self.G.at[s, self.c, g.nx + self.y, self.b], [self.rx2[j, k] for k in range(g.B - 1)]
            )

    def after3(self, j):
        g, s = self.g, j % self.slots
        total = self.ryx[j, 0].astype(F32)
        for k in range(1, g.Y):
            total = total + self.ryx[j, k].astype(F32)
        for col in range(g.nx):
            self.emit(j, col, total[col])
        if g.ny:
            total = self.G[s, self.c, g.nx + self.y, self.b, self.a].astype(F32)
            for k in range(g.A - 1):
                total = total + self.rz2[j, k].astype(F32)
            self.rag[j, self.y] = total.astype(BF)

    def after4(self, j):
        for k in range(self.g.ny):
            self.emit(j, self.g.nx + k, self.rag[j, k].astype(F32))

    def start(self, stage, j):
        for copy in (self.stage0, self.stage1, self.stage2, self.stage3, self.stage4)[stage](j):
            copy.start()

    def finish(self, stage, j):
        for copy in (self.stage0, self.stage1, self.stage2, self.stage3, self.stage4)[stage](j):
            copy.wait()
        (self.after0, self.after1, self.after2, self.after3, self.after4)[stage](j)
        if stage < 4:
            self.start(stage + 1, j)

    def advance(self, t, first=0, last=CHUNKS):
        for stage in range(4, -1, -1):
            j = t - LAG * stage
            if isinstance(j, int):
                if first <= j < last:
                    self.finish(stage, j)
            else:

                @pl.when((j >= first) & (j < last))
                def _(stage=stage, j=j):
                    self.finish(stage, j)


def emit_to(g, j_ref, o_ref, e_ref, r_ref):
    R = g.R

    def emit(j, col, value):
        @pl.when(j < 6)
        def _():
            e_ref[:, pl.ds(pl.multiple_of(j * 512 + col * 128, 128), 128)] = value

        @pl.when((j >= 6) & (j < 12))
        def _():
            r_ref[pl.ds(col * R, R), pl.ds(pl.multiple_of((j - 6) * 128, 128), 128)] = value

        @pl.when(j >= 12)
        def _():
            at = pl.multiple_of((j - 12) * 128, 128)
            if col < 3:
                j_ref[:, pl.ds(pl.multiple_of(col * 768 + at, 128), 128)] = value
            else:
                o_ref[:, pl.ds(at, 128)] = value

    return emit


HEADS = 12
VECTORS = (
    "entry_gain", "entry_shift", "joint_bias", "output_bias",
    "middle_gain", "middle_shift", "expand_bias", "reduce_bias",
)
HD = 64
D = 768
FF = 3072
ROWS = 512
EDGE = 128
SPAN = 3 * EDGE
PAIRS = HEADS // 2
SLOTS = 12
STREAM = 2
TICK = 512
TICKS = FF // TICK


def nn(left, right):
    return jnp.dot(left, right, preferred_element_type=F32)


def nt(left, right):
    return lax.dot_general(left, right, (((1,), (1,)), ((), ())), preferred_element_type=F32)


def stats(values):
    average = jnp.mean(values, axis=-1, keepdims=True)
    centred = values - average
    spread = jnp.mean(centred * centred, axis=-1, keepdims=True)
    inverse = lax.rsqrt(spread + 1e-06)
    return centred * inverse, inverse


def normal_parts(hidden):
    half = hidden * (0.5**0.5)
    size = jnp.abs(half)
    ratio = 1.0 / (1.0 + 0.3275911 * size)
    bell = jnp.exp(-half * half)
    tail = ((((1.061405429 * ratio - 1.453152027) * ratio + 1.421413741) * ratio - 0.284496736) * ratio + 0.254829592) * ratio
    tail = 0.5 * tail * bell
    share = jnp.where(hidden >= 0, 1.0 - tail, tail)
    return share, hidden * bell * 0.3989422804014327


def column_sum(values):
    return jnp.sum(values, axis=0, keepdims=True)


def layer_kernel(g, names, *refs):
    r = dict(zip(names, refs))
    A, B, R, Y = g.A, g.B, g.R, g.Y
    (patches, cotangent, segments, w_joint, w_output, w_expand, w_reduce) = (
        r[n] for n in ("patches", "cotangent", "segments", "w_joint", "w_output", "w_expand", "w_reduce")
    )
    G, vec = r["G"], r["vec"]
    for name in VECTORS:
        r[name + "_row"][...] = r[name][...].reshape(1, -1)
        r[name] = r[name + "_row"]
    r["oe"], r["oo"] = r["vT"], r["n2"]
    out_rows, dx_rows = r["k"].at[pl.ds(0, ROWS)], r["ml"]
    x, xh, dy = r["x"], r["xh"], r["dy"]
    comm = Comm(g, G, SLOTS, r, emit_to(g, r["j_out"], r["o_out"], r["e_out"], r["r_out"]))
    y = comm.y
    has_left, has_right = y > 0, y < Y - 1

    def load(src, dst, k):
        return pltpu.make_async_copy(src, dst, r["load"].at[k])

    load_x = load(patches, x, 0)
    load_wj = load(w_joint, r["wj"], 1)
    load_wo = load(w_output, r["wo"], 2)
    load_dy = load(cotangent, dy, 3)

    def ffn_loads(i):
        s = i % STREAM
        at = pl.ds(pl.multiple_of(i * TICK, TICK), TICK)
        return (
            pltpu.make_async_copy(w_expand.at[:, at], r["we"].at[s], r["stream"].at[0, s]),
            pltpu.make_async_copy(w_reduce.at[at], r["wr"].at[s], r["stream"].at[1, s]),
        )

    load_x.start()
    load_wj.start()
    comm.barrier()

    def edge(k, side, src, dst, sems):
        other = comm.dev(y=(y + Y - 1) % Y) if side == 0 else comm.dev(y=(y + 1) % Y)
        return pltpu.make_async_remote_copy(
            src_ref=src, dst_ref=dst, send_sem=sems.at[(0,) + k + (side,)], recv_sem=sems.at[(1,) + k + (1 - side,)],
            device_id=other, device_id_type=MESH,
        )

    def x_edges():
        return (
            edge((), 0, patches.at[pl.ds(0, EDGE)], xh.at[1], r["s_edge"]),
            edge((), 1, patches.at[pl.ds(ROWS - EDGE, EDGE)], xh.at[0], r["s_edge"]),
        )

    to_left, to_right = x_edges()

    @pl.when(has_left)
    def _():
        to_left.start()

    @pl.when(has_right)
    def _():
        to_right.start()

    @pl.when(jnp.logical_not(has_left))
    def _():
        xh[0] = jnp.zeros((EDGE, D), BF)

    @pl.when(jnp.logical_not(has_right))
    def _():
        xh[1] = jnp.zeros((EDGE, D), BF)

    first_block = y * (ROWS // EDGE)
    count = segments.shape[0]
    columns = []
    for k in range(6):
        index = first_block + k - 1
        inside = (index >= 0) & (index < count)
        row = segments[pl.ds(jnp.clip(index, 0, count - 1), 1), :]
        row = jnp.where(inside, row, -1)
        columns.append(row)
    for b in range(4):
        for k in range(3):
            keys = jnp.broadcast_to(columns[b + k].astype(F32), (EDGE, EDGE)).T
            own = columns[b + 1].astype(F32)
            r["bias"][b, k * EDGE : (k + 1) * EDGE, :] = jnp.where(keys == own, 0.0, -1e30)

    vec[...] = jnp.zeros_like(vec)
    entry_gain, entry_shift = r["entry_gain"][...], r["entry_shift"][...]
    lanes = lax.broadcasted_iota(jnp.int32, (1, D), 1) % 128
    even = lanes < HD

    def project(rows, at, own, row_at):
        count = rows.shape[0]
        normal, _ = stats(rows.astype(F32))
        low = (normal * entry_gain + entry_shift).astype(BF)
        wj = r["wj"]
        key_rows = nn(low, wj[:, D : 2 * D]).astype(BF)
        r["k"][pl.ds(at, count), :] = key_rows
        r["kT"][:, pl.ds(at, count)] = key_rows.T
        value_rows = (nn(low, wj[:, 2 * D :]) + r["joint_bias"][:, D:]).astype(BF)
        r["v"][pl.ds(at, count), :] = value_rows
        r["vT"][:, pl.ds(at, count)] = value_rows.T
        if own:
            r["n1T"][:, pl.ds(row_at, count)] = low.T
            queries = (nn(low, wj[:, :D]) + r["joint_bias"][:, :D]).astype(BF) * BF(HD**-0.5)
            r["qe"][pl.ds(row_at, count), :] = jnp.where(even, queries, BF(0))
            r["qo"][pl.ds(row_at, count), :] = jnp.where(even, BF(0), queries)

    load_x.wait()
    load_wj.wait()
    load_wo.start()
    load_dy.start()
    for i in range(STREAM):
        for copy in ffn_loads(i):
            copy.start()

    def own_rows(i, _):
        at = pl.multiple_of(i * 256, 256)
        project(x[pl.ds(at, 256), :], pl.multiple_of(at + EDGE, EDGE), True, at)
        return 0

    lax.fori_loop(0, 2, own_rows, 0)

    @pl.when(has_left)
    def _():
        to_left.wait_send()
        to_right.wait_recv() if Y == 1 else edge((), 1, patches.at[pl.ds(0, EDGE)], xh.at[0], r["s_edge"]).wait_recv()

    @pl.when(has_right)
    def _():
        to_right.wait_send()
        edge((), 0, patches.at[pl.ds(0, EDGE)], xh.at[1], r["s_edge"]).wait_recv()

    def edge_rows(i, _):
        project(xh[i], pl.multiple_of(i * (ROWS + EDGE), EDGE), False, 0)
        return 0

    lax.fori_loop(0, 2, edge_rows, 0)

    top = lax.broadcasted_iota(jnp.int32, (EDGE, 1), 0) < HD

    def attend(p, _):
        at = pl.ds(pl.multiple_of(p * 128, 128), 128)
        for b in range(4):
            keys, own = pl.ds(b * EDGE, SPAN), pl.ds(b * EDGE, EDGE)
            both = jnp.concatenate([r["qe"][own, at], r["qo"][own, at]], axis=0)
            scores = nt(r["k"][keys, at], both)
            bias = r["bias"][b]
            scores = scores + jnp.concatenate([bias, bias], axis=1)
            powers = jnp.exp(scores - jnp.max(scores, axis=0, keepdims=True))
            probs = (powers * (1.0 / column_sum(powers))).astype(BF)
            r["probs"][p, b] = probs
            mixed = nn(r["vT"][at, keys], probs)
            r["attT"][at, own] = jnp.where(top, mixed[:, :128], mixed[:, 128:]).astype(BF)
        return 0

    lax.fori_loop(0, PAIRS, attend, 0)

    load_wo.wait()
    mid, total, n2, n2T = r["mid"], r["total"], r["n2"], r["n2T"]
    middle_gain, middle_shift = r["middle_gain"][...], r["middle_shift"][...]

    def finish_attention(i, _):
        at = pl.ds(pl.multiple_of(i * 256, 256), 256)
        mixed = r["attT"][:, at].T
        middle = x[at, :].astype(F32) + nn(mixed, r["wo"][...]) + r["output_bias"][...]
        mid[at, :] = middle
        total[at, :] = middle + r["reduce_bias"][...]
        normal, _ = stats(middle)
        low = (normal * middle_gain + middle_shift).astype(BF)
        n2[at, :] = low
        n2T[:, at] = low.T
        r["dn"][at, :] = jnp.zeros((256, D), F32)
        return 0

    lax.fori_loop(0, 2, finish_attention, 0)
    load_dy.wait()

    def feed_forward(i, _):
        s = i % STREAM
        for copy in ffn_loads(i):
            copy.wait()
        we, wr = r["we"].at[s], r["wr"].at[s]
        at = pl.ds(pl.multiple_of(i * TICK, TICK), TICK)
        bias = r["expand_bias"][:, at]
        bias_sum = jnp.zeros((1, TICK), F32)
        for half in range(2):
            rows = pl.ds(half * 256, 256)
            hidden = nn(n2[rows, :], we[...]) + bias
            back = nt(dy[rows, :], wr[...])
            share, slope = normal_parts(hidden)
            active = (hidden * share).astype(BF)
            hidden_gradient = back * (share + slope)
            bias_sum = bias_sum + column_sum(hidden_gradient)
            low = hidden_gradient.astype(BF)
            r["hl"][rows, :] = low
            r["actT"][at, rows] = active.T
            total[rows, :] += nn(active, wr[...])
            r["dn"][rows, :] += nt(low, we[...])
        r["eb"][:, at] = bias_sum
        for part in range(2):
            block = nn(n2T[part * 384 : (part + 1) * 384, :], r["hl"][...]).astype(BF)
            store_rows(block, i, part * 2, 2)
        comm.start(0, i)

        @pl.when(i + STREAM < TICKS)
        def _():
            for copy in ffn_loads(i + STREAM):
                copy.start()

        comm.advance(i - 1)
        return 0

    def store_rows(block, chunk, a0, na):
        slot = chunk % SLOTS
        for a in range(na):
            for b in range(B):
                for c in range(2):
                    row = ((a * B + b) * 2 + c) * R
                    for col in range(block.shape[1] // 128):
                        G[slot, c, col, b, a0 + a] = block[row : row + R, col * 128 : (col + 1) * 128]

    lax.fori_loop(0, TICKS, feed_forward, 0)

    def reduce_gradient(p, _):
        at = pl.ds(pl.multiple_of(p * 256, 256), 256)
        chunk = 6 + 2 * p

        def part(a, _):
            block = nn(r["actT"][pl.ds(pl.multiple_of(a * D, D), D), :], dy[:, at]).astype(BF)
            for h in range(2):
                slot = (chunk + h) % SLOTS
                for b in range(B):
                    for c in range(2):
                        for k in range(4):
                            row = ((b * 2 + c) * 4 + k) * R
                            G[slot, c, k, b, a] = block[row : row + R, h * 128 : (h + 1) * 128]
            return 0

        lax.fori_loop(0, A, part, 0)
        comm.start(0, chunk)
        comm.start(0, chunk + 1)
        comm.advance(5 + p)
        return 0

    lax.fori_loop(0, 3, reduce_gradient, 0)

    def middle_back(i, _):
        at = pl.ds(pl.multiple_of(i * 256, 256), 256)
        out_rows[at, :] = total[at, :].astype(BF)
        error = r["dn"][at, :]
        normal, inverse = stats(mid[at, :])
        scaled = error * middle_gain
        part = inverse * (
            scaled
            - jnp.mean(scaled, axis=-1, keepdims=True)
            - normal * jnp.mean(scaled * normal, axis=-1, keepdims=True)
        )
        incoming = dy[at, :].astype(F32)
        gradient = incoming + part
        vec[5:6, :] += column_sum(error * normal)
        vec[6:7, :] += column_sum(error)
        vec[4:5, :] += column_sum(gradient)
        vec[11:12, :] += column_sum(incoming)
        mid[at, :] = gradient
        low = gradient.astype(BF)
        r["ml"][at, :] = low
        back = nt(low, r["wo"][...]).astype(BF)
        r["oe"][at, :] = jnp.where(even, back, BF(0))
        r["oo"][at, :] = jnp.where(even, BF(0), back)
        total[at, :] = jnp.zeros((256, D), F32)
        return 0

    lax.fori_loop(0, 2, middle_back, 0)
    save_out = pltpu.make_async_copy(out_rows, r["out"], r["save"].at[0])
    save_out.start()
    for k in range(4):
        vec[7 + k : 8 + k, :] = r["eb"][:, k * D : (k + 1) * D]
    comm.advance(8)

    parts, jq, sent, got, s_part = r["parts"], r["jq"], r["sent"], r["got"], r["s_part"]

    def part_copies(p):
        return (
            edge((p,), 0, sent.at[p % 2, 0], got.at[p, 1], s_part),
            edge((p,), 1, sent.at[p % 2, 1], got.at[p, 0], s_part),
        )

    def attend_back(p):
        at = pl.ds(pl.multiple_of(p * 128, 128), 128)
        slot = p % 2
        own_sum = jnp.zeros((1, 128), F32)
        parts[slot] = jnp.zeros((ROWS + 2 * EDGE, 256), F32)
        for b in range(4):
            keys, own = pl.ds(b * EDGE, SPAN), pl.ds(b * EDGE, EDGE)
            queries = jnp.concatenate([r["qe"][own, at], r["qo"][own, at]], axis=0)
            errors = jnp.concatenate([r["oe"][own, at], r["oo"][own, at]], axis=0)
            shares = nt(r["v"][keys, at], errors)
            probs = r["probs"][p, b]
            wide = probs.astype(F32)
            product = wide * shares
            delta = column_sum(product)
            low = (product - wide * delta).astype(BF)
            parts[slot, keys, 0:128] += nn(low, queries)
            parts[slot, keys, 128:256] += nn(probs, errors)
            turned = nn(r["kT"][at, keys], low)
            mine = (jnp.where(top, turned[:, :128], turned[:, 128:]) * HD**-0.5).T
            own_sum = own_sum + column_sum(mine)
            jq[slot, own, :] = mine.astype(BF)
        vec[2:3, at] = own_sum
        to_left, to_right = part_copies(p)

        @pl.when(has_left)
        def _():
            sent[slot, 0] = parts[slot, 0:EDGE, :].astype(BF)
            to_left.start()

        @pl.when(has_right)
        def _():
            sent[slot, 1] = parts[slot, ROWS + EDGE :, :].astype(BF)
            to_right.start()

    def joint_gradient(p):
        at = pl.ds(pl.multiple_of(p * 128, 128), 128)
        slot = p % 2
        to_left, to_right = part_copies(p)

        @pl.when(has_left)
        def _():
            to_left.wait_send()
            to_right.wait_recv()
            parts[slot, EDGE : 2 * EDGE, :] += got[p, 0].astype(F32)

        @pl.when(has_right)
        def _():
            to_right.wait_send()
            to_left.wait_recv()
            parts[slot, ROWS : ROWS + EDGE, :] += got[p, 1].astype(F32)

        sums = parts[slot, EDGE : ROWS + EDGE, :]
        vec[3:4, at] = column_sum(sums[:, 128:])
        low = jnp.concatenate([jq[slot], sums.astype(BF)], axis=1)
        wj = r["wj"]
        weights = jnp.concatenate([wj[:, pl.ds(pl.multiple_of(k * D + p * 128, 128), 128)] for k in range(3)], axis=1)
        total[...] += nt(low, weights)
        low_out = r["ml"][:, at]
        for part in range(2):
            rows = pl.ds(part * 384, 384)
            block = nn(r["n1T"][rows, :], low).astype(BF)
            block_out = nn(r["attT"][rows, :], low_out).astype(BF)
            store_rows(jnp.concatenate([block, block_out], axis=1), 12 + p, part * 2, 2)
        comm.start(0, 12 + p)

    def pair_step(i, _):
        @pl.when(i < PAIRS)
        def _():
            attend_back(i)

        @pl.when(i > 0)
        def _():
            joint_gradient(i - 1)

        comm.advance(9 + i)
        return 0

    lax.fori_loop(0, PAIRS + 1, pair_step, 0)

    def entry_back(i, _):
        at = pl.ds(pl.multiple_of(i * 256, 256), 256)
        error = total[at, :]
        normal, inverse = stats(x[at, :].astype(F32))
        scaled = error * entry_gain
        part = inverse * (
            scaled
            - jnp.mean(scaled, axis=-1, keepdims=True)
            - normal * jnp.mean(scaled * normal, axis=-1, keepdims=True)
        )
        vec[0:1, :] += column_sum(error * normal)
        vec[1:2, :] += column_sum(error)
        dx_rows[at, :] = (mid[at, :] + part).astype(BF)
        return 0

    lax.fori_loop(0, 2, entry_back, 0)
    save_dx = pltpu.make_async_copy(dx_rows, r["dx"], r["save"].at[1])
    save_dx.start()

    rv, s_vec = r["rv"], r["s_vec"]

    def vector_copies(step):
        groups = (
            [comm.dev(c=1 - comm.c)],
            [comm.dev(b=(comm.b + k) % B) for k in range(1, B)],
            [comm.dev(a=(comm.a + k) % A) for k in range(1, A)],
            [comm.dev(y=(comm.y + k) % Y) for k in range(1, Y)],
        )
        ids = (comm.c, comm.b, comm.a, comm.y)
        base = (0, 2, 0, A)[step]
        held = rv if step < 2 else r["rvl"]
        here = held.at[base + ids[step]]
        return here, [
            comm.copy(here, here, s_vec, ((0, 2, 2 + B, 2 + B + A)[step] + k,), other) for k, other in enumerate(groups[step])
        ]

    def vector_sum(step):
        base, size = ((0, 2), (2, B), (0, A), (A, Y))[step]
        held = rv if step < 2 else r["rvl"]
        value = held[base].astype(F32)
        for k in range(1, size):
            value = value + held[base + k].astype(F32)
        return value

    def vector_start(step, value):
        here, copies = vector_copies(step)
        here[...] = value.astype(here.dtype)
        for copy in copies:
            copy.start()

    def vector_wait(step):
        for copy in vector_copies(step)[1]:
            copy.wait()

    vector_start(0, vec[...])
    for step in range(4):
        comm.advance(16 + step)
        vector_wait(step)
        if step < 3:
            vector_start(step + 1, vector_sum(step))
    summed = vector_sum(3)
    place = lax.axis_index("dp")
    spot = lax.broadcasted_iota(jnp.int32, (D, 512), 0)
    lane = lax.broadcasted_iota(jnp.int32, (D, 512), 1)
    n2v, n4v = g.dp // 2, g.dp // 4
    want = jnp.where(
        lane < 128,
        lane + place * R,
        jnp.where(lane < 256, lane - 128 + (place % n2v) * (2 * R), lane - 256 + (place % n4v) * (4 * R)),
    )
    pick = jnp.where(spot == want, 1.0, 0.0).astype(F32)
    picked = jnp.dot(summed, pick, precision=lax.Precision.HIGHEST, preferred_element_type=F32)
    kind = lax.broadcasted_iota(jnp.int32, (16, 1), 0)
    r["v_out"][...] = picked[:, 0:128]
    r["jb_out"][...] = column_sum(jnp.where(kind == 2 + place // n2v, picked[:, 128:256], 0.0))
    r["eb_out"][...] = column_sum(jnp.where(kind == 7 + place // n4v, picked[:, 256:512], 0.0))
    for t in range(20, CHUNKS + 4 * LAG):
        comm.advance(t)
    save_out.wait()
    save_dx.wait()


def layer(g, patches, segments, vectors, weights, cotangent):
    A, B, R, Y = g.A, g.B, g.R, g.Y
    comm_shapes = comm_scratch(g)
    V = pl.BlockSpec(memory_space=pltpu.VMEM)
    H = pl.BlockSpec(memory_space=pl.ANY)
    inputs = dict(
        patches=(patches, H),
        cotangent=(cotangent, H),
        segments=(segments, V),
        w_joint=(weights[0], H),
        w_output=(weights[1], H),
        w_expand=(weights[2], H),
        w_reduce=(weights[3], H),
        **{name: (value, V) for name, value in vectors.items()},
    )
    outputs = dict(
        out=((ROWS, D), BF),
        dx=((ROWS, D), BF),
        j_out=((R, 3 * D), F32),
        o_out=((R, D), F32),
        e_out=((R, FF), F32),
        r_out=((4 * R, D), F32),
        v_out=((16, 128), F32),
        jb_out=((1, 128), F32),
        eb_out=((1, 256), F32),
    )
    ext = ROWS + 2 * EDGE
    scratch = dict(
        x=pltpu.VMEM((ROWS, D), BF),
        xh=pltpu.VMEM((2, EDGE, D), BF),
        dy=pltpu.VMEM((ROWS, D), BF),
        wj=pltpu.VMEM((D, 3 * D), BF),
        wo=pltpu.VMEM((D, D), BF),
        we=pltpu.VMEM((STREAM, D, TICK), BF),
        wr=pltpu.VMEM((STREAM, TICK, D), BF),
        n1T=pltpu.VMEM((D, ROWS), BF),
        qe=pltpu.VMEM((ROWS, D), BF),
        qo=pltpu.VMEM((ROWS, D), BF),
        k=pltpu.VMEM((ext, D), BF),
        v=pltpu.VMEM((ext, D), BF),
        kT=pltpu.VMEM((D, ext), BF),
        vT=pltpu.VMEM((D, ext), BF),
        bias=pltpu.VMEM((4, SPAN, EDGE), F32),
        probs=pltpu.VMEM((PAIRS, 4, SPAN, 2 * EDGE), BF),
        attT=pltpu.VMEM((D, ROWS), BF),
        mid=pltpu.VMEM((ROWS, D), F32),
        total=pltpu.VMEM((ROWS, D), F32),
        dn=pltpu.VMEM((ROWS, D), F32),
        n2=pltpu.VMEM((ROWS, D), BF),
        n2T=pltpu.VMEM((D, ROWS), BF),
        hl=pltpu.VMEM((ROWS, TICK), BF),
        actT=pltpu.VMEM((FF, ROWS), BF),
        eb=pltpu.VMEM((1, FF), F32),
        ml=pltpu.VMEM((ROWS, D), BF),
        parts=pltpu.VMEM((2, ext, 256), F32),
        jq=pltpu.VMEM((2, ROWS, 128), BF),
        sent=pltpu.VMEM((2, 2, EDGE, 256), BF),
        got=pltpu.VMEM((PAIRS, 2, EDGE, 256), BF),
        vec=pltpu.VMEM((16, D), F32),
        rv=pltpu.VMEM((2 + B, 16, D), F32),
        rvl=pltpu.VMEM((A + Y, 16, D), BF),
        G=pltpu.VMEM((SLOTS, 2, 4, B, A, R, 128), BF),
        load=pltpu.SemaphoreType.DMA((4,)),
        save=pltpu.SemaphoreType.DMA((2,)),
        stream=pltpu.SemaphoreType.DMA((2, STREAM)),
        s_edge=pltpu.SemaphoreType.DMA((2, 2)),
        s_part=pltpu.SemaphoreType.DMA((2, PAIRS, 2)),
        s_vec=pltpu.SemaphoreType.DMA((2, 2 + B + A + Y)),
        **{name + "_row": pltpu.VMEM((1, value.shape[0]), F32) for name, value in vectors.items()},
        **comm_shapes,
    )
    names = (*inputs, *outputs, *scratch)
    results = pl.pallas_call(
        functools.partial(layer_kernel, g, names),
        out_shape=tuple(jax.ShapeDtypeStruct(*shape) for shape in outputs.values()),
        in_specs=[spec for _, spec in inputs.values()],
        out_specs=[H, H] + [V] * (len(outputs) - 2),
        scratch_shapes=list(scratch.values()),
        compiler_params=pltpu.CompilerParams(
            collective_id=0, has_side_effects=True, vmem_limit_bytes=64 << 20
        ),
    )(*(value for value, _ in inputs.values()))
    return hand_over(g, dict(zip(outputs, results)))


def hand_over_kernel(g, out, dx, j, o, e, w, v, jb, eb, *refs):
    outs, sems = refs[:14], refs[14]
    R = g.R
    moves = [(out, 0), (dx, 1), (j, 4), (o, 6), (e, 10), (w, 12)]
    copies = [pltpu.make_async_copy(src, outs[k], sems.at[i]) for i, (src, k) in enumerate(moves)]
    for copy in copies:
        copy.start()
    for row, k in ((0, 2), (1, 3), (4, 7), (5, 8), (6, 9), (11, 13)):
        outs[k][...] = v[row, :R]
    outs[5][...] = jb[0, : 2 * R]
    outs[11][...] = eb[0, : 4 * R]
    for copy in copies:
        copy.wait()


def hand_over(g, o):
    R = g.R
    V = pl.BlockSpec(memory_space=pltpu.VMEM)
    H = pl.BlockSpec(memory_space=pl.ANY)
    shapes = [
        ((ROWS, D), BF), ((ROWS, D), BF), ((R,), F32), ((R,), F32), ((R, 3 * D), F32), ((2 * R,), F32), ((R, D), F32),
        ((R,), F32), ((R,), F32), ((R,), F32), ((R, FF), F32), ((4 * R,), F32), ((4 * R, D), F32), ((R,), F32),
    ]
    names = ("out", "dx", "j_out", "o_out", "e_out", "r_out", "v_out", "jb_out", "eb_out")
    return pl.pallas_call(
        functools.partial(hand_over_kernel, g),
        out_shape=tuple(jax.ShapeDtypeStruct(*shape) for shape in shapes),
        in_specs=[V] * 9,
        out_specs=[V if len(shape) == 1 else H for shape, _ in shapes],
        scratch_shapes=[pltpu.SemaphoreType.DMA((6,))],
    )(*(o[name] for name in names))


def local(
    patches,
    segments,
    entry_gain,
    entry_shift,
    joint_weight,
    joint_bias,
    output_weight,
    output_bias,
    middle_gain,
    middle_shift,
    expand_weight,
    expand_bias,
    reduce_weight,
    reduce_bias,
    cotangent,
):
    g = Grid(lax.axis_size("dp"), lax.axis_size("blk"), D)
    R = g.R
    vectors = dict(
        entry_gain=entry_gain,
        entry_shift=entry_shift,
        joint_bias=joint_bias,
        output_bias=output_bias,
        middle_gain=middle_gain,
        middle_shift=middle_shift,
        expand_bias=expand_bias,
        reduce_bias=reduce_bias,
    )
    o = layer(
        g,
        patches[0],
        segments.reshape(-1, EDGE),
        vectors,
        (joint_weight, output_weight, expand_weight, reduce_weight),
        cotangent[0],
    )
    return (o[0][None], o[1][None], *o[2:])


def solution(mesh):
    return jax.shard_map(
        local,
        mesh=mesh,
        in_specs=(
            P("dp", "blk", None),
            P("dp", None),
            P(),
            P(),
            P(),
            P(),
            P(),
            P(),
            P(),
            P(),
            P(),
            P(),
            P(),
            P(),
            P("dp", "blk", None),
        ),
        out_specs=(
            P("dp", "blk", None),
            P("dp", "blk", None),
            P("dp"),
            P("dp"),
            P("dp", None),
            P("dp"),
            P("dp", None),
            P("dp"),
            P("dp"),
            P("dp"),
            P("dp", None),
            P("dp"),
            P("dp", None),
            P("dp"),
        ),
        check_vma=False,
    )
```

```python
import functools
import jax
import jax.numpy as jnp
from jax import lax
from jax.experimental import pallas as pl
from jax.experimental.pallas import tpu as pltpu
from jax.sharding import PartitionSpec as P

MESH = pl.DeviceIdType.MESH
CHUNKS = 18
AFTER = (2, 6, 10, 14, 18)
RING = 9
BF = jnp.bfloat16
F32 = jnp.float32


class Grid:
    def __init__(self, dp, blk, width):
        self.A = 4
        self.B = dp // 8
        self.Y = blk
        self.dp = dp
        self.R = width // dp
        self.kinds = 2 if blk == 2 else 1


def comm_scratch(g):
    A, B, Y, R = g.A, g.B, g.Y, g.R
    n = CHUNKS // g.kinds
    shapes = dict(
        r0=pltpu.VMEM((RING, 4, B, A, R, 128), BF),
        rx=pltpu.VMEM((n, B - 1, 4, A, R, 128), BF),
        rz=pltpu.VMEM((n, A - 1, 4, R, 128), BF),
        ryx=pltpu.VMEM((n, Y, 4, R, 128), BF),
        s_core=pltpu.SemaphoreType.DMA((2, CHUNKS)),
        s_x=pltpu.SemaphoreType.DMA((2, CHUNKS, B - 1)),
        s_z=pltpu.SemaphoreType.DMA((2, CHUNKS)),
        s_y=pltpu.SemaphoreType.DMA((2, CHUNKS, Y - 1)),
    )
    if g.kinds == 2:
        shapes.update(
            ry=pltpu.VMEM((n, 2, B, A, R, 128), BF),
            rx2=pltpu.VMEM((n, B - 1, 2, A, R, 128), BF),
            rz2=pltpu.VMEM((n, A - 1, 2, R, 128), BF),
            rag=pltpu.VMEM((n, 2, 2, R, 128), BF),
            s_ag=pltpu.SemaphoreType.DMA((2, CHUNKS)),
        )
    return shapes


class Comm:
    def __init__(self, g, G, slots, refs, emit):
        self.g, self.G, self.slots, self.emit = g, G, slots, emit
        self.__dict__.update(refs)
        dp = lax.axis_index("dp")
        self.y = lax.axis_index("blk")
        self.c = dp % 2
        self.b = (dp // 2) % g.B
        self.a = dp // (2 * g.B)

    def dev(self, a=None, b=None, c=None, y=None):
        a = self.a if a is None else a
        b = self.b if b is None else b
        c = self.c if c is None else c
        y = self.y if y is None else y
        return ((a * self.g.B + b) * 2 + c, y)

    def partners(self):
        g = self.g
        return (
            [self.dev(c=1 - self.c)]
            + [self.dev(b=(self.b + k) % g.B) for k in range(1, g.B)]
            + [self.dev(a=(self.a + k) % g.A) for k in range(1, g.A)]
            + [self.dev(y=(self.y + k) % g.Y) for k in range(1, g.Y)]
        )

    def barrier(self):
        sem = pltpu.get_barrier_semaphore()
        others = self.partners()
        for other in others:
            pl.semaphore_signal(sem, inc=1, device_id=other, device_id_type=MESH)
        pl.semaphore_wait(sem, len(others))

    def copy(self, src, dst, sems, index, device):
        return pltpu.make_async_remote_copy(
            src_ref=src,
            dst_ref=dst,
            send_sem=sems.at[(0,) + index],
            recv_sem=sems.at[(1,) + index],
            device_id=device,
            device_id_type=MESH,
        )

    def core(self, j, kind):
        copy = self.copy(
            self.G.at[j % self.slots, 1 - self.c], self.r0.at[j % RING], self.s_core, (j,), self.dev(c=1 - self.c)
        )
        return [copy], [copy]

    def along_b(self, j, kind):
        g, i = self.g, j // self.g.kinds
        landing = self.rx2 if kind else self.rx
        cols = pl.ds(2 * self.y, 2) if kind else pl.ds(0, 4)
        copies = []
        for k in range(1, g.B):
            other = (self.b + k) % g.B
            source = self.G.at[j % self.slots, self.c, cols, other]
            copies.append(self.copy(source, landing.at[i, k - 1], self.s_x, (j, k - 1), self.dev(b=other)))
        return copies, copies

    def along_a(self, j, kind):
        g, i = self.g, j // self.g.kinds
        landing = self.rz2 if kind else self.rz
        cols = pl.ds(2 * self.y, 2) if kind else pl.ds(0, 4)
        copies = []
        for k in range(1, g.A):
            other = (self.a + k) % g.A
            source = self.G.at[j % self.slots, self.c, cols, self.b, other]
            copies.append(self.copy(source, landing.at[i, k - 1], self.s_z, (j,), self.dev(a=other)))
        return copies, [self.copy(landing.at[i], landing.at[i], self.s_z, (j,), self.dev(a=(self.a + 1) % g.A))]

    def along_blk(self, j, kind):
        g, i = self.g, j // self.g.kinds
        if kind:
            source = self.G.at[j % self.slots, self.c, pl.ds(2 * (1 - self.y), 2)]
            copies = [self.copy(source, self.ry.at[i], self.s_y, (j, 0), self.dev(y=1 - self.y))]
            return copies, copies
        mine = self.ryx.at[i, self.y]
        copies = [
            self.copy(mine, mine, self.s_y, (j, k - 1), self.dev(y=(self.y + k) % g.Y)) for k in range(1, g.Y)
        ]
        return copies, copies

    def share(self, j, kind):
        mine = self.rag.at[j // 2, self.y]
        copies = [self.copy(mine, mine, self.s_ag, (j,), self.dev(y=1 - self.y))]
        return copies, copies

    def add(self, mine, parts):
        if len(parts) == 1:
            mine[...] = mine[...] + parts[0]
        else:
            mine[...] = self.summed(mine, parts)

    def summed(self, mine, parts):
        total = mine[...].astype(F32)
        for part in parts:
            total = total + part.astype(F32)
        return total.astype(BF)

    def after_core(self, j, kind):
        self.add(self.G.at[j % self.slots, self.c], [self.r0[j % RING]])

    def after_b(self, j, kind):
        g, i = self.g, j // self.g.kinds
        landing = self.rx2 if kind else self.rx
        cols = pl.ds(2 * self.y, 2) if kind else pl.ds(0, 4)
        self.add(self.G.at[j % self.slots, self.c, cols, self.b], [landing[i, k] for k in range(g.B - 1)])

    def after_a(self, j, kind):
        g, i = self.g, j // self.g.kinds
        landing = self.rz2 if kind else self.rz
        cols = pl.ds(2 * self.y, 2) if kind else pl.ds(0, 4)
        total = self.summed(
            self.G.at[j % self.slots, self.c, cols, self.b, self.a], [landing[i, k] for k in range(g.A - 1)]
        )
        if kind:
            self.rag[i, self.y] = total
        else:
            self.ryx[i, self.y] = total

    def after_blk(self, j, kind):
        g, i = self.g, j // self.g.kinds
        if kind:
            self.add(self.G.at[j % self.slots, self.c, pl.ds(2 * self.y, 2)], [self.ry[i]])
            return
        total = self.ryx[i, 0].astype(F32)
        for k in range(1, g.Y):
            total = total + self.ryx[i, k].astype(F32)
        self.emit(j, [total[col] for col in range(4)])

    def after_share(self, j, kind):
        i = j // 2
        self.emit(j, [self.rag[i, col // 2, col % 2].astype(F32) for col in range(4)])

    def plan(self, kind):
        core = (self.core, self.after_core)
        b = (self.along_b, self.after_b)
        a = (self.along_a, self.after_a)
        blk = (self.along_blk, self.after_blk)
        share = (self.share, self.after_share)
        return (core, blk, b, a, share) if kind else (core, b, a, blk)

    def start(self, j):
        self.core(j, 0)[0][0].start()

    def finish(self, stage, j):
        for kind in range(self.g.kinds):
            plan = self.plan(kind)
            if stage >= len(plan):
                continue

            def go(kind=kind, plan=plan):
                for copy in plan[stage][0](j, kind)[1]:
                    copy.wait()
                plan[stage][1](j, kind)
                if stage + 1 < len(plan):
                    for copy in plan[stage + 1][0](j, kind)[0]:
                        copy.start()

            if self.g.kinds == 1:
                go()
            elif isinstance(j, int):
                if j % 2 == kind:
                    go()
            else:
                pl.when(j % 2 == kind)(go)

    def advance(self, t):
        for stage in range(5):
            twice = t - AFTER[stage]
            if twice % 2 == 0 and 0 <= twice < 2 * CHUNKS:
                self.finish(stage, twice // 2)

    def advance_two(self, t, odd):
        for stage in range(5):
            if (odd - AFTER[stage]) % 2 == 0:
                j = t + (odd - AFTER[stage]) // 2

                @pl.when((j >= 0) & (j < CHUNKS))
                def _(stage=stage, j=j):
                    self.finish(stage, j)


def emit_to(g, j_ref, o_ref, e_ref, r_ref):
    R = g.R

    def emit(j, values):
        @pl.when(j < 6)
        def _():
            for col in range(4):
                e_ref[:, pl.ds(pl.multiple_of(j * 512 + col * 128, 128), 128)] = values[col]

        @pl.when((j >= 6) & (j < 12))
        def _():
            for k in range(4):
                r_ref[k * R : (k + 1) * R, pl.ds(pl.multiple_of((j - 6) * 128, 128), 128)] = values[k]

        @pl.when(j >= 12)
        def _():
            at = pl.multiple_of((j - 12) * 128, 128)
            for k in range(3):
                j_ref[:, pl.ds(pl.multiple_of(k * 768 + at, 128), 128)] = values[k]
            o_ref[:, pl.ds(at, 128)] = values[3]

    return emit


HEADS = 12
VECTORS = (
    "entry_gain", "entry_shift", "joint_bias", "output_bias",
    "middle_gain", "middle_shift", "expand_bias", "reduce_bias",
)
HD = 64
D = 768
FF = 3072
ROWS = 512
EDGE = 128
SPAN = 3 * EDGE
PAIRS = HEADS // 2
NEAR = 112
SLOTS = 12
STREAM = 2
TICK = 512
TICKS = FF // TICK


def nn(left, right):
    return jnp.dot(left, right, preferred_element_type=F32)


def nt(left, right):
    return lax.dot_general(left, right, (((1,), (1,)), ((), ())), preferred_element_type=F32)


def stats(values):
    average = jnp.mean(values, axis=-1, keepdims=True)
    centred = values - average
    spread = jnp.mean(centred * centred, axis=-1, keepdims=True)
    inverse = lax.rsqrt(spread + 1e-06)
    return centred * inverse, inverse


def normal_parts(hidden):
    half = hidden * (0.5**0.5)
    size = jnp.abs(half)
    ratio = 1.0 / (1.0 + 0.3275911 * size)
    bell = jnp.exp(-half * half)
    tail = ((((1.061405429 * ratio - 1.453152027) * ratio + 1.421413741) * ratio - 0.284496736) * ratio + 0.254829592) * ratio
    tail = 0.5 * tail * bell
    share = jnp.where(hidden >= 0, 1.0 - tail, tail)
    return share, hidden * bell * 0.3989422804014327


def column_sum(values):
    return jnp.sum(values, axis=0, keepdims=True)


def layer_kernel(g, names, *refs):
    r = dict(zip(names, refs))
    A, B, R, Y = g.A, g.B, g.R, g.Y
    (patches, cotangent, segments, w_joint, w_output, w_expand, w_reduce) = (
        r[n] for n in ("patches", "cotangent", "segments", "w_joint", "w_output", "w_expand", "w_reduce")
    )
    G, vec = r["G"], r["vec"]
    for name in VECTORS:
        r[name + "_row"][...] = r[name][...].reshape(1, -1)
        r[name] = r[name + "_row"]
    r["oe"], r["oo"] = r["vT"], r["n2"]
    out_rows, dx_rows = r["k"].at[pl.ds(0, ROWS)], r["ml"]
    x, xh, dy = r["x"], r["xh"], r["dy"]
    comm = Comm(g, G, SLOTS, r, emit_to(g, r["j_out"], r["o_out"], r["e_out"], r["r_out"]))
    y = comm.y
    has_left, has_right = y > 0, y < Y - 1

    def load(src, dst, k):
        return pltpu.make_async_copy(src, dst, r["load"].at[k])

    load_x = load(patches, x, 0)
    load_wj = load(w_joint, r["wj"], 1)
    load_wo = load(w_output, r["wo"], 2)
    load_dy = load(cotangent, dy, 3)

    def ffn_loads(i):
        s = i % STREAM
        at = pl.ds(pl.multiple_of(i * TICK, TICK), TICK)
        return (
            pltpu.make_async_copy(w_expand.at[:, at], r["we"].at[s], r["stream"].at[0, s]),
            pltpu.make_async_copy(w_reduce.at[at], r["wr"].at[s], r["stream"].at[1, s]),
        )

    load_x.start()
    load_wj.start()
    comm.barrier()

    def edge(k, side, src, dst, sems):
        other = comm.dev(y=(y + Y - 1) % Y) if side == 0 else comm.dev(y=(y + 1) % Y)
        return pltpu.make_async_remote_copy(
            src_ref=src, dst_ref=dst, send_sem=sems.at[(0,) + k + (side,)], recv_sem=sems.at[(1,) + k + (1 - side,)],
            device_id=other, device_id_type=MESH,
        )

    def x_edges():
        return (
            edge((), 0, patches.at[pl.ds(0, EDGE)], xh.at[1], r["s_edge"]),
            edge((), 1, patches.at[pl.ds(ROWS - EDGE, EDGE)], xh.at[0], r["s_edge"]),
        )

    to_left, to_right = x_edges()

    @pl.when(has_left)
    def _():
        to_left.start()

    @pl.when(has_right)
    def _():
        to_right.start()

    @pl.when(jnp.logical_not(has_left))
    def _():
        xh[0] = jnp.zeros((EDGE, D), BF)

    @pl.when(jnp.logical_not(has_right))
    def _():
        xh[1] = jnp.zeros((EDGE, D), BF)

    first_block = y * (ROWS // EDGE)
    count = segments.shape[0]
    columns = []
    for k in range(6):
        index = first_block + k - 1
        inside = (index >= 0) & (index < count)
        row = segments[pl.ds(jnp.clip(index, 0, count - 1), 1), :]
        row = jnp.where(inside, row, -1)
        columns.append(row)
    for b in range(4):
        for k in range(3):
            keys = jnp.broadcast_to(columns[b + k].astype(F32), (EDGE, EDGE)).T
            own = columns[b + 1].astype(F32)
            r["bias"][b, k * EDGE : (k + 1) * EDGE, :] = jnp.where(keys == own, 0.0, -1e30)

    vec[...] = jnp.zeros_like(vec)
    entry_gain, entry_shift = r["entry_gain"][...], r["entry_shift"][...]
    lanes = lax.broadcasted_iota(jnp.int32, (1, D), 1) % 128
    even = lanes < HD

    def project(rows, at, own, row_at):
        count = rows.shape[0]
        normal, _ = stats(rows.astype(F32))
        low = (normal * entry_gain + entry_shift).astype(BF)
        wj = r["wj"]
        key_rows = nn(low, wj[:, D : 2 * D]).astype(BF)
        r["k"][pl.ds(at, count), :] = key_rows
        r["kT"][:, pl.ds(at, count)] = key_rows.T
        value_rows = (nn(low, wj[:, 2 * D :]) + r["joint_bias"][:, D:]).astype(BF)
        r["v"][pl.ds(at, count), :] = value_rows
        r["vT"][:, pl.ds(at, count)] = value_rows.T
        if own:
            r["n1T"][:, pl.ds(row_at, count)] = low.T
            queries = (nn(low, wj[:, :D]) + r["joint_bias"][:, :D]).astype(BF) * BF(HD**-0.5)
            r["qe"][pl.ds(row_at, count), :] = jnp.where(even, queries, BF(0))
            r["qo"][pl.ds(row_at, count), :] = jnp.where(even, BF(0), queries)

    load_x.wait()
    load_wj.wait()
    load_wo.start()
    load_dy.start()
    for i in range(STREAM):
        for copy in ffn_loads(i):
            copy.start()

    def own_rows(i, _):
        at = pl.multiple_of(i * 256, 256)
        project(x[pl.ds(at, 256), :], pl.multiple_of(at + EDGE, EDGE), True, at)
        return 0

    lax.fori_loop(0, 2, own_rows, 0)

    @pl.when(has_left)
    def _():
        to_left.wait_send()
        to_right.wait_recv() if Y == 1 else edge((), 1, patches.at[pl.ds(0, EDGE)], xh.at[0], r["s_edge"]).wait_recv()

    @pl.when(has_right)
    def _():
        to_right.wait_send()
        edge((), 0, patches.at[pl.ds(0, EDGE)], xh.at[1], r["s_edge"]).wait_recv()

    def edge_rows(i, _):
        project(xh[i], pl.multiple_of(i * (ROWS + EDGE), EDGE), False, 0)
        return 0

    lax.fori_loop(0, 2, edge_rows, 0)

    top = lax.broadcasted_iota(jnp.int32, (EDGE, 1), 0) < HD

    def scores_of(p, b):
        at = pl.ds(pl.multiple_of(p * 128, 128), 128)
        keys, own = pl.ds(b * EDGE, SPAN), pl.ds(b * EDGE, EDGE)
        both = jnp.concatenate([r["qe"][own, at], r["qo"][own, at]], axis=0)
        return nt(r["k"][keys, at], both)

    def probs_of(b, scores):
        bias = r["bias"][b]
        scores = scores + jnp.concatenate([bias, bias], axis=1)
        powers = jnp.exp(scores - jnp.max(scores, axis=0, keepdims=True))
        return (powers * (1.0 / column_sum(powers))).astype(BF)

    def mix(p, b, probs):
        at = pl.ds(pl.multiple_of(p * 128, 128), 128)
        keys, own = pl.ds(b * EDGE, SPAN), pl.ds(b * EDGE, EDGE)
        r["probs"][p, b] = probs
        mixed = nn(r["vT"][at, keys], probs)
        r["attT"][at, own] = jnp.where(top, mixed[:, :128], mixed[:, 128:]).astype(BF)

    def attend(p, _):
        scores = scores_of(p, 0)
        before = None
        for b in range(4):
            following = scores_of(p, b + 1) if b < 3 else None
            probs = probs_of(b, scores)
            if b > 0:
                mix(p, b - 1, before)
            before, scores = probs, following
        mix(p, 3, before)
        return 0

    lax.fori_loop(0, PAIRS, attend, 0)

    load_wo.wait()
    mid, total, n2, n2T = r["mid"], r["total"], r["n2"], r["n2T"]
    middle_gain, middle_shift = r["middle_gain"][...], r["middle_shift"][...]

    def finish_attention(i, _):
        at = pl.ds(pl.multiple_of(i * 256, 256), 256)
        mixed = r["attT"][:, at].T
        middle = x[at, :].astype(F32) + nn(mixed, r["wo"][...]) + r["output_bias"][...]
        mid[at, :] = middle
        total[at, :] = middle + r["reduce_bias"][...]
        normal, _ = stats(middle)
        low = (normal * middle_gain + middle_shift).astype(BF)
        n2[at, :] = low
        n2T[:, at] = low.T
        r["dn"][at, :] = jnp.zeros((256, D), F32)
        return 0

    lax.fori_loop(0, 2, finish_attention, 0)
    load_dy.wait()

    def feed_forward(i, _):
        s = i % STREAM
        for copy in ffn_loads(i):
            copy.wait()
        we, wr = r["we"].at[s], r["wr"].at[s]
        at = pl.ds(pl.multiple_of(i * TICK, TICK), TICK)
        bias = r["expand_bias"][:, at]
        bias_sum = jnp.zeros((1, TICK), F32)
        rows = [pl.ds(half * 256, 256) for half in range(2)]
        hidden = [nn(n2[part, :], we[...]) + bias for part in rows]
        back = [nt(dy[part, :], wr[...]) for part in rows]
        for half, part in enumerate(rows):
            share, slope = normal_parts(hidden[half])
            active = (hidden[half] * share).astype(BF)
            hidden_gradient = back[half] * (share + slope)
            bias_sum = bias_sum + column_sum(hidden_gradient)
            low = hidden_gradient.astype(BF)
            r["hl"][part, :] = low
            r["actT"][at, part] = active.T
            total[part, :] += nn(active, wr[...])
            r["dn"][part, :] += nt(low, we[...])
            if half == 0:
                comm.advance_two(i, -1)
        r["eb"][:, at] = bias_sum
        for part in range(2):
            block = nn(n2T[part * 384 : (part + 1) * 384, :], r["hl"][...]).astype(BF)
            store_rows(block, i, part * 2, 2)
        comm.start(i)

        @pl.when(i + STREAM < TICKS)
        def _():
            for copy in ffn_loads(i + STREAM):
                copy.start()

        comm.advance_two(i, 0)
        return 0

    def store_rows(block, chunk, a0, na):
        slot = chunk % SLOTS
        for a in range(na):
            for b in range(B):
                for c in range(2):
                    row = ((a * B + b) * 2 + c) * R
                    for col in range(block.shape[1] // 128):
                        G[slot, c, col, b, a0 + a] = block[row : row + R, col * 128 : (col + 1) * 128]

    lax.fori_loop(0, TICKS, feed_forward, 0)

    def reduce_gradient(p, _):
        at = pl.ds(pl.multiple_of(p * 256, 256), 256)
        chunk = 6 + 2 * p

        def part(a, _):
            block = nn(r["actT"][pl.ds(pl.multiple_of(a * D, D), D), :], dy[:, at]).astype(BF)
            for h in range(2):
                slot = (chunk + h) % SLOTS
                for b in range(B):
                    for c in range(2):
                        for k in range(4):
                            row = ((b * 2 + c) * 4 + k) * R
                            G[slot, c, k, b, a] = block[row : row + R, h * 128 : (h + 1) * 128]
            return 0

        lax.fori_loop(0, A, part, 0)
        comm.start(chunk)
        comm.start(chunk + 1)
        comm.advance_two(6 + p, -1)
        comm.advance_two(6 + p, 0)
        return 0

    lax.fori_loop(0, 3, reduce_gradient, 0)

    def middle_back(i, _):
        at = pl.ds(pl.multiple_of(i * 256, 256), 256)
        out_rows[at, :] = total[at, :].astype(BF)
        error = r["dn"][at, :]
        normal, inverse = stats(mid[at, :])
        scaled = error * middle_gain
        part = inverse * (
            scaled
            - jnp.mean(scaled, axis=-1, keepdims=True)
            - normal * jnp.mean(scaled * normal, axis=-1, keepdims=True)
        )
        incoming = dy[at, :].astype(F32)
        gradient = incoming + part
        vec[5:6, :] += column_sum(error * normal)
        vec[6:7, :] += column_sum(error)
        vec[4:5, :] += column_sum(gradient)
        vec[11:12, :] += column_sum(incoming)
        mid[at, :] = gradient
        low = gradient.astype(BF)
        r["ml"][at, :] = low
        back = nt(low, r["wo"][...]).astype(BF)
        r["oe"][at, :] = jnp.where(even, back, BF(0))
        r["oo"][at, :] = jnp.where(even, BF(0), back)
        total[at, :] = jnp.zeros((256, D), F32)
        return 0

    lax.fori_loop(0, 2, middle_back, 0)
    save_out = pltpu.make_async_copy(out_rows, r["out"], r["save"].at[0])
    save_out.start()
    for k in range(4):
        vec[7 + k : 8 + k, :] = r["eb"][:, k * D : (k + 1) * D]
    comm.advance(17)
    comm.advance(18)

    parts, jq, sent, got, s_part = r["parts"], r["jq"], r["sent"], r["got"], r["s_part"]

    def part_copies(p):
        return (
            edge((p,), 0, sent.at[p % 2, 0], got.at[p, 1], s_part),
            edge((p,), 1, sent.at[p % 2, 1], got.at[p, 0], s_part),
        )

    def attend_back(p):
        at = pl.ds(pl.multiple_of(p * 128, 128), 128)
        slot = p % 2
        own_sum = jnp.zeros((1, 128), F32)
        parts[slot] = jnp.zeros((ROWS + 2 * EDGE, 256), F32)

        def errors_of(b):
            own = pl.ds(b * EDGE, EDGE)
            return jnp.concatenate([r["oe"][own, at], r["oo"][own, at]], axis=0)

        def shares_of(b):
            return nt(r["v"][pl.ds(b * EDGE, SPAN), at], errors_of(b))

        def score_gradient_of(b, shares):
            wide = r["probs"][p, b].astype(F32)
            product = wide * shares
            return (product - wide * column_sum(product)).astype(BF)

        def spread(b, low):
            keys, own = pl.ds(b * EDGE, SPAN), pl.ds(b * EDGE, EDGE)
            queries = jnp.concatenate([r["qe"][own, at], r["qo"][own, at]], axis=0)
            parts[slot, keys, 0:128] += nn(low, queries)
            parts[slot, keys, 128:256] += nn(r["probs"][p, b], errors_of(b))
            turned = nn(r["kT"][at, keys], low)
            mine = (jnp.where(top, turned[:, :128], turned[:, 128:]) * HD**-0.5).T
            jq[slot, own, :] = mine.astype(BF)
            return column_sum(mine)

        shares = shares_of(0)
        before = None
        for b in range(4):
            following = shares_of(b + 1) if b < 3 else None
            low = score_gradient_of(b, shares)
            if b > 0:
                own_sum = own_sum + spread(b - 1, before)
            before, shares = low, following
        own_sum = own_sum + spread(3, before)
        vec[2:3, at] = own_sum
        to_left, to_right = part_copies(p)

        @pl.when(has_left)
        def _():
            sent[slot, 0] = parts[slot, EDGE - NEAR : EDGE, :].astype(BF)
            to_left.start()

        @pl.when(has_right)
        def _():
            sent[slot, 1] = parts[slot, ROWS + EDGE : ROWS + EDGE + NEAR, :].astype(BF)
            to_right.start()

    def joint_gradient(p):
        at = pl.ds(pl.multiple_of(p * 128, 128), 128)
        slot = p % 2
        to_left, to_right = part_copies(p)

        @pl.when(has_left)
        def _():
            to_left.wait_send()
            to_right.wait_recv()
            parts[slot, EDGE : EDGE + NEAR, :] += got[p, 0].astype(F32)

        @pl.when(has_right)
        def _():
            to_right.wait_send()
            to_left.wait_recv()
            parts[slot, ROWS + EDGE - NEAR : ROWS + EDGE, :] += got[p, 1].astype(F32)

        sums = parts[slot, EDGE : ROWS + EDGE, :]
        vec[3:4, at] = column_sum(sums[:, 128:])
        low = jnp.concatenate([jq[slot], sums.astype(BF)], axis=1)
        wj = r["wj"]
        weights = jnp.concatenate([wj[:, pl.ds(pl.multiple_of(k * D + p * 128, 128), 128)] for k in range(3)], axis=1)
        total[...] += nt(low, weights)
        low_out = r["ml"][:, at]
        for part in range(2):
            rows = pl.ds(part * 384, 384)
            block = nn(r["n1T"][rows, :], low).astype(BF)
            block_out = nn(r["attT"][rows, :], low_out).astype(BF)
            store_rows(jnp.concatenate([block, block_out], axis=1), 12 + p, part * 2, 2)
        comm.start(12 + p)

    def pair_step(i, _):
        @pl.when(i < PAIRS)
        def _():
            attend_back(i)

        comm.advance_two(9 + i, 1)

        @pl.when(i > 0)
        def _():
            joint_gradient(i - 1)

        comm.advance_two(10 + i, 0)
        return 0

    lax.fori_loop(0, PAIRS + 1, pair_step, 0)

    def entry_back(i, _):
        at = pl.ds(pl.multiple_of(i * 256, 256), 256)
        error = total[at, :]
        normal, inverse = stats(x[at, :].astype(F32))
        scaled = error * entry_gain
        part = inverse * (
            scaled
            - jnp.mean(scaled, axis=-1, keepdims=True)
            - normal * jnp.mean(scaled * normal, axis=-1, keepdims=True)
        )
        vec[0:1, :] += column_sum(error * normal)
        vec[1:2, :] += column_sum(error)
        dx_rows[at, :] = (mid[at, :] + part).astype(BF)
        return 0

    lax.fori_loop(0, 2, entry_back, 0)
    save_dx = pltpu.make_async_copy(dx_rows, r["dx"], r["save"].at[1])
    save_dx.start()

    rv, s_vec = r["rv"], r["s_vec"]

    def vector_copies(step):
        groups = (
            [comm.dev(c=1 - comm.c)],
            [comm.dev(b=(comm.b + k) % B) for k in range(1, B)],
            [comm.dev(a=(comm.a + k) % A) for k in range(1, A)],
            [comm.dev(y=(comm.y + k) % Y) for k in range(1, Y)],
        )
        ids = (comm.c, comm.b, comm.a, comm.y)
        base = (0, 2, 0, A)[step]
        held = rv if step < 2 else r["rvl"]
        here = held.at[base + ids[step]]
        return here, [
            comm.copy(here, here, s_vec, ((0, 2, 2 + B, 2 + B + A)[step] + k,), other) for k, other in enumerate(groups[step])
        ]

    def vector_sum(step):
        base, size = ((0, 2), (2, B), (0, A), (A, Y))[step]
        held = rv if step < 2 else r["rvl"]
        value = held[base].astype(F32)
        for k in range(1, size):
            value = value + held[base + k].astype(F32)
        return value

    def vector_start(step, value):
        here, copies = vector_copies(step)
        here[...] = value.astype(here.dtype)
        for copy in copies:
            copy.start()

    def vector_wait(step):
        for copy in vector_copies(step)[1]:
            copy.wait()

    vector_start(0, vec[...])
    for step in range(4):
        comm.advance(33 + 2 * step)
        comm.advance(34 + 2 * step)
        vector_wait(step)
        if step < 3:
            vector_start(step + 1, vector_sum(step))
    summed = vector_sum(3)
    place = lax.axis_index("dp")
    spot = lax.broadcasted_iota(jnp.int32, (D, 512), 0)
    lane = lax.broadcasted_iota(jnp.int32, (D, 512), 1)
    n2v, n4v = g.dp // 2, g.dp // 4
    want = jnp.where(
        lane < 128,
        lane + place * R,
        jnp.where(lane < 256, lane - 128 + (place % n2v) * (2 * R), lane - 256 + (place % n4v) * (4 * R)),
    )
    pick = jnp.where(spot == want, 1.0, 0.0).astype(F32)
    picked = jnp.dot(summed, pick, precision=lax.Precision.HIGHEST, preferred_element_type=F32)
    kind = lax.broadcasted_iota(jnp.int32, (16, 1), 0)
    r["v_out"][...] = picked[:, 0:128]
    r["jb_out"][...] = column_sum(jnp.where(kind == 2 + place // n2v, picked[:, 128:256], 0.0))
    r["eb_out"][...] = column_sum(jnp.where(kind == 7 + place // n4v, picked[:, 256:512], 0.0))
    for t in range(41, 2 * CHUNKS + AFTER[4]):
        comm.advance(t)
    save_out.wait()
    save_dx.wait()


def layer(g, patches, segments, vectors, weights, cotangent):
    A, B, R, Y = g.A, g.B, g.R, g.Y
    comm_shapes = comm_scratch(g)
    V = pl.BlockSpec(memory_space=pltpu.VMEM)
    H = pl.BlockSpec(memory_space=pl.ANY)
    inputs = dict(
        patches=(patches, H),
        cotangent=(cotangent, H),
        segments=(segments, V),
        w_joint=(weights[0], H),
        w_output=(weights[1], H),
        w_expand=(weights[2], H),
        w_reduce=(weights[3], H),
        **{name: (value, V) for name, value in vectors.items()},
    )
    outputs = dict(
        out=((ROWS, D), BF),
        dx=((ROWS, D), BF),
        j_out=((R, 3 * D), F32),
        o_out=((R, D), F32),
        e_out=((R, FF), F32),
        r_out=((4 * R, D), F32),
        v_out=((16, 128), F32),
        jb_out=((1, 128), F32),
        eb_out=((1, 256), F32),
    )
    ext = ROWS + 2 * EDGE
    scratch = dict(
        x=pltpu.VMEM((ROWS, D), BF),
        xh=pltpu.VMEM((2, EDGE, D), BF),
        dy=pltpu.VMEM((ROWS, D), BF),
        wj=pltpu.VMEM((D, 3 * D), BF),
        wo=pltpu.VMEM((D, D), BF),
        we=pltpu.VMEM((STREAM, D, TICK), BF),
        wr=pltpu.VMEM((STREAM, TICK, D), BF),
        n1T=pltpu.VMEM((D, ROWS), BF),
        qe=pltpu.VMEM((ROWS, D), BF),
        qo=pltpu.VMEM((ROWS, D), BF),
        k=pltpu.VMEM((ext, D), BF),
        v=pltpu.VMEM((ext, D), BF),
        kT=pltpu.VMEM((D, ext), BF),
        vT=pltpu.VMEM((D, ext), BF),
        bias=pltpu.VMEM((4, SPAN, EDGE), F32),
        probs=pltpu.VMEM((PAIRS, 4, SPAN, 2 * EDGE), BF),
        attT=pltpu.VMEM((D, ROWS), BF),
        mid=pltpu.VMEM((ROWS, D), F32),
        total=pltpu.VMEM((ROWS, D), F32),
        dn=pltpu.VMEM((ROWS, D), F32),
        n2=pltpu.VMEM((ROWS, D), BF),
        n2T=pltpu.VMEM((D, ROWS), BF),
        hl=pltpu.VMEM((ROWS, TICK), BF),
        actT=pltpu.VMEM((FF, ROWS), BF),
        eb=pltpu.VMEM((1, FF), F32),
        ml=pltpu.VMEM((ROWS, D), BF),
        parts=pltpu.VMEM((2, ext, 256), F32),
        jq=pltpu.VMEM((2, ROWS, 128), BF),
        sent=pltpu.VMEM((2, 2, NEAR, 256), BF),
        got=pltpu.VMEM((PAIRS, 2, NEAR, 256), BF),
        vec=pltpu.VMEM((16, D), F32),
        rv=pltpu.VMEM((2 + B, 16, D), F32),
        rvl=pltpu.VMEM((A + Y, 16, D), BF),
        G=pltpu.VMEM((SLOTS, 2, 4, B, A, R, 128), BF),
        load=pltpu.SemaphoreType.DMA((4,)),
        save=pltpu.SemaphoreType.DMA((2,)),
        stream=pltpu.SemaphoreType.DMA((2, STREAM)),
        s_edge=pltpu.SemaphoreType.DMA((2, 2)),
        s_part=pltpu.SemaphoreType.DMA((2, PAIRS, 2)),
        s_vec=pltpu.SemaphoreType.DMA((2, 2 + B + A + Y)),
        **{name + "_row": pltpu.VMEM((1, value.shape[0]), F32) for name, value in vectors.items()},
        **comm_shapes,
    )
    names = (*inputs, *outputs, *scratch)
    results = pl.pallas_call(
        functools.partial(layer_kernel, g, names),
        out_shape=tuple(jax.ShapeDtypeStruct(*shape) for shape in outputs.values()),
        in_specs=[spec for _, spec in inputs.values()],
        out_specs=[H, H] + [V] * (len(outputs) - 2),
        scratch_shapes=list(scratch.values()),
        compiler_params=pltpu.CompilerParams(
            collective_id=0, has_side_effects=True, vmem_limit_bytes=64 << 20
        ),
    )(*(value for value, _ in inputs.values()))
    return hand_over(g, dict(zip(outputs, results)))


def hand_over_kernel(g, out, dx, j, o, e, w, v, jb, eb, *refs):
    outs, sems = refs[:14], refs[14]
    R = g.R
    moves = [(out, 0), (dx, 1), (j, 4), (o, 6), (e, 10), (w, 12)]
    copies = [pltpu.make_async_copy(src, outs[k], sems.at[i]) for i, (src, k) in enumerate(moves)]
    for copy in copies:
        copy.start()
    for row, k in ((0, 2), (1, 3), (4, 7), (5, 8), (6, 9), (11, 13)):
        outs[k][...] = v[row, :R]
    outs[5][...] = jb[0, : 2 * R]
    outs[11][...] = eb[0, : 4 * R]
    for copy in copies:
        copy.wait()


def hand_over(g, o):
    R = g.R
    V = pl.BlockSpec(memory_space=pltpu.VMEM)
    H = pl.BlockSpec(memory_space=pl.ANY)
    shapes = [
        ((ROWS, D), BF), ((ROWS, D), BF), ((R,), F32), ((R,), F32), ((R, 3 * D), F32), ((2 * R,), F32), ((R, D), F32),
        ((R,), F32), ((R,), F32), ((R,), F32), ((R, FF), F32), ((4 * R,), F32), ((4 * R, D), F32), ((R,), F32),
    ]
    names = ("out", "dx", "j_out", "o_out", "e_out", "r_out", "v_out", "jb_out", "eb_out")
    return pl.pallas_call(
        functools.partial(hand_over_kernel, g),
        out_shape=tuple(jax.ShapeDtypeStruct(*shape) for shape in shapes),
        in_specs=[V] * 9,
        out_specs=[V if len(shape) == 1 else H for shape, _ in shapes],
        scratch_shapes=[pltpu.SemaphoreType.DMA((6,))],
    )(*(o[name] for name in names))


def local(
    patches,
    segments,
    entry_gain,
    entry_shift,
    joint_weight,
    joint_bias,
    output_weight,
    output_bias,
    middle_gain,
    middle_shift,
    expand_weight,
    expand_bias,
    reduce_weight,
    reduce_bias,
    cotangent,
):
    g = Grid(lax.axis_size("dp"), lax.axis_size("blk"), D)
    R = g.R
    vectors = dict(
        entry_gain=entry_gain,
        entry_shift=entry_shift,
        joint_bias=joint_bias,
        output_bias=output_bias,
        middle_gain=middle_gain,
        middle_shift=middle_shift,
        expand_bias=expand_bias,
        reduce_bias=reduce_bias,
    )
    o = layer(
        g,
        patches[0],
        segments.reshape(-1, EDGE),
        vectors,
        (joint_weight, output_weight, expand_weight, reduce_weight),
        cotangent[0],
    )
    return (o[0][None], o[1][None], *o[2:])


def solution(mesh):
    return jax.shard_map(
        local,
        mesh=mesh,
        in_specs=(
            P("dp", "blk", None),
            P("dp", None),
            P(),
            P(),
            P(),
            P(),
            P(),
            P(),
            P(),
            P(),
            P(),
            P(),
            P(),
            P(),
            P("dp", "blk", None),
        ),
        out_specs=(
            P("dp", "blk", None),
            P("dp", "blk", None),
            P("dp"),
            P("dp"),
            P("dp", None),
            P("dp"),
            P("dp", None),
            P("dp"),
            P("dp"),
            P("dp"),
            P("dp", None),
            P("dp"),
            P("dp", None),
            P("dp"),
        ),
        check_vma=False,
    )
```

```python
import functools
import jax
import jax.numpy as jnp
from jax import lax
from jax.experimental import pallas as pl
from jax.experimental.pallas import tpu as pltpu
from jax.sharding import PartitionSpec as P

MESH = pl.DeviceIdType.MESH
CHUNKS = 18
AFTER = (2, 6, 10, 14, 18)
RING = 9
BF = jnp.bfloat16
F32 = jnp.float32


class Grid:
    def __init__(self, dp, blk, width):
        self.A = 4
        self.B = dp // 8
        self.Y = blk
        self.dp = dp
        self.R = width // dp
        self.kinds = 2 if blk == 2 else 1


def comm_scratch(g):
    A, B, Y, R = g.A, g.B, g.Y, g.R
    n = CHUNKS // g.kinds
    shapes = dict(
        r0=pltpu.VMEM((RING, 4, B, A, R, 128), BF),
        rx=pltpu.VMEM((n, B - 1, 4, A, R, 128), BF),
        rz=pltpu.VMEM((n, A - 1, 4, R, 128), BF),
        ryx=pltpu.VMEM((n, Y, 4, R, 128), BF),
        s_core=pltpu.SemaphoreType.DMA((2, CHUNKS)),
        s_x=pltpu.SemaphoreType.DMA((2, CHUNKS, B - 1)),
        s_z=pltpu.SemaphoreType.DMA((2, CHUNKS)),
        s_y=pltpu.SemaphoreType.DMA((2, CHUNKS, Y - 1)),
    )
    if g.kinds == 2:
        shapes.update(
            ry=pltpu.VMEM((n, 2, B, A, R, 128), BF),
            rx2=pltpu.VMEM((n, B - 1, 2, A, R, 128), BF),
            rz2=pltpu.VMEM((n, A - 1, 2, R, 128), BF),
            rag=pltpu.VMEM((n, 2, 2, R, 128), BF),
            s_ag=pltpu.SemaphoreType.DMA((2, CHUNKS)),
        )
    return shapes


class Comm:
    def __init__(self, g, G, slots, refs, emit):
        self.g, self.G, self.slots, self.emit = g, G, slots, emit
        self.__dict__.update(refs)
        dp = lax.axis_index("dp")
        self.y = lax.axis_index("blk")
        self.c = dp % 2
        self.b = (dp // 2) % g.B
        self.a = dp // (2 * g.B)

    def dev(self, a=None, b=None, c=None, y=None):
        a = self.a if a is None else a
        b = self.b if b is None else b
        c = self.c if c is None else c
        y = self.y if y is None else y
        return ((a * self.g.B + b) * 2 + c, y)

    def partners(self):
        g = self.g
        return (
            [self.dev(c=1 - self.c)]
            + [self.dev(b=(self.b + k) % g.B) for k in range(1, g.B)]
            + [self.dev(a=(self.a + k) % g.A) for k in range(1, g.A)]
            + [self.dev(y=(self.y + k) % g.Y) for k in range(1, g.Y)]
        )

    def barrier(self):
        sem = pltpu.get_barrier_semaphore()
        others = self.partners()
        for other in others:
            pl.semaphore_signal(sem, inc=1, device_id=other, device_id_type=MESH)
        pl.semaphore_wait(sem, len(others))

    def copy(self, src, dst, sems, index, device):
        return pltpu.make_async_remote_copy(
            src_ref=src,
            dst_ref=dst,
            send_sem=sems.at[(0,) + index],
            recv_sem=sems.at[(1,) + index],
            device_id=device,
            device_id_type=MESH,
        )

    def core(self, j, kind):
        copy = self.copy(
            self.G.at[j % self.slots, 1 - self.c], self.r0.at[j % RING], self.s_core, (j,), self.dev(c=1 - self.c)
        )
        return [copy], [copy]

    def along_b(self, j, kind):
        g, i = self.g, j // self.g.kinds
        landing = self.rx2 if kind else self.rx
        cols = pl.ds(2 * self.y, 2) if kind else pl.ds(0, 4)
        copies = []
        for k in range(1, g.B):
            other = (self.b + k) % g.B
            source = self.G.at[j % self.slots, self.c, cols, other]
            copies.append(self.copy(source, landing.at[i, k - 1], self.s_x, (j, k - 1), self.dev(b=other)))
        return copies, copies

    def along_a(self, j, kind):
        g, i = self.g, j // self.g.kinds
        landing = self.rz2 if kind else self.rz
        cols = pl.ds(2 * self.y, 2) if kind else pl.ds(0, 4)
        copies = []
        for k in range(1, g.A):
            other = (self.a + k) % g.A
            source = self.G.at[j % self.slots, self.c, cols, self.b, other]
            copies.append(self.copy(source, landing.at[i, k - 1], self.s_z, (j,), self.dev(a=other)))
        return copies, [self.copy(landing.at[i], landing.at[i], self.s_z, (j,), self.dev(a=(self.a + 1) % g.A))]

    def along_blk(self, j, kind):
        g, i = self.g, j // self.g.kinds
        if kind:
            source = self.G.at[j % self.slots, self.c, pl.ds(2 * (1 - self.y), 2)]
            copies = [self.copy(source, self.ry.at[i], self.s_y, (j, 0), self.dev(y=1 - self.y))]
            return copies, copies
        mine = self.ryx.at[i, self.y]
        copies = [
            self.copy(mine, mine, self.s_y, (j, k - 1), self.dev(y=(self.y + k) % g.Y)) for k in range(1, g.Y)
        ]
        return copies, copies

    def share(self, j, kind):
        mine = self.rag.at[j // 2, self.y]
        copies = [self.copy(mine, mine, self.s_ag, (j,), self.dev(y=1 - self.y))]
        return copies, copies

    def add(self, mine, parts):
        if len(parts) == 1:
            mine[...] = mine[...] + parts[0]
        else:
            mine[...] = self.summed(mine, parts)

    def summed(self, mine, parts):
        total = mine[...].astype(F32)
        for part in parts:
            total = total + part.astype(F32)
        return total.astype(BF)

    def after_core(self, j, kind):
        self.add(self.G.at[j % self.slots, self.c], [self.r0[j % RING]])

    def after_b(self, j, kind):
        g, i = self.g, j // self.g.kinds
        landing = self.rx2 if kind else self.rx
        cols = pl.ds(2 * self.y, 2) if kind else pl.ds(0, 4)
        self.add(self.G.at[j % self.slots, self.c, cols, self.b], [landing[i, k] for k in range(g.B - 1)])

    def after_a(self, j, kind):
        g, i = self.g, j // self.g.kinds
        landing = self.rz2 if kind else self.rz
        cols = pl.ds(2 * self.y, 2) if kind else pl.ds(0, 4)
        total = self.summed(
            self.G.at[j % self.slots, self.c, cols, self.b, self.a], [landing[i, k] for k in range(g.A - 1)]
        )
        if kind:
            self.rag[i, self.y] = total
        else:
            self.ryx[i, self.y] = total

    def after_blk(self, j, kind):
        g, i = self.g, j // self.g.kinds
        if kind:
            self.add(self.G.at[j % self.slots, self.c, pl.ds(2 * self.y, 2)], [self.ry[i]])
            return
        total = self.ryx[i, 0].astype(F32)
        for k in range(1, g.Y):
            total = total + self.ryx[i, k].astype(F32)
        self.emit(j, [total[col] for col in range(4)])

    def after_share(self, j, kind):
        i = j // 2
        self.emit(j, [self.rag[i, col // 2, col % 2].astype(F32) for col in range(4)])

    def plan(self, kind):
        core = (self.core, self.after_core)
        b = (self.along_b, self.after_b)
        a = (self.along_a, self.after_a)
        blk = (self.along_blk, self.after_blk)
        share = (self.share, self.after_share)
        return (core, blk, b, a, share) if kind else (core, b, a, blk)

    def start(self, j):
        self.core(j, 0)[0][0].start()

    def finish(self, stage, j):
        for kind in range(self.g.kinds):
            plan = self.plan(kind)
            if stage >= len(plan):
                continue

            def go(kind=kind, plan=plan):
                for copy in plan[stage][0](j, kind)[1]:
                    copy.wait()
                plan[stage][1](j, kind)
                if stage + 1 < len(plan):
                    for copy in plan[stage + 1][0](j, kind)[0]:
                        copy.start()

            if self.g.kinds == 1:
                go()
            elif isinstance(j, int):
                if (j + (j >= CHUNKS - 2)) % 2 == kind:
                    go()
            else:
                pl.when(jnp.where(j >= CHUNKS - 2, j + 1, j) % 2 == kind)(go)

    def advance(self, t):
        for stage in range(5):
            twice = t - AFTER[stage]
            if twice % 2 == 0 and 0 <= twice < 2 * CHUNKS:
                self.finish(stage, twice // 2)

    def advance_two(self, t, odd):
        for stage in range(5):
            if (odd - AFTER[stage]) % 2 == 0:
                j = t + (odd - AFTER[stage]) // 2

                @pl.when((j >= 0) & (j < CHUNKS))
                def _(stage=stage, j=j):
                    self.finish(stage, j)


def emit_to(g, j_ref, o_ref, e_ref, r_ref):
    R = g.R

    def emit(j, values):
        @pl.when(j < 6)
        def _():
            for col in range(4):
                e_ref[:, pl.ds(pl.multiple_of(j * 512 + col * 128, 128), 128)] = values[col]

        @pl.when((j >= 6) & (j < 12))
        def _():
            for k in range(4):
                r_ref[k * R : (k + 1) * R, pl.ds(pl.multiple_of((j - 6) * 128, 128), 128)] = values[k]

        @pl.when(j >= 12)
        def _():
            at = pl.multiple_of((j - 12) * 128, 128)
            for k in range(3):
                j_ref[:, pl.ds(pl.multiple_of(k * 768 + at, 128), 128)] = values[k]
            o_ref[:, pl.ds(at, 128)] = values[3]

    return emit


HEADS = 12
VECTORS = (
    "entry_gain", "entry_shift", "joint_bias", "output_bias",
    "middle_gain", "middle_shift", "expand_bias", "reduce_bias",
)
HD = 64
D = 768
FF = 3072
ROWS = 512
EDGE = 128
SPAN = 3 * EDGE
PAIRS = HEADS // 2
NEAR = 112
SLOTS = 12
STREAM = 2
TICK = 512
TICKS = FF // TICK


def nn(left, right):
    return jnp.dot(left, right, preferred_element_type=F32)


def nt(left, right):
    return lax.dot_general(left, right, (((1,), (1,)), ((), ())), preferred_element_type=F32)


def stats(values):
    average = jnp.mean(values, axis=-1, keepdims=True)
    centred = values - average
    spread = jnp.mean(centred * centred, axis=-1, keepdims=True)
    inverse = lax.rsqrt(spread + 1e-06)
    return centred * inverse, inverse


def normal_parts(hidden):
    half = hidden * (0.5**0.5)
    size = jnp.abs(half)
    ratio = 1.0 / (1.0 + 0.3275911 * size)
    bell = jnp.exp(-half * half)
    tail = ((((1.061405429 * ratio - 1.453152027) * ratio + 1.421413741) * ratio - 0.284496736) * ratio + 0.254829592) * ratio
    tail = 0.5 * tail * bell
    share = jnp.where(hidden >= 0, 1.0 - tail, tail)
    return share, hidden * bell * 0.3989422804014327


def column_sum(values):
    return jnp.sum(values, axis=0, keepdims=True)


def layer_kernel(g, names, *refs):
    r = dict(zip(names, refs))
    A, B, R, Y = g.A, g.B, g.R, g.Y
    (patches, cotangent, segments, w_joint, w_output, w_expand, w_reduce) = (
        r[n] for n in ("patches", "cotangent", "segments", "w_joint", "w_output", "w_expand", "w_reduce")
    )
    G, vec = r["G"], r["vec"]
    for name in VECTORS:
        r[name + "_row"][...] = r[name][...].reshape(1, -1)
        r[name] = r[name + "_row"]
    r["oe"], r["oo"] = r["vT"], r["n2"]
    out_rows, dx_rows = r["k"].at[pl.ds(0, ROWS)], r["ml"]
    x, xh, dy = r["x"], r["xh"], r["dy"]
    comm = Comm(g, G, SLOTS, r, emit_to(g, r["j_out"], r["o_out"], r["e_out"], r["r_out"]))
    y = comm.y
    has_left, has_right = y > 0, y < Y - 1

    def load(src, dst, k):
        return pltpu.make_async_copy(src, dst, r["load"].at[k])

    load_x = load(patches, x, 0)
    load_wj = load(w_joint, r["wj"], 1)
    load_wo = load(w_output, r["wo"], 2)
    load_dy = load(cotangent, dy, 3)

    def ffn_loads(i):
        s = i % STREAM
        at = pl.ds(pl.multiple_of(i * TICK, TICK), TICK)
        return (
            pltpu.make_async_copy(w_expand.at[:, at], r["we"].at[s], r["stream"].at[0, s]),
            pltpu.make_async_copy(w_reduce.at[at], r["wr"].at[s], r["stream"].at[1, s]),
        )

    load_x.start()
    load_wj.start()
    comm.barrier()

    def edge(k, side, src, dst, sems):
        other = comm.dev(y=(y + Y - 1) % Y) if side == 0 else comm.dev(y=(y + 1) % Y)
        return pltpu.make_async_remote_copy(
            src_ref=src, dst_ref=dst, send_sem=sems.at[(0,) + k + (side,)], recv_sem=sems.at[(1,) + k + (1 - side,)],
            device_id=other, device_id_type=MESH,
        )

    def x_edges():
        return (
            edge((), 0, patches.at[pl.ds(0, EDGE)], xh.at[1], r["s_edge"]),
            edge((), 1, patches.at[pl.ds(ROWS - EDGE, EDGE)], xh.at[0], r["s_edge"]),
        )

    to_left, to_right = x_edges()

    @pl.when(has_left)
    def _():
        to_left.start()

    @pl.when(has_right)
    def _():
        to_right.start()

    @pl.when(jnp.logical_not(has_left))
    def _():
        xh[0] = jnp.zeros((EDGE, D), BF)

    @pl.when(jnp.logical_not(has_right))
    def _():
        xh[1] = jnp.zeros((EDGE, D), BF)

    first_block = y * (ROWS // EDGE)
    count = segments.shape[0]
    columns = []
    for k in range(6):
        index = first_block + k - 1
        inside = (index >= 0) & (index < count)
        row = segments[pl.ds(jnp.clip(index, 0, count - 1), 1), :]
        row = jnp.where(inside, row, -1)
        columns.append(row)
    for b in range(4):
        for k in range(3):
            keys = jnp.broadcast_to(columns[b + k].astype(F32), (EDGE, EDGE)).T
            own = columns[b + 1].astype(F32)
            r["bias"][b, k * EDGE : (k + 1) * EDGE, :] = jnp.where(keys == own, 0.0, -1e30)

    vec[...] = jnp.zeros_like(vec)
    entry_gain, entry_shift = r["entry_gain"][...], r["entry_shift"][...]
    lanes = lax.broadcasted_iota(jnp.int32, (1, D), 1) % 128
    even = lanes < HD

    def project(rows, at, own, row_at):
        count = rows.shape[0]
        normal, _ = stats(rows.astype(F32))
        low = (normal * entry_gain + entry_shift).astype(BF)
        wj = r["wj"]
        key_rows = nn(low, wj[:, D : 2 * D]).astype(BF)
        r["k"][pl.ds(at, count), :] = key_rows
        value_rows = (nn(low, wj[:, 2 * D :]) + r["joint_bias"][:, D:]).astype(BF)
        r["v"][pl.ds(at, count), :] = value_rows
        r["vT"][:, pl.ds(at, count)] = value_rows.T
        if own:
            r["ml"][pl.ds(row_at, count), :] = low
            queries = (nn(low, wj[:, :D]) + r["joint_bias"][:, :D]).astype(BF) * BF(HD**-0.5)
            r["qe"][pl.ds(row_at, count), :] = jnp.where(even, queries, BF(0))
            r["qo"][pl.ds(row_at, count), :] = jnp.where(even, BF(0), queries)

    load_x.wait()
    load_wj.wait()
    load_wo.start()
    load_dy.start()
    for i in range(STREAM):
        for copy in ffn_loads(i):
            copy.start()

    def own_rows(i, _):
        at = pl.multiple_of(i * 256, 256)
        project(x[pl.ds(at, 256), :], pl.multiple_of(at + EDGE, EDGE), True, at)
        return 0

    lax.fori_loop(0, 2, own_rows, 0)

    @pl.when(has_left)
    def _():
        to_left.wait_send()
        to_right.wait_recv() if Y == 1 else edge((), 1, patches.at[pl.ds(0, EDGE)], xh.at[0], r["s_edge"]).wait_recv()

    @pl.when(has_right)
    def _():
        to_right.wait_send()
        edge((), 0, patches.at[pl.ds(0, EDGE)], xh.at[1], r["s_edge"]).wait_recv()

    def edge_rows(i, _):
        project(xh[i], pl.multiple_of(i * (ROWS + EDGE), EDGE), False, 0)
        return 0

    lax.fori_loop(0, 2, edge_rows, 0)

    top = lax.broadcasted_iota(jnp.int32, (EDGE, 1), 0) < HD

    def scores_of(p, b):
        at = pl.ds(pl.multiple_of(p * 128, 128), 128)
        keys, own = pl.ds(b * EDGE, SPAN), pl.ds(b * EDGE, EDGE)
        both = jnp.concatenate([r["qe"][own, at], r["qo"][own, at]], axis=0)
        return nt(r["k"][keys, at], both)

    def probs_of(b, scores):
        bias = r["bias"][b]
        scores = scores + jnp.concatenate([bias, bias], axis=1)
        powers = jnp.exp(scores - jnp.max(scores, axis=0, keepdims=True))
        return (powers * (1.0 / column_sum(powers))).astype(BF)

    def mix(p, b, probs):
        at = pl.ds(pl.multiple_of(p * 128, 128), 128)
        keys, own = pl.ds(b * EDGE, SPAN), pl.ds(b * EDGE, EDGE)
        r["probs"][p, b] = probs
        mixed = nn(r["vT"][at, keys], probs)
        r["attT"][at, own] = jnp.where(top, mixed[:, :128], mixed[:, 128:]).astype(BF)

    def attend(p, _):
        scores = scores_of(p, 0)
        before = None
        for b in range(4):
            following = scores_of(p, b + 1) if b < 3 else None
            probs = probs_of(b, scores)
            if b > 0:
                mix(p, b - 1, before)
            before, scores = probs, following
        mix(p, 3, before)
        return 0

    lax.fori_loop(0, PAIRS, attend, 0)

    load_wo.wait()
    mid, total, n2, n2T = r["mid"], r["total"], r["n2"], r["n2T"]
    middle_gain, middle_shift = r["middle_gain"][...], r["middle_shift"][...]

    def finish_attention(i, _):
        at = pl.ds(pl.multiple_of(i * 256, 256), 256)
        mixed = r["attT"][:, at].T
        middle = x[at, :].astype(F32) + nn(mixed, r["wo"][...]) + r["output_bias"][...]
        mid[at, :] = middle
        total[at, :] = middle + r["reduce_bias"][...]
        normal, _ = stats(middle)
        low = (normal * middle_gain + middle_shift).astype(BF)
        n2[at, :] = low
        n2T[:, at] = low.T
        r["dn"][at, :] = jnp.zeros((256, D), F32)
        return 0

    lax.fori_loop(0, 2, finish_attention, 0)
    load_dy.wait()

    def feed_forward(i, _):
        s = i % STREAM
        for copy in ffn_loads(i):
            copy.wait()
        we, wr = r["we"].at[s], r["wr"].at[s]
        at = pl.ds(pl.multiple_of(i * TICK, TICK), TICK)
        bias = r["expand_bias"][:, at]
        bias_sum = jnp.zeros((1, TICK), F32)
        rows = [pl.ds(half * 256, 256) for half in range(2)]
        hidden = [nn(n2[part, :], we[...]) + bias for part in rows]
        back = [nt(dy[part, :], wr[...]) for part in rows]
        for half, part in enumerate(rows):
            share, slope = normal_parts(hidden[half])
            active = (hidden[half] * share).astype(BF)
            hidden_gradient = back[half] * (share + slope)
            bias_sum = bias_sum + column_sum(hidden_gradient)
            low = hidden_gradient.astype(BF)
            r["hl"][part, :] = low
            r["actT"][at, part] = active.T
            total[part, :] += nn(active, wr[...])
            r["dn"][part, :] += nt(low, we[...])
            if half == 0:
                comm.advance_two(i, -1)
        r["eb"][:, at] = bias_sum
        for part in range(2):
            block = nn(n2T[part * 384 : (part + 1) * 384, :], r["hl"][...]).astype(BF)
            store_rows(block, i, part * 2, 2)
        comm.start(i)

        @pl.when(i + STREAM < TICKS)
        def _():
            for copy in ffn_loads(i + STREAM):
                copy.start()

        comm.advance_two(i, 0)
        return 0

    def store_rows(block, chunk, a0, na):
        slot = chunk % SLOTS
        for a in range(na):
            for b in range(B):
                for c in range(2):
                    row = ((a * B + b) * 2 + c) * R
                    for col in range(block.shape[1] // 128):
                        G[slot, c, col, b, a0 + a] = block[row : row + R, col * 128 : (col + 1) * 128]

    lax.fori_loop(0, TICKS, feed_forward, 0)

    def turn(i, _):
        at = pl.ds(pl.multiple_of(i * 256, 256), 256)
        r["kT"][:, at] = r["k"][at, :].T

        @pl.when(i < 2)
        def _():
            r["n1T"][:, at] = r["ml"][at, :].T

        return 0

    lax.fori_loop(0, 3, turn, 0)

    def reduce_gradient(p, _):
        at = pl.ds(pl.multiple_of(p * 256, 256), 256)
        chunk = 6 + 2 * p

        def part(a, _):
            block = nn(r["actT"][pl.ds(pl.multiple_of(a * D, D), D), :], dy[:, at]).astype(BF)
            for h in range(2):
                slot = (chunk + h) % SLOTS
                for b in range(B):
                    for c in range(2):
                        for k in range(4):
                            row = ((b * 2 + c) * 4 + k) * R
                            G[slot, c, k, b, a] = block[row : row + R, h * 128 : (h + 1) * 128]
            return 0

        lax.fori_loop(0, A, part, 0)
        comm.start(chunk)
        comm.start(chunk + 1)
        comm.advance_two(6 + p, -1)
        comm.advance_two(6 + p, 0)
        return 0

    lax.fori_loop(0, 3, reduce_gradient, 0)

    def middle_back(i, _):
        at = pl.ds(pl.multiple_of(i * 256, 256), 256)
        out_rows[at, :] = total[at, :].astype(BF)
        error = r["dn"][at, :]
        normal, inverse = stats(mid[at, :])
        scaled = error * middle_gain
        part = inverse * (
            scaled
            - jnp.mean(scaled, axis=-1, keepdims=True)
            - normal * jnp.mean(scaled * normal, axis=-1, keepdims=True)
        )
        incoming = dy[at, :].astype(F32)
        gradient = incoming + part
        vec[5:6, :] += column_sum(error * normal)
        vec[6:7, :] += column_sum(error)
        vec[4:5, :] += column_sum(gradient)
        vec[11:12, :] += column_sum(incoming)
        mid[at, :] = gradient
        low = gradient.astype(BF)
        r["ml"][at, :] = low
        back = nt(low, r["wo"][...]).astype(BF)
        r["oe"][at, :] = jnp.where(even, back, BF(0))
        r["oo"][at, :] = jnp.where(even, BF(0), back)
        total[at, :] = jnp.zeros((256, D), F32)
        return 0

    lax.fori_loop(0, 2, middle_back, 0)
    save_out = pltpu.make_async_copy(out_rows, r["out"], r["save"].at[0])
    save_out.start()
    for k in range(4):
        vec[7 + k : 8 + k, :] = r["eb"][:, k * D : (k + 1) * D]
    comm.advance(17)
    comm.advance(18)

    parts, jq, sent, got, s_part = r["parts"], r["jq"], r["sent"], r["got"], r["s_part"]

    def part_copies(p):
        return (
            edge((p,), 0, sent.at[p % 2, 0], got.at[p, 1], s_part),
            edge((p,), 1, sent.at[p % 2, 1], got.at[p, 0], s_part),
        )

    def attend_back(p):
        at = pl.ds(pl.multiple_of(p * 128, 128), 128)
        slot = p % 2
        own_sum = jnp.zeros((1, 128), F32)
        parts[slot] = jnp.zeros((ROWS + 2 * EDGE, 256), F32)

        def errors_of(b):
            own = pl.ds(b * EDGE, EDGE)
            return jnp.concatenate([r["oe"][own, at], r["oo"][own, at]], axis=0)

        def shares_of(b):
            return nt(r["v"][pl.ds(b * EDGE, SPAN), at], errors_of(b))

        def score_gradient_of(b, shares):
            wide = r["probs"][p, b].astype(F32)
            product = wide * shares
            return (product - wide * column_sum(product)).astype(BF)

        def spread(b, low):
            keys, own = pl.ds(b * EDGE, SPAN), pl.ds(b * EDGE, EDGE)
            queries = jnp.concatenate([r["qe"][own, at], r["qo"][own, at]], axis=0)
            parts[slot, keys, 0:128] += nn(low, queries)
            parts[slot, keys, 128:256] += nn(r["probs"][p, b], errors_of(b))
            turned = nn(r["kT"][at, keys], low)
            mine = (jnp.where(top, turned[:, :128], turned[:, 128:]) * HD**-0.5).T
            jq[slot, own, :] = mine.astype(BF)
            return column_sum(mine)

        shares = shares_of(0)
        before = None
        for b in range(4):
            following = shares_of(b + 1) if b < 3 else None
            low = score_gradient_of(b, shares)
            if b > 0:
                own_sum = own_sum + spread(b - 1, before)
            before, shares = low, following
        own_sum = own_sum + spread(3, before)
        vec[2:3, at] = own_sum
        to_left, to_right = part_copies(p)

        @pl.when(has_left)
        def _():
            sent[slot, 0] = parts[slot, EDGE - NEAR : EDGE, :].astype(BF)
            to_left.start()

        @pl.when(has_right)
        def _():
            sent[slot, 1] = parts[slot, ROWS + EDGE : ROWS + EDGE + NEAR, :].astype(BF)
            to_right.start()

    def joint_gradient(p):
        at = pl.ds(pl.multiple_of(p * 128, 128), 128)
        slot = p % 2
        to_left, to_right = part_copies(p)

        @pl.when(has_left)
        def _():
            to_left.wait_send()
            to_right.wait_recv()
            parts[slot, EDGE : EDGE + NEAR, :] += got[p, 0].astype(F32)

        @pl.when(has_right)
        def _():
            to_right.wait_send()
            to_left.wait_recv()
            parts[slot, ROWS + EDGE - NEAR : ROWS + EDGE, :] += got[p, 1].astype(F32)

        sums = parts[slot, EDGE : ROWS + EDGE, :]
        vec[3:4, at] = column_sum(sums[:, 128:])
        low = jnp.concatenate([jq[slot], sums.astype(BF)], axis=1)
        wj = r["wj"]
        weights = jnp.concatenate([wj[:, pl.ds(pl.multiple_of(k * D + p * 128, 128), 128)] for k in range(3)], axis=1)
        total[...] += nt(low, weights)
        low_out = r["ml"][:, at]
        for part in range(2):
            rows = pl.ds(part * 384, 384)
            block = nn(r["n1T"][rows, :], low).astype(BF)
            block_out = nn(r["attT"][rows, :], low_out).astype(BF)
            store_rows(jnp.concatenate([block, block_out], axis=1), 12 + p, part * 2, 2)
        comm.start(12 + p)

    def pair_step(i, _):
        @pl.when(i < PAIRS)
        def _():
            attend_back(i)

        @pl.when(i > 0)
        def _():
            joint_gradient(i - 1)

        comm.advance_two(10 + i, 0)
        return 0

    lax.fori_loop(0, PAIRS + 1, pair_step, 0)

    def entry_back(i, _):
        at = pl.ds(pl.multiple_of(i * 256, 256), 256)
        error = total[at, :]
        normal, inverse = stats(x[at, :].astype(F32))
        scaled = error * entry_gain
        part = inverse * (
            scaled
            - jnp.mean(scaled, axis=-1, keepdims=True)
            - normal * jnp.mean(scaled * normal, axis=-1, keepdims=True)
        )
        vec[0:1, :] += column_sum(error * normal)
        vec[1:2, :] += column_sum(error)
        dx_rows[at, :] = (mid[at, :] + part).astype(BF)
        return 0

    lax.fori_loop(0, 2, entry_back, 0)
    save_dx = pltpu.make_async_copy(dx_rows, r["dx"], r["save"].at[1])
    save_dx.start()

    rv, s_vec = r["rv"], r["s_vec"]

    def vector_copies(step):
        groups = (
            [comm.dev(c=1 - comm.c)],
            [comm.dev(b=(comm.b + k) % B) for k in range(1, B)],
            [comm.dev(a=(comm.a + k) % A) for k in range(1, A)],
            [comm.dev(y=(comm.y + k) % Y) for k in range(1, Y)],
        )
        ids = (comm.c, comm.b, comm.a, comm.y)
        base = (0, 2, 0, A)[step]
        held = rv if step < 2 else r["rvl"]
        here = held.at[base + ids[step]]
        return here, [
            comm.copy(here, here, s_vec, ((0, 2, 2 + B, 2 + B + A)[step] + k,), other) for k, other in enumerate(groups[step])
        ]

    def vector_sum(step):
        base, size = ((0, 2), (2, B), (0, A), (A, Y))[step]
        held = rv if step < 2 else r["rvl"]
        value = held[base].astype(F32)
        for k in range(1, size):
            value = value + held[base + k].astype(F32)
        return value

    def vector_start(step, value):
        here, copies = vector_copies(step)
        here[...] = value.astype(here.dtype)
        for copy in copies:
            copy.start()

    def vector_wait(step):
        for copy in vector_copies(step)[1]:
            copy.wait()

    vector_start(0, vec[...])
    for step in range(4):
        comm.advance(33 + 2 * step)
        comm.advance(34 + 2 * step)
        vector_wait(step)
        if step < 3:
            vector_start(step + 1, vector_sum(step))
    summed = vector_sum(3)
    place = lax.axis_index("dp")
    spot = lax.broadcasted_iota(jnp.int32, (D, 512), 0)
    lane = lax.broadcasted_iota(jnp.int32, (D, 512), 1)
    n2v, n4v = g.dp // 2, g.dp // 4
    want = jnp.where(
        lane < 128,
        lane + place * R,
        jnp.where(lane < 256, lane - 128 + (place % n2v) * (2 * R), lane - 256 + (place % n4v) * (4 * R)),
    )
    pick = jnp.where(spot == want, 1.0, 0.0).astype(F32)
    picked = jnp.dot(summed, pick, precision=lax.Precision.HIGHEST, preferred_element_type=F32)
    kind = lax.broadcasted_iota(jnp.int32, (16, 1), 0)
    r["v_out"][...] = picked[:, 0:128]
    r["jb_out"][...] = column_sum(jnp.where(kind == 2 + place // n2v, picked[:, 128:256], 0.0))
    r["eb_out"][...] = column_sum(jnp.where(kind == 7 + place // n4v, picked[:, 256:512], 0.0))
    for t in range(41, 2 * CHUNKS + AFTER[4]):
        comm.advance(t)
    save_out.wait()
    save_dx.wait()


def layer(g, patches, segments, vectors, weights, cotangent):
    A, B, R, Y = g.A, g.B, g.R, g.Y
    comm_shapes = comm_scratch(g)
    V = pl.BlockSpec(memory_space=pltpu.VMEM)
    H = pl.BlockSpec(memory_space=pl.ANY)
    inputs = dict(
        patches=(patches, H),
        cotangent=(cotangent, H),
        segments=(segments, V),
        w_joint=(weights[0], H),
        w_output=(weights[1], H),
        w_expand=(weights[2], H),
        w_reduce=(weights[3], H),
        **{name: (value, V) for name, value in vectors.items()},
    )
    outputs = dict(
        out=((ROWS, D), BF),
        dx=((ROWS, D), BF),
        j_out=((R, 3 * D), F32),
        o_out=((R, D), F32),
        e_out=((R, FF), F32),
        r_out=((4 * R, D), F32),
        v_out=((16, 128), F32),
        jb_out=((1, 128), F32),
        eb_out=((1, 256), F32),
    )
    ext = ROWS + 2 * EDGE
    scratch = dict(
        x=pltpu.VMEM((ROWS, D), BF),
        xh=pltpu.VMEM((2, EDGE, D), BF),
        dy=pltpu.VMEM((ROWS, D), BF),
        wj=pltpu.VMEM((D, 3 * D), BF),
        wo=pltpu.VMEM((D, D), BF),
        we=pltpu.VMEM((STREAM, D, TICK), BF),
        wr=pltpu.VMEM((STREAM, TICK, D), BF),
        n1T=pltpu.VMEM((D, ROWS), BF),
        qe=pltpu.VMEM((ROWS, D), BF),
        qo=pltpu.VMEM((ROWS, D), BF),
        k=pltpu.VMEM((ext, D), BF),
        v=pltpu.VMEM((ext, D), BF),
        kT=pltpu.VMEM((D, ext), BF),
        vT=pltpu.VMEM((D, ext), BF),
        bias=pltpu.VMEM((4, SPAN, EDGE), F32),
        probs=pltpu.VMEM((PAIRS, 4, SPAN, 2 * EDGE), BF),
        attT=pltpu.VMEM((D, ROWS), BF),
        mid=pltpu.VMEM((ROWS, D), F32),
        total=pltpu.VMEM((ROWS, D), F32),
        dn=pltpu.VMEM((ROWS, D), F32),
        n2=pltpu.VMEM((ROWS, D), BF),
        n2T=pltpu.VMEM((D, ROWS), BF),
        hl=pltpu.VMEM((ROWS, TICK), BF),
        actT=pltpu.VMEM((FF, ROWS), BF),
        eb=pltpu.VMEM((1, FF), F32),
        ml=pltpu.VMEM((ROWS, D), BF),
        parts=pltpu.VMEM((2, ext, 256), F32),
        jq=pltpu.VMEM((2, ROWS, 128), BF),
        sent=pltpu.VMEM((2, 2, NEAR, 256), BF),
        got=pltpu.VMEM((PAIRS, 2, NEAR, 256), BF),
        vec=pltpu.VMEM((16, D), F32),
        rv=pltpu.VMEM((2 + B, 16, D), F32),
        rvl=pltpu.VMEM((A + Y, 16, D), BF),
        G=pltpu.VMEM((SLOTS, 2, 4, B, A, R, 128), BF),
        load=pltpu.SemaphoreType.DMA((4,)),
        save=pltpu.SemaphoreType.DMA((2,)),
        stream=pltpu.SemaphoreType.DMA((2, STREAM)),
        s_edge=pltpu.SemaphoreType.DMA((2, 2)),
        s_part=pltpu.SemaphoreType.DMA((2, PAIRS, 2)),
        s_vec=pltpu.SemaphoreType.DMA((2, 2 + B + A + Y)),
        **{name + "_row": pltpu.VMEM((1, value.shape[0]), F32) for name, value in vectors.items()},
        **comm_shapes,
    )
    names = (*inputs, *outputs, *scratch)
    results = pl.pallas_call(
        functools.partial(layer_kernel, g, names),
        out_shape=tuple(jax.ShapeDtypeStruct(*shape) for shape in outputs.values()),
        in_specs=[spec for _, spec in inputs.values()],
        out_specs=[H, H] + [V] * (len(outputs) - 2),
        scratch_shapes=list(scratch.values()),
        compiler_params=pltpu.CompilerParams(
            collective_id=0, has_side_effects=True, vmem_limit_bytes=64 << 20
        ),
    )(*(value for value, _ in inputs.values()))
    return hand_over(g, dict(zip(outputs, results)))


def hand_over_kernel(g, out, dx, j, o, e, w, v, jb, eb, *refs):
    outs, held, sems = refs[:14], refs[14:20], refs[20]
    R = g.R
    moves = [(out, 0), (dx, 1), (j, 4), (o, 6), (e, 10), (w, 12)]
    loads = [pltpu.make_async_copy(src, held[i], sems.at[0, i]) for i, (src, _) in enumerate(moves)]
    copies = [pltpu.make_async_copy(held[i], outs[k], sems.at[1, i]) for i, (_, k) in enumerate(moves)]
    for load in loads:
        load.start()
    for load, copy in zip(loads, copies):
        load.wait()
        copy.start()
    for row, k in ((0, 2), (1, 3), (4, 7), (5, 8), (6, 9), (11, 13)):
        outs[k][...] = v[row, :R]
    outs[5][...] = jb[0, : 2 * R]
    outs[11][...] = eb[0, : 4 * R]
    for copy in copies:
        copy.wait()


def hand_over(g, o):
    R = g.R
    V = pl.BlockSpec(memory_space=pltpu.VMEM)
    H = pl.BlockSpec(memory_space=pl.ANY)
    shapes = [
        ((ROWS, D), BF), ((ROWS, D), BF), ((R,), F32), ((R,), F32), ((R, 3 * D), F32), ((2 * R,), F32), ((R, D), F32),
        ((R,), F32), ((R,), F32), ((R,), F32), ((R, FF), F32), ((4 * R,), F32), ((4 * R, D), F32), ((R,), F32),
    ]
    names = ("out", "dx", "j_out", "o_out", "e_out", "r_out", "v_out", "jb_out", "eb_out")
    return pl.pallas_call(
        functools.partial(hand_over_kernel, g),
        out_shape=tuple(jax.ShapeDtypeStruct(*shape) for shape in shapes),
        in_specs=[H] * 6 + [V] * 3,
        out_specs=[V if len(shape) == 1 else H for shape, _ in shapes],
        scratch_shapes=[
            *(pltpu.VMEM(o[name].shape, o[name].dtype) for name in names[:6]),
            pltpu.SemaphoreType.DMA((2, 6)),
        ],
    )(*(o[name] for name in names))


def local(
    patches,
    segments,
    entry_gain,
    entry_shift,
    joint_weight,
    joint_bias,
    output_weight,
    output_bias,
    middle_gain,
    middle_shift,
    expand_weight,
    expand_bias,
    reduce_weight,
    reduce_bias,
    cotangent,
):
    g = Grid(lax.axis_size("dp"), lax.axis_size("blk"), D)
    R = g.R
    vectors = dict(
        entry_gain=entry_gain,
        entry_shift=entry_shift,
        joint_bias=joint_bias,
        output_bias=output_bias,
        middle_gain=middle_gain,
        middle_shift=middle_shift,
        expand_bias=expand_bias,
        reduce_bias=reduce_bias,
    )
    o = layer(
        g,
        patches[0],
        segments.reshape(-1, EDGE),
        vectors,
        (joint_weight, output_weight, expand_weight, reduce_weight),
        cotangent[0],
    )
    return (o[0][None], o[1][None], *o[2:])


def solution(mesh):
    return jax.shard_map(
        local,
        mesh=mesh,
        in_specs=(
            P("dp", "blk", None),
            P("dp", None),
            P(),
            P(),
            P(),
            P(),
            P(),
            P(),
            P(),
            P(),
            P(),
            P(),
            P(),
            P(),
            P("dp", "blk", None),
        ),
        out_specs=(
            P("dp", "blk", None),
            P("dp", "blk", None),
            P("dp"),
            P("dp"),
            P("dp", None),
            P("dp"),
            P("dp", None),
            P("dp"),
            P("dp"),
            P("dp"),
            P("dp", None),
            P("dp"),
            P("dp", None),
            P("dp"),
        ),
        check_vma=False,
    )
```

```python
import functools
import jax
import jax.numpy as jnp
from jax import lax
from jax.experimental import pallas as pl
from jax.experimental.pallas import tpu as pltpu
from jax.sharding import PartitionSpec as P

MESH = pl.DeviceIdType.MESH
CHUNKS = 18
AFTER = (2, 6, 10, 14, 18)
RING = 9
VECTOR_STEPS = (36, 40, 44, 48)
BF = jnp.bfloat16
F32 = jnp.float32


class Grid:
    def __init__(self, dp, blk, width):
        self.A = 4
        self.B = dp // 8
        self.Y = blk
        self.dp = dp
        self.R = width // dp
        self.kinds = 2 if blk == 2 else 1


def comm_scratch(g):
    A, B, Y, R = g.A, g.B, g.Y, g.R
    n = CHUNKS // g.kinds
    shapes = dict(
        r0=pltpu.VMEM((RING, 4, B, A, R, 128), BF),
        rx=pltpu.VMEM((n, B - 1, 4, A, R, 128), BF),
        rz=pltpu.VMEM((n, A - 1, 4, R, 128), BF),
        ryx=pltpu.VMEM((n, Y, 4, R, 128), BF),
        s_core=pltpu.SemaphoreType.DMA((2, CHUNKS)),
        s_x=pltpu.SemaphoreType.DMA((2, CHUNKS, B - 1)),
        s_z=pltpu.SemaphoreType.DMA((2, CHUNKS)),
        s_y=pltpu.SemaphoreType.DMA((2, CHUNKS, Y - 1)),
    )
    if g.kinds == 2:
        shapes.update(
            ry=pltpu.VMEM((n, 2, B, A, R, 128), BF),
            rx2=pltpu.VMEM((n, B - 1, 2, A, R, 128), BF),
            rz2=pltpu.VMEM((n, A - 1, 2, R, 128), BF),
            rag=pltpu.VMEM((n, 2, 2, R, 128), BF),
            s_ag=pltpu.SemaphoreType.DMA((2, CHUNKS)),
        )
    return shapes


class Comm:
    def __init__(self, g, G, slots, refs, emit):
        self.g, self.G, self.slots, self.emit = g, G, slots, emit
        self.__dict__.update(refs)
        dp = lax.axis_index("dp")
        self.y = lax.axis_index("blk")
        self.c = dp % 2
        self.b = (dp // 2) % g.B
        self.a = dp // (2 * g.B)

    def dev(self, a=None, b=None, c=None, y=None):
        a = self.a if a is None else a
        b = self.b if b is None else b
        c = self.c if c is None else c
        y = self.y if y is None else y
        return ((a * self.g.B + b) * 2 + c, y)

    def partners(self):
        g = self.g
        return (
            [self.dev(c=1 - self.c)]
            + [self.dev(b=(self.b + k) % g.B) for k in range(1, g.B)]
            + [self.dev(a=(self.a + k) % g.A) for k in range(1, g.A)]
            + [self.dev(y=(self.y + k) % g.Y) for k in range(1, g.Y)]
        )

    def barrier(self):
        sem = pltpu.get_barrier_semaphore()
        others = self.partners()
        for other in others:
            pl.semaphore_signal(sem, inc=1, device_id=other, device_id_type=MESH)
        pl.semaphore_wait(sem, len(others))

    def copy(self, src, dst, sems, index, device):
        return pltpu.make_async_remote_copy(
            src_ref=src,
            dst_ref=dst,
            send_sem=sems.at[(0,) + index],
            recv_sem=sems.at[(1,) + index],
            device_id=device,
            device_id_type=MESH,
        )

    def core(self, j, kind):
        copy = self.copy(
            self.G.at[j % self.slots, 1 - self.c], self.r0.at[j % RING], self.s_core, (j,), self.dev(c=1 - self.c)
        )
        return [copy], [copy]

    def along_b(self, j, kind):
        g, i = self.g, j // self.g.kinds
        landing = self.rx2 if kind else self.rx
        cols = pl.ds(2 * self.y, 2) if kind else pl.ds(0, 4)
        copies = []
        for k in range(1, g.B):
            other = (self.b + k) % g.B
            source = self.G.at[j % self.slots, self.c, cols, other]
            copies.append(self.copy(source, landing.at[i, k - 1], self.s_x, (j, k - 1), self.dev(b=other)))
        return copies, copies

    def along_a(self, j, kind):
        g, i = self.g, j // self.g.kinds
        landing = self.rz2 if kind else self.rz
        cols = pl.ds(2 * self.y, 2) if kind else pl.ds(0, 4)
        copies = []
        for k in range(1, g.A):
            other = (self.a + k) % g.A
            source = self.G.at[j % self.slots, self.c, cols, self.b, other]
            copies.append(self.copy(source, landing.at[i, k - 1], self.s_z, (j,), self.dev(a=other)))
        return copies, [self.copy(landing.at[i], landing.at[i], self.s_z, (j,), self.dev(a=(self.a + 1) % g.A))]

    def along_blk(self, j, kind):
        g, i = self.g, j // self.g.kinds
        if kind:
            source = self.G.at[j % self.slots, self.c, pl.ds(2 * (1 - self.y), 2)]
            copies = [self.copy(source, self.ry.at[i], self.s_y, (j, 0), self.dev(y=1 - self.y))]
            return copies, copies
        mine = self.ryx.at[i, self.y]
        copies = [
            self.copy(mine, mine, self.s_y, (j, k - 1), self.dev(y=(self.y + k) % g.Y)) for k in range(1, g.Y)
        ]
        return copies, copies

    def share(self, j, kind):
        mine = self.rag.at[j // 2, self.y]
        copies = [self.copy(mine, mine, self.s_ag, (j,), self.dev(y=1 - self.y))]
        return copies, copies

    def add(self, mine, parts):
        if len(parts) == 1:
            mine[...] = mine[...] + parts[0]
        else:
            mine[...] = self.summed(mine, parts)

    def summed(self, mine, parts):
        total = mine[...].astype(F32)
        for part in parts:
            total = total + part.astype(F32)
        return total.astype(BF)

    def after_core(self, j, kind):
        self.add(self.G.at[j % self.slots, self.c], [self.r0[j % RING]])

    def after_b(self, j, kind):
        g, i = self.g, j // self.g.kinds
        landing = self.rx2 if kind else self.rx
        cols = pl.ds(2 * self.y, 2) if kind else pl.ds(0, 4)
        self.add(self.G.at[j % self.slots, self.c, cols, self.b], [landing[i, k] for k in range(g.B - 1)])

    def after_a(self, j, kind):
        g, i = self.g, j // self.g.kinds
        landing = self.rz2 if kind else self.rz
        cols = pl.ds(2 * self.y, 2) if kind else pl.ds(0, 4)
        total = self.summed(
            self.G.at[j % self.slots, self.c, cols, self.b, self.a], [landing[i, k] for k in range(g.A - 1)]
        )
        if kind:
            self.rag[i, self.y] = total
        else:
            self.ryx[i, self.y] = total

    def after_blk(self, j, kind):
        g, i = self.g, j // self.g.kinds
        if kind:
            self.add(self.G.at[j % self.slots, self.c, pl.ds(2 * self.y, 2)], [self.ry[i]])
            return
        total = self.ryx[i, 0].astype(F32)
        for k in range(1, g.Y):
            total = total + self.ryx[i, k].astype(F32)
        self.emit(j, [total[col] for col in range(4)])

    def after_share(self, j, kind):
        i = j // 2
        self.emit(j, [self.rag[i, col // 2, col % 2].astype(F32) for col in range(4)])

    def plan(self, kind):
        core = (self.core, self.after_core)
        b = (self.along_b, self.after_b)
        a = (self.along_a, self.after_a)
        blk = (self.along_blk, self.after_blk)
        share = (self.share, self.after_share)
        return (core, blk, b, a, share) if kind else (core, b, a, blk)

    def start(self, j):
        self.core(j, 0)[0][0].start()

    def finish(self, stage, j):
        for kind in range(self.g.kinds):
            plan = self.plan(kind)
            if stage >= len(plan):
                continue

            def go(kind=kind, plan=plan):
                for copy in plan[stage][0](j, kind)[1]:
                    copy.wait()
                plan[stage][1](j, kind)
                if stage + 1 < len(plan):
                    for copy in plan[stage + 1][0](j, kind)[0]:
                        copy.start()

            if self.g.kinds == 1:
                go()
            elif isinstance(j, int):
                if (j + (j >= CHUNKS - 2)) % 2 == kind:
                    go()
            else:
                pl.when(jnp.where(j >= CHUNKS - 2, j + 1, j) % 2 == kind)(go)

    def advance(self, t):
        for stage in range(5):
            twice = t - AFTER[stage]
            if twice % 2 == 0 and 0 <= twice < 2 * CHUNKS:
                self.finish(stage, twice // 2)

    def advance_two(self, t, odd):
        for stage in range(5):
            if (odd - AFTER[stage]) % 2 == 0:
                j = t + (odd - AFTER[stage]) // 2

                @pl.when((j >= 0) & (j < CHUNKS))
                def _(stage=stage, j=j):
                    self.finish(stage, j)


def emit_to(g, j_ref, o_ref, e_ref, r_ref):
    R = g.R

    def emit(j, values):
        @pl.when(j < 6)
        def _():
            for col in range(4):
                e_ref[:, pl.ds(pl.multiple_of(j * 512 + col * 128, 128), 128)] = values[col]

        @pl.when((j >= 6) & (j < 12))
        def _():
            for k in range(4):
                r_ref[k * R : (k + 1) * R, pl.ds(pl.multiple_of((j - 6) * 128, 128), 128)] = values[k]

        @pl.when(j >= 12)
        def _():
            at = pl.multiple_of((j - 12) * 128, 128)
            for k in range(3):
                j_ref[:, pl.ds(pl.multiple_of(k * 768 + at, 128), 128)] = values[k]
            o_ref[:, pl.ds(at, 128)] = values[3]

    return emit


HEADS = 12
VECTORS = (
    "entry_gain", "entry_shift", "joint_bias", "output_bias",
    "middle_gain", "middle_shift", "expand_bias", "reduce_bias",
)
HD = 64
D = 768
FF = 3072
ROWS = 512
EDGE = 128
SPAN = 3 * EDGE
PAIRS = HEADS // 2
NEAR = 112
SLOTS = 12
STREAM = 2
TICK = 512
TICKS = FF // TICK


def nn(left, right):
    return jnp.dot(left, right, preferred_element_type=F32)


def nt(left, right):
    return lax.dot_general(left, right, (((1,), (1,)), ((), ())), preferred_element_type=F32)


def stats(values):
    average = jnp.mean(values, axis=-1, keepdims=True)
    centred = values - average
    spread = jnp.mean(centred * centred, axis=-1, keepdims=True)
    inverse = lax.rsqrt(spread + 1e-06)
    return centred * inverse, inverse


def normal_parts(hidden):
    half = hidden * (0.5**0.5)
    size = jnp.abs(half)
    ratio = 1.0 / (1.0 + 0.3275911 * size)
    bell = jnp.exp(-half * half)
    tail = ((((1.061405429 * ratio - 1.453152027) * ratio + 1.421413741) * ratio - 0.284496736) * ratio + 0.254829592) * ratio
    tail = 0.5 * tail * bell
    share = jnp.where(hidden >= 0, 1.0 - tail, tail)
    return share, hidden * bell * 0.3989422804014327


def column_sum(values):
    return jnp.sum(values, axis=0, keepdims=True)


def layer_kernel(g, names, *refs):
    r = dict(zip(names, refs))
    A, B, R, Y = g.A, g.B, g.R, g.Y
    (patches, cotangent, segments, w_joint, w_output, w_expand, w_reduce) = (
        r[n] for n in ("patches", "cotangent", "segments", "w_joint", "w_output", "w_expand", "w_reduce")
    )
    G, vec = r["G"], r["vec"]
    for name in VECTORS:
        r[name + "_row"][...] = r[name][...].reshape(1, -1)
        r[name] = r[name + "_row"]
    r["oe"], r["oo"] = r["vT"], r["n2"]
    out_rows, dx_rows = r["k"].at[pl.ds(0, ROWS)], r["ml"]
    x, xh, dy = r["x"], r["xh"], r["dy"]
    comm = Comm(g, G, SLOTS, r, emit_to(g, r["j_out"], r["o_out"], r["e_sum"], r["r_sum"]))
    y = comm.y
    has_left, has_right = y > 0, y < Y - 1

    def load(src, dst, k):
        return pltpu.make_async_copy(src, dst, r["load"].at[k])

    load_x = load(patches, x, 0)
    load_wj = load(w_joint, r["wj"], 1)
    load_wo = load(w_output, r["wo"], 2)
    load_dy = load(cotangent, dy, 3)

    def ffn_loads(i):
        s = i % STREAM
        at = pl.ds(pl.multiple_of(i * TICK, TICK), TICK)
        return (
            pltpu.make_async_copy(w_expand.at[:, at], r["we"].at[s], r["stream"].at[0, s]),
            pltpu.make_async_copy(w_reduce.at[at], r["wr"].at[s], r["stream"].at[1, s]),
        )

    load_x.start()
    load_wj.start()
    comm.barrier()

    def edge(k, side, src, dst, sems):
        other = comm.dev(y=(y + Y - 1) % Y) if side == 0 else comm.dev(y=(y + 1) % Y)
        return pltpu.make_async_remote_copy(
            src_ref=src, dst_ref=dst, send_sem=sems.at[(0,) + k + (side,)], recv_sem=sems.at[(1,) + k + (1 - side,)],
            device_id=other, device_id_type=MESH,
        )

    def x_edges():
        return (
            edge((), 0, patches.at[pl.ds(0, EDGE)], xh.at[1], r["s_edge"]),
            edge((), 1, patches.at[pl.ds(ROWS - EDGE, EDGE)], xh.at[0], r["s_edge"]),
        )

    to_left, to_right = x_edges()

    @pl.when(has_left)
    def _():
        to_left.start()

    @pl.when(has_right)
    def _():
        to_right.start()

    @pl.when(jnp.logical_not(has_left))
    def _():
        xh[0] = jnp.zeros((EDGE, D), BF)

    @pl.when(jnp.logical_not(has_right))
    def _():
        xh[1] = jnp.zeros((EDGE, D), BF)

    first_block = y * (ROWS // EDGE)
    count = segments.shape[0]
    columns = []
    for k in range(6):
        index = first_block + k - 1
        inside = (index >= 0) & (index < count)
        row = segments[pl.ds(jnp.clip(index, 0, count - 1), 1), :]
        row = jnp.where(inside, row, -1)
        columns.append(row)
    for b in range(4):
        for k in range(3):
            keys = jnp.broadcast_to(columns[b + k].astype(F32), (EDGE, EDGE)).T
            own = columns[b + 1].astype(F32)
            r["bias"][b, k * EDGE : (k + 1) * EDGE, :] = jnp.where(keys == own, 0.0, -1e30)

    vec[...] = jnp.zeros_like(vec)
    entry_gain, entry_shift = r["entry_gain"][...], r["entry_shift"][...]
    lanes = lax.broadcasted_iota(jnp.int32, (1, D), 1) % 128
    even = lanes < HD

    def project(rows, at, own, row_at):
        count = rows.shape[0]
        normal, _ = stats(rows.astype(F32))
        low = (normal * entry_gain + entry_shift).astype(BF)
        wj = r["wj"]
        key_rows = nn(low, wj[:, D : 2 * D]).astype(BF)
        r["k"][pl.ds(at, count), :] = key_rows
        value_rows = (nn(low, wj[:, 2 * D :]) + r["joint_bias"][:, D:]).astype(BF)
        r["v"][pl.ds(at, count), :] = value_rows
        r["vT"][:, pl.ds(at, count)] = value_rows.T
        if own:
            r["ml"][pl.ds(row_at, count), :] = low
            queries = (nn(low, wj[:, :D]) + r["joint_bias"][:, :D]).astype(BF) * BF(HD**-0.5)
            r["qe"][pl.ds(row_at, count), :] = jnp.where(even, queries, BF(0))
            r["qo"][pl.ds(row_at, count), :] = jnp.where(even, BF(0), queries)

    load_x.wait()
    load_wj.wait()
    load_wo.start()
    load_dy.start()
    for i in range(STREAM):
        for copy in ffn_loads(i):
            copy.start()

    def own_rows(i, _):
        at = pl.multiple_of(i * 256, 256)
        project(x[pl.ds(at, 256), :], pl.multiple_of(at + EDGE, EDGE), True, at)
        return 0

    lax.fori_loop(0, 2, own_rows, 0)

    @pl.when(has_left)
    def _():
        to_left.wait_send()
        to_right.wait_recv() if Y == 1 else edge((), 1, patches.at[pl.ds(0, EDGE)], xh.at[0], r["s_edge"]).wait_recv()

    @pl.when(has_right)
    def _():
        to_right.wait_send()
        edge((), 0, patches.at[pl.ds(0, EDGE)], xh.at[1], r["s_edge"]).wait_recv()

    def edge_rows(i, _):
        project(xh[i], pl.multiple_of(i * (ROWS + EDGE), EDGE), False, 0)
        return 0

    lax.fori_loop(0, 2, edge_rows, 0)

    top = lax.broadcasted_iota(jnp.int32, (EDGE, 1), 0) < HD

    def scores_of(p, b):
        at = pl.ds(pl.multiple_of(p * 128, 128), 128)
        keys, own = pl.ds(b * EDGE, SPAN), pl.ds(b * EDGE, EDGE)
        both = jnp.concatenate([r["qe"][own, at], r["qo"][own, at]], axis=0)
        return nt(r["k"][keys, at], both)

    def probs_of(b, scores):
        bias = r["bias"][b]
        scores = scores + jnp.concatenate([bias, bias], axis=1)
        powers = jnp.exp(scores - jnp.max(scores, axis=0, keepdims=True))
        return (powers * (1.0 / column_sum(powers))).astype(BF)

    def mix(p, b, probs):
        at = pl.ds(pl.multiple_of(p * 128, 128), 128)
        keys, own = pl.ds(b * EDGE, SPAN), pl.ds(b * EDGE, EDGE)
        r["probs"][p, b] = probs
        mixed = nn(r["vT"][at, keys], probs)
        r["attT"][at, own] = jnp.where(top, mixed[:, :128], mixed[:, 128:]).astype(BF)

    def attend(p, _):
        scores = scores_of(p, 0)
        before = None
        for b in range(4):
            following = scores_of(p, b + 1) if b < 3 else None
            probs = probs_of(b, scores)
            if b > 0:
                mix(p, b - 1, before)
            before, scores = probs, following
        mix(p, 3, before)
        return 0

    lax.fori_loop(0, PAIRS, attend, 0)

    load_wo.wait()
    mid, total, n2, n2T = r["mid"], r["total"], r["n2"], r["n2T"]
    middle_gain, middle_shift = r["middle_gain"][...], r["middle_shift"][...]

    def finish_attention(i, _):
        at = pl.ds(pl.multiple_of(i * 256, 256), 256)
        mixed = r["attT"][:, at].T
        middle = x[at, :].astype(F32) + nn(mixed, r["wo"][...]) + r["output_bias"][...]
        mid[at, :] = middle
        total[at, :] = middle + r["reduce_bias"][...]
        normal, _ = stats(middle)
        low = (normal * middle_gain + middle_shift).astype(BF)
        n2[at, :] = low
        n2T[:, at] = low.T
        r["dn"][at, :] = jnp.zeros((256, D), F32)
        return 0

    lax.fori_loop(0, 2, finish_attention, 0)
    load_dy.wait()

    def feed_forward(i, _):
        s = i % STREAM
        for copy in ffn_loads(i):
            copy.wait()
        we, wr = r["we"].at[s], r["wr"].at[s]
        at = pl.ds(pl.multiple_of(i * TICK, TICK), TICK)
        bias = r["expand_bias"][:, at]
        bias_sum = jnp.zeros((1, TICK), F32)
        rows = [pl.ds(half * 256, 256) for half in range(2)]
        hidden = [nn(n2[part, :], we[...]) + bias for part in rows]
        back = [nt(dy[part, :], wr[...]) for part in rows]
        for half, part in enumerate(rows):
            share, slope = normal_parts(hidden[half])
            active = (hidden[half] * share).astype(BF)
            hidden_gradient = back[half] * (share + slope)
            bias_sum = bias_sum + column_sum(hidden_gradient)
            low = hidden_gradient.astype(BF)
            r["hl"][part, :] = low
            r["actT"][at, part] = active.T
            total[part, :] += nn(active, wr[...])
            r["dn"][part, :] += nt(low, we[...])
        r["eb"][:, at] = bias_sum
        for part in range(2):
            block = nn(n2T[part * 384 : (part + 1) * 384, :], r["hl"][...]).astype(BF)
            store_rows(block, i, part * 2, 2)
        comm.start(i)

        @pl.when(i + STREAM < TICKS)
        def _():
            for copy in ffn_loads(i + STREAM):
                copy.start()

        comm.advance_two(i, 0)
        return 0

    def store_rows(block, chunk, a0, na):
        slot = chunk % SLOTS
        for a in range(na):
            for b in range(B):
                for c in range(2):
                    row = ((a * B + b) * 2 + c) * R
                    for col in range(block.shape[1] // 128):
                        G[slot, c, col, b, a0 + a] = block[row : row + R, col * 128 : (col + 1) * 128]

    lax.fori_loop(0, TICKS, feed_forward, 0)

    def turn(i, _):
        at = pl.ds(pl.multiple_of(i * 256, 256), 256)
        r["kT"][:, at] = r["k"][at, :].T

        @pl.when(i < 2)
        def _():
            r["n1T"][:, at] = r["ml"][at, :].T

        return 0

    lax.fori_loop(0, 3, turn, 0)

    def reduce_gradient(p, _):
        at = pl.ds(pl.multiple_of(p * 256, 256), 256)
        chunk = 6 + 2 * p

        def part(a, _):
            block = nn(r["actT"][pl.ds(pl.multiple_of(a * D, D), D), :], dy[:, at]).astype(BF)
            for h in range(2):
                slot = (chunk + h) % SLOTS
                for b in range(B):
                    for c in range(2):
                        for k in range(4):
                            row = ((b * 2 + c) * 4 + k) * R
                            G[slot, c, k, b, a] = block[row : row + R, h * 128 : (h + 1) * 128]
            return 0

        lax.fori_loop(0, A, part, 0)
        comm.start(chunk)
        comm.start(chunk + 1)
        comm.advance_two(6 + p, 0)
        return 0

    lax.fori_loop(0, 3, reduce_gradient, 0)

    def middle_back(i, _):
        at = pl.ds(pl.multiple_of(i * 256, 256), 256)
        out_rows[at, :] = total[at, :].astype(BF)
        error = r["dn"][at, :]
        normal, inverse = stats(mid[at, :])
        scaled = error * middle_gain
        part = inverse * (
            scaled
            - jnp.mean(scaled, axis=-1, keepdims=True)
            - normal * jnp.mean(scaled * normal, axis=-1, keepdims=True)
        )
        incoming = dy[at, :].astype(F32)
        gradient = incoming + part
        vec[5:6, :] += column_sum(error * normal)
        vec[6:7, :] += column_sum(error)
        vec[4:5, :] += column_sum(gradient)
        vec[11:12, :] += column_sum(incoming)
        mid[at, :] = gradient
        low = gradient.astype(BF)
        r["ml"][at, :] = low
        back = nt(low, r["wo"][...]).astype(BF)
        r["oe"][at, :] = jnp.where(even, back, BF(0))
        r["oo"][at, :] = jnp.where(even, BF(0), back)
        total[at, :] = jnp.zeros((256, D), F32)
        return 0

    lax.fori_loop(0, 2, middle_back, 0)
    save_out = pltpu.make_async_copy(out_rows, r["out"], r["save"].at[0])
    save_out.start()
    for k in range(4):
        vec[7 + k : 8 + k, :] = r["eb"][:, k * D : (k + 1) * D]
    comm.advance(17)
    comm.advance(18)

    place = lax.axis_index("dp")
    n2v, n4v = g.dp // 2, g.dp // 4
    lane = lax.broadcasted_iota(jnp.int32, (1, ROWS), 1)
    want = jnp.where(
        lane < 128,
        lane + place * R,
        jnp.where(lane < 256, lane - 128 + (place % n2v) * (2 * R), lane - 256 + (place % n4v) * (4 * R)),
    )
    spot = lax.broadcasted_iota(jnp.int32, (D, ROWS), 0)
    r["n2T"][...] = jnp.where(spot == want, 1.0, 0.0).astype(BF)

    parts, jq, sent, got, s_part = r["parts"], r["jq"], r["sent"], r["got"], r["s_part"]

    def part_copies(p):
        return (
            edge((p,), 0, sent.at[p % 2, 0], got.at[p, 1], s_part),
            edge((p,), 1, sent.at[p % 2, 1], got.at[p, 0], s_part),
        )

    def attend_back(p):
        at = pl.ds(pl.multiple_of(p * 128, 128), 128)
        slot = p % 2
        own_sum = jnp.zeros((1, 128), F32)
        parts[slot] = jnp.zeros((ROWS + 2 * EDGE, 256), F32)

        def errors_of(b):
            own = pl.ds(b * EDGE, EDGE)
            return jnp.concatenate([r["oe"][own, at], r["oo"][own, at]], axis=0)

        def shares_of(b):
            return nt(r["v"][pl.ds(b * EDGE, SPAN), at], errors_of(b))

        def score_gradient_of(b, shares):
            wide = r["probs"][p, b].astype(F32)
            product = wide * shares
            return (product - wide * column_sum(product)).astype(BF)

        def spread(b, low):
            keys, own = pl.ds(b * EDGE, SPAN), pl.ds(b * EDGE, EDGE)
            queries = jnp.concatenate([r["qe"][own, at], r["qo"][own, at]], axis=0)
            parts[slot, keys, 0:128] += nn(low, queries)
            parts[slot, keys, 128:256] += nn(r["probs"][p, b], errors_of(b))
            turned = nn(r["kT"][at, keys], low)
            mine = (jnp.where(top, turned[:, :128], turned[:, 128:]) * HD**-0.5).T
            jq[slot, own, :] = mine.astype(BF)
            return column_sum(mine)

        to_left, to_right = part_copies(p)

        def send_edges():
            @pl.when(has_left)
            def _():
                sent[slot, 0] = parts[slot, EDGE - NEAR : EDGE, :].astype(BF)
                to_left.start()

            @pl.when(has_right)
            def _():
                sent[slot, 1] = parts[slot, ROWS + EDGE : ROWS + EDGE + NEAR, :].astype(BF)
                to_right.start()

        order = (0, 3, 1, 2)
        shares = shares_of(order[0])
        before = None
        for step, b in enumerate(order):
            following = shares_of(order[step + 1]) if step < 3 else None
            low = score_gradient_of(b, shares)
            if step > 0:
                own_sum = own_sum + spread(order[step - 1], before)
            if step == 2:
                send_edges()
            before, shares = low, following
        own_sum = own_sum + spread(order[3], before)
        vec[2:3, at] = own_sum

    def joint_gradient(p):
        at = pl.ds(pl.multiple_of(p * 128, 128), 128)
        slot = p % 2
        to_left, to_right = part_copies(p)

        @pl.when(has_left)
        def _():
            to_left.wait_send()
            to_right.wait_recv()
            parts[slot, EDGE : EDGE + NEAR, :] += got[p, 0].astype(F32)

        @pl.when(has_right)
        def _():
            to_right.wait_send()
            to_left.wait_recv()
            parts[slot, ROWS + EDGE - NEAR : ROWS + EDGE, :] += got[p, 1].astype(F32)

        sums = parts[slot, EDGE : ROWS + EDGE, :]
        vec[3:4, at] = column_sum(sums[:, 128:])
        low = jnp.concatenate([jq[slot], sums.astype(BF)], axis=1)
        wj = r["wj"]
        weights = jnp.concatenate([wj[:, pl.ds(pl.multiple_of(k * D + p * 128, 128), 128)] for k in range(3)], axis=1)
        total[...] += nt(low, weights)
        low_out = r["ml"][:, at]
        for part in range(2):
            rows = pl.ds(part * 384, 384)
            block = nn(r["n1T"][rows, :], low).astype(BF)
            block_out = nn(r["attT"][rows, :], low_out).astype(BF)
            store_rows(jnp.concatenate([block, block_out], axis=1), 12 + p, part * 2, 2)
        comm.start(12 + p)

    def pair_step(i, _):
        @pl.when(i < PAIRS)
        def _():
            attend_back(i)

        @pl.when(i > 0)
        def _():
            joint_gradient(i - 1)

        comm.advance_two(10 + i, 0)
        return 0

    lax.fori_loop(0, PAIRS + 1, pair_step, 0)

    def entry_back(i, _):
        at = pl.ds(pl.multiple_of(i * 256, 256), 256)
        error = total[at, :]
        normal, inverse = stats(x[at, :].astype(F32))
        scaled = error * entry_gain
        part = inverse * (
            scaled
            - jnp.mean(scaled, axis=-1, keepdims=True)
            - normal * jnp.mean(scaled * normal, axis=-1, keepdims=True)
        )
        vec[0:1, :] += column_sum(error * normal)
        vec[1:2, :] += column_sum(error)
        dx_rows[at, :] = (mid[at, :] + part).astype(BF)
        return 0

    lax.fori_loop(0, 2, entry_back, 0)
    save_dx = pltpu.make_async_copy(dx_rows, r["dx"], r["save"].at[1])
    save_dx.start()

    rv, s_vec = r["rv"], r["s_vec"]

    def vector_copies(step):
        groups = (
            [comm.dev(c=1 - comm.c)],
            [comm.dev(b=(comm.b + k) % B) for k in range(1, B)],
            [comm.dev(a=(comm.a + k) % A) for k in range(1, A)],
            [comm.dev(y=(comm.y + k) % Y) for k in range(1, Y)],
        )
        ids = (comm.c, comm.b, comm.a, comm.y)
        base = (0, 2, 0, A)[step]
        held = rv if step < 2 else r["rvl"]
        here = held.at[base + ids[step]]
        return here, [
            comm.copy(here, here, s_vec, ((0, 2, 2 + B, 2 + B + A)[step] + k,), other) for k, other in enumerate(groups[step])
        ]

    def vector_sum(step):
        base, size = ((0, 2), (2, B), (0, A), (A, Y))[step]
        held = rv if step < 2 else r["rvl"]
        value = held[base].astype(F32)
        for k in range(1, size):
            value = value + held[base + k].astype(F32)
        return value

    def vector_start(step, value):
        here, copies = vector_copies(step)
        here[...] = value.astype(here.dtype)
        for copy in copies:
            copy.start()

    def vector_wait(step):
        for copy in vector_copies(step)[1]:
            copy.wait()

    def pick_vectors():
        summed = vector_sum(3)
        high = summed.astype(BF)
        rest = (summed - high.astype(F32)).astype(BF)
        picked = nn(high, r["n2T"][...]) + nn(rest, r["n2T"][...])
        kind = lax.broadcasted_iota(jnp.int32, (16, 1), 0)
        r["v_out"][...] = picked[:, 0:128]
        r["jb_out"][...] = column_sum(jnp.where(kind == 2 + place // n2v, picked[:, 128:256], 0.0))
        r["eb_out"][...] = column_sum(jnp.where(kind == 7 + place // n4v, picked[:, 256:512], 0.0))

    save_e = pltpu.make_async_copy(r["e_sum"], r["e_out"], r["save"].at[2])
    save_r = pltpu.make_async_copy(r["r_sum"], r["r_out"], r["save"].at[3])
    vector_start(0, vec[...])
    for t in range(34, 2 * CHUNKS + AFTER[4] - 1, 2):
        comm.advance(t)
        if t in VECTOR_STEPS:
            step = VECTOR_STEPS.index(t)
            vector_wait(step)
            if step < 3:
                vector_start(step + 1, vector_sum(step))
            else:
                pick_vectors()
        if t == 2 * 11 + AFTER[4]:
            save_e.start()
            save_r.start()
    save_e.wait()
    save_r.wait()
    save_out.wait()
    save_dx.wait()


def layer(g, patches, segments, vectors, weights, cotangent):
    A, B, R, Y = g.A, g.B, g.R, g.Y
    comm_shapes = comm_scratch(g)
    V = pl.BlockSpec(memory_space=pltpu.VMEM)
    H = pl.BlockSpec(memory_space=pl.ANY)
    inputs = dict(
        patches=(patches, H),
        cotangent=(cotangent, H),
        segments=(segments, V),
        w_joint=(weights[0], H),
        w_output=(weights[1], H),
        w_expand=(weights[2], H),
        w_reduce=(weights[3], H),
        **{name: (value, V) for name, value in vectors.items()},
    )
    outputs = dict(
        out=((ROWS, D), BF),
        dx=((ROWS, D), BF),
        j_out=((R, 3 * D), F32),
        o_out=((R, D), F32),
        e_out=((R, FF), F32),
        r_out=((4 * R, D), F32),
        v_out=((16, 128), F32),
        jb_out=((1, 128), F32),
        eb_out=((1, 256), F32),
    )
    ext = ROWS + 2 * EDGE
    scratch = dict(
        x=pltpu.VMEM((ROWS, D), BF),
        xh=pltpu.VMEM((2, EDGE, D), BF),
        dy=pltpu.VMEM((ROWS, D), BF),
        wj=pltpu.VMEM((D, 3 * D), BF),
        wo=pltpu.VMEM((D, D), BF),
        we=pltpu.VMEM((STREAM, D, TICK), BF),
        wr=pltpu.VMEM((STREAM, TICK, D), BF),
        n1T=pltpu.VMEM((D, ROWS), BF),
        qe=pltpu.VMEM((ROWS, D), BF),
        qo=pltpu.VMEM((ROWS, D), BF),
        k=pltpu.VMEM((ext, D), BF),
        v=pltpu.VMEM((ext, D), BF),
        kT=pltpu.VMEM((D, ext), BF),
        vT=pltpu.VMEM((D, ext), BF),
        bias=pltpu.VMEM((4, SPAN, EDGE), F32),
        probs=pltpu.VMEM((PAIRS, 4, SPAN, 2 * EDGE), BF),
        attT=pltpu.VMEM((D, ROWS), BF),
        mid=pltpu.VMEM((ROWS, D), F32),
        total=pltpu.VMEM((ROWS, D), F32),
        dn=pltpu.VMEM((ROWS, D), F32),
        n2=pltpu.VMEM((ROWS, D), BF),
        n2T=pltpu.VMEM((D, ROWS), BF),
        hl=pltpu.VMEM((ROWS, TICK), BF),
        actT=pltpu.VMEM((FF, ROWS), BF),
        eb=pltpu.VMEM((1, FF), F32),
        ml=pltpu.VMEM((ROWS, D), BF),
        parts=pltpu.VMEM((2, ext, 256), F32),
        jq=pltpu.VMEM((2, ROWS, 128), BF),
        sent=pltpu.VMEM((2, 2, NEAR, 256), BF),
        got=pltpu.VMEM((PAIRS, 2, NEAR, 256), BF),
        vec=pltpu.VMEM((16, D), F32),
        rv=pltpu.VMEM((2 + B, 16, D), F32),
        rvl=pltpu.VMEM((A + Y, 16, D), BF),
        G=pltpu.VMEM((SLOTS, 2, 4, B, A, R, 128), BF),
        load=pltpu.SemaphoreType.DMA((4,)),
        save=pltpu.SemaphoreType.DMA((4,)),
        e_sum=pltpu.VMEM((R, FF), F32),
        r_sum=pltpu.VMEM((4 * R, D), F32),
        stream=pltpu.SemaphoreType.DMA((2, STREAM)),
        s_edge=pltpu.SemaphoreType.DMA((2, 2)),
        s_part=pltpu.SemaphoreType.DMA((2, PAIRS, 2)),
        s_vec=pltpu.SemaphoreType.DMA((2, 2 + B + A + Y)),
        **{name + "_row": pltpu.VMEM((1, value.shape[0]), F32) for name, value in vectors.items()},
        **comm_shapes,
    )
    names = (*inputs, *outputs, *scratch)
    results = pl.pallas_call(
        functools.partial(layer_kernel, g, names),
        out_shape=tuple(jax.ShapeDtypeStruct(*shape) for shape in outputs.values()),
        in_specs=[spec for _, spec in inputs.values()],
        out_specs=[H if name in ("out", "dx", "e_out", "r_out") else V for name in outputs],
        scratch_shapes=list(scratch.values()),
        compiler_params=pltpu.CompilerParams(
            collective_id=0, has_side_effects=True, vmem_limit_bytes=64 << 20
        ),
    )(*(value for value, _ in inputs.values()))
    return hand_over(g, dict(zip(outputs, results)))


def hand_over_kernel(g, out, dx, j, o, e, w, v, jb, eb, *refs):
    outs, held, sems = refs[:14], refs[14:20], refs[20]
    R = g.R
    moves = [(out, 0), (dx, 1), (j, 4), (o, 6), (e, 10), (w, 12)]
    loads = [pltpu.make_async_copy(src, held[i], sems.at[0, i]) for i, (src, _) in enumerate(moves)]
    copies = [pltpu.make_async_copy(held[i], outs[k], sems.at[1, i]) for i, (_, k) in enumerate(moves)]
    for load in loads:
        load.start()
    for load, copy in zip(loads, copies):
        load.wait()
        copy.start()
    for row, k in ((0, 2), (1, 3), (4, 7), (5, 8), (6, 9), (11, 13)):
        outs[k][...] = v[row, :R]
    outs[5][...] = jb[0, : 2 * R]
    outs[11][...] = eb[0, : 4 * R]
    for copy in copies:
        copy.wait()


def hand_over(g, o):
    R = g.R
    V = pl.BlockSpec(memory_space=pltpu.VMEM)
    H = pl.BlockSpec(memory_space=pl.ANY)
    shapes = [
        ((ROWS, D), BF), ((ROWS, D), BF), ((R,), F32), ((R,), F32), ((R, 3 * D), F32), ((2 * R,), F32), ((R, D), F32),
        ((R,), F32), ((R,), F32), ((R,), F32), ((R, FF), F32), ((4 * R,), F32), ((4 * R, D), F32), ((R,), F32),
    ]
    names = ("out", "dx", "j_out", "o_out", "e_out", "r_out", "v_out", "jb_out", "eb_out")
    return pl.pallas_call(
        functools.partial(hand_over_kernel, g),
        out_shape=tuple(jax.ShapeDtypeStruct(*shape) for shape in shapes),
        in_specs=[H] * 6 + [V] * 3,
        out_specs=[V if len(shape) == 1 else H for shape, _ in shapes],
        scratch_shapes=[
            *(pltpu.VMEM(o[name].shape, o[name].dtype) for name in names[:6]),
            pltpu.SemaphoreType.DMA((2, 6)),
        ],
    )(*(o[name] for name in names))


def local(
    patches,
    segments,
    entry_gain,
    entry_shift,
    joint_weight,
    joint_bias,
    output_weight,
    output_bias,
    middle_gain,
    middle_shift,
    expand_weight,
    expand_bias,
    reduce_weight,
    reduce_bias,
    cotangent,
):
    g = Grid(lax.axis_size("dp"), lax.axis_size("blk"), D)
    R = g.R
    vectors = dict(
        entry_gain=entry_gain,
        entry_shift=entry_shift,
        joint_bias=joint_bias,
        output_bias=output_bias,
        middle_gain=middle_gain,
        middle_shift=middle_shift,
        expand_bias=expand_bias,
        reduce_bias=reduce_bias,
    )
    o = layer(
        g,
        patches[0],
        segments.reshape(-1, EDGE),
        vectors,
        (joint_weight, output_weight, expand_weight, reduce_weight),
        cotangent[0],
    )
    return (o[0][None], o[1][None], *o[2:])


def solution(mesh):
    return jax.shard_map(
        local,
        mesh=mesh,
        in_specs=(
            P("dp", "blk", None),
            P("dp", None),
            P(),
            P(),
            P(),
            P(),
            P(),
            P(),
            P(),
            P(),
            P(),
            P(),
            P(),
            P(),
            P("dp", "blk", None),
        ),
        out_specs=(
            P("dp", "blk", None),
            P("dp", "blk", None),
            P("dp"),
            P("dp"),
            P("dp", None),
            P("dp"),
            P("dp", None),
            P("dp"),
            P("dp"),
            P("dp"),
            P("dp", None),
            P("dp"),
            P("dp", None),
            P("dp"),
        ),
        check_vma=False,
    )
```

```python
import functools
import jax
import jax.numpy as jnp
from jax import lax
from jax.experimental import pallas as pl
from jax.experimental.pallas import tpu as pltpu
from jax.sharding import PartitionSpec as P

MESH = pl.DeviceIdType.MESH
CHUNKS = 18
AFTER = (2, 6, 10, 14, 18)
RING = 9
VECTOR_STEPS = (36, 40, 44, 48)
BF = jnp.bfloat16
F32 = jnp.float32


class Grid:
    def __init__(self, dp, blk, width):
        self.A = 4
        self.B = dp // 8
        self.Y = blk
        self.dp = dp
        self.R = width // dp
        self.kinds = 2 if blk == 2 else 1


def comm_scratch(g):
    A, B, Y, R = g.A, g.B, g.Y, g.R
    n = CHUNKS // g.kinds
    shapes = dict(
        r0=pltpu.VMEM((RING, 4, B, A, R, 128), BF),
        rx=pltpu.VMEM((n, B - 1, 4, A, R, 128), BF),
        rz=pltpu.VMEM((n, A - 1, 4, R, 128), BF),
        ryx=pltpu.VMEM((n, Y, 4, R, 128), BF),
        s_core=pltpu.SemaphoreType.DMA((2, CHUNKS)),
        s_x=pltpu.SemaphoreType.DMA((2, CHUNKS, B - 1)),
        s_z=pltpu.SemaphoreType.DMA((2, CHUNKS)),
        s_y=pltpu.SemaphoreType.DMA((2, CHUNKS, Y - 1)),
    )
    if g.kinds == 2:
        shapes.update(
            ry=pltpu.VMEM((n, 2, B, A, R, 128), BF),
            rx2=pltpu.VMEM((n, B - 1, 2, A, R, 128), BF),
            rz2=pltpu.VMEM((n, A - 1, 2, R, 128), BF),
            rag=pltpu.VMEM((n, 2, 2, R, 128), BF),
            s_ag=pltpu.SemaphoreType.DMA((2, CHUNKS)),
        )
    return shapes


class Comm:
    def __init__(self, g, G, slots, refs, emit):
        self.g, self.G, self.slots, self.emit = g, G, slots, emit
        self.__dict__.update(refs)
        dp = lax.axis_index("dp")
        self.y = lax.axis_index("blk")
        self.c = dp % 2
        self.b = (dp // 2) % g.B
        self.a = dp // (2 * g.B)

    def dev(self, a=None, b=None, c=None, y=None):
        a = self.a if a is None else a
        b = self.b if b is None else b
        c = self.c if c is None else c
        y = self.y if y is None else y
        return ((a * self.g.B + b) * 2 + c, y)

    def partners(self):
        g = self.g
        return (
            [self.dev(c=1 - self.c)]
            + [self.dev(b=(self.b + k) % g.B) for k in range(1, g.B)]
            + [self.dev(a=(self.a + k) % g.A) for k in range(1, g.A)]
            + [self.dev(y=(self.y + k) % g.Y) for k in range(1, g.Y)]
        )

    def barrier(self):
        sem = pltpu.get_barrier_semaphore()
        others = self.partners()
        for other in others:
            pl.semaphore_signal(sem, inc=1, device_id=other, device_id_type=MESH)
        pl.semaphore_wait(sem, len(others))

    def copy(self, src, dst, sems, index, device):
        return pltpu.make_async_remote_copy(
            src_ref=src,
            dst_ref=dst,
            send_sem=sems.at[(0,) + index],
            recv_sem=sems.at[(1,) + index],
            device_id=device,
            device_id_type=MESH,
        )

    def core(self, j, kind):
        copy = self.copy(
            self.G.at[j % self.slots, 1 - self.c], self.r0.at[j % RING], self.s_core, (j,), self.dev(c=1 - self.c)
        )
        return [copy], [copy]

    def along_b(self, j, kind):
        g, i = self.g, j // self.g.kinds
        landing = self.rx2 if kind else self.rx
        cols = pl.ds(2 * self.y, 2) if kind else pl.ds(0, 4)
        copies = []
        for k in range(1, g.B):
            other = (self.b + k) % g.B
            source = self.G.at[j % self.slots, self.c, cols, other]
            copies.append(self.copy(source, landing.at[i, k - 1], self.s_x, (j, k - 1), self.dev(b=other)))
        return copies, copies

    def along_a(self, j, kind):
        g, i = self.g, j // self.g.kinds
        landing = self.rz2 if kind else self.rz
        cols = pl.ds(2 * self.y, 2) if kind else pl.ds(0, 4)
        copies = []
        for k in range(1, g.A):
            other = (self.a + k) % g.A
            source = self.G.at[j % self.slots, self.c, cols, self.b, other]
            copies.append(self.copy(source, landing.at[i, k - 1], self.s_z, (j,), self.dev(a=other)))
        return copies, [self.copy(landing.at[i], landing.at[i], self.s_z, (j,), self.dev(a=(self.a + 1) % g.A))]

    def along_blk(self, j, kind):
        g, i = self.g, j // self.g.kinds
        if kind:
            source = self.G.at[j % self.slots, self.c, pl.ds(2 * (1 - self.y), 2)]
            copies = [self.copy(source, self.ry.at[i], self.s_y, (j, 0), self.dev(y=1 - self.y))]
            return copies, copies
        mine = self.ryx.at[i, self.y]
        copies = [
            self.copy(mine, mine, self.s_y, (j, k - 1), self.dev(y=(self.y + k) % g.Y)) for k in range(1, g.Y)
        ]
        return copies, copies

    def share(self, j, kind):
        mine = self.rag.at[j // 2, self.y]
        copies = [self.copy(mine, mine, self.s_ag, (j,), self.dev(y=1 - self.y))]
        return copies, copies

    def add(self, mine, parts):
        if len(parts) == 1:
            mine[...] = mine[...] + parts[0]
        else:
            mine[...] = self.summed(mine, parts)

    def summed(self, mine, parts):
        total = mine[...].astype(F32)
        for part in parts:
            total = total + part.astype(F32)
        return total.astype(BF)

    def after_core(self, j, kind):
        self.add(self.G.at[j % self.slots, self.c], [self.r0[j % RING]])

    def after_b(self, j, kind):
        g, i = self.g, j // self.g.kinds
        landing = self.rx2 if kind else self.rx
        cols = pl.ds(2 * self.y, 2) if kind else pl.ds(0, 4)
        self.add(self.G.at[j % self.slots, self.c, cols, self.b], [landing[i, k] for k in range(g.B - 1)])

    def after_a(self, j, kind):
        g, i = self.g, j // self.g.kinds
        landing = self.rz2 if kind else self.rz
        cols = pl.ds(2 * self.y, 2) if kind else pl.ds(0, 4)
        total = self.summed(
            self.G.at[j % self.slots, self.c, cols, self.b, self.a], [landing[i, k] for k in range(g.A - 1)]
        )
        if kind:
            self.rag[i, self.y] = total
        else:
            self.ryx[i, self.y] = total

    def after_blk(self, j, kind):
        g, i = self.g, j // self.g.kinds
        if kind:
            self.add(self.G.at[j % self.slots, self.c, pl.ds(2 * self.y, 2)], [self.ry[i]])
            return
        total = self.ryx[i, 0].astype(F32)
        for k in range(1, g.Y):
            total = total + self.ryx[i, k].astype(F32)
        self.emit(j, [total[col] for col in range(4)])

    def after_share(self, j, kind):
        i = j // 2
        self.emit(j, [self.rag[i, col // 2, col % 2].astype(F32) for col in range(4)])

    def plan(self, kind):
        core = (self.core, self.after_core)
        b = (self.along_b, self.after_b)
        a = (self.along_a, self.after_a)
        blk = (self.along_blk, self.after_blk)
        share = (self.share, self.after_share)
        return (core, blk, b, a, share) if kind else (core, b, a, blk)

    def start(self, j):
        self.core(j, 0)[0][0].start()

    def finish(self, stage, j):
        for kind in range(self.g.kinds):
            plan = self.plan(kind)
            if stage >= len(plan):
                continue

            def go(kind=kind, plan=plan):
                for copy in plan[stage][0](j, kind)[1]:
                    copy.wait()
                plan[stage][1](j, kind)
                if stage + 1 < len(plan):
                    for copy in plan[stage + 1][0](j, kind)[0]:
                        copy.start()

            if self.g.kinds == 1:
                go()
            elif isinstance(j, int):
                if (j + (j >= CHUNKS - 2)) % 2 == kind:
                    go()
            else:
                pl.when(jnp.where(j >= CHUNKS - 2, j + 1, j) % 2 == kind)(go)

    def advance(self, t):
        for stage in range(5):
            twice = t - AFTER[stage]
            if twice % 2 == 0 and 0 <= twice < 2 * CHUNKS:
                self.finish(stage, twice // 2)

    def advance_two(self, t, odd):
        for stage in range(5):
            if (odd - AFTER[stage]) % 2 == 0:
                j = t + (odd - AFTER[stage]) // 2

                @pl.when((j >= 0) & (j < CHUNKS))
                def _(stage=stage, j=j):
                    self.finish(stage, j)


def emit_to(g, j_ref, o_ref, e_ref, r_ref):
    R = g.R

    def emit(j, values):
        @pl.when(j < 6)
        def _():
            for col in range(4):
                e_ref[:, pl.ds(pl.multiple_of(j * 512 + col * 128, 128), 128)] = values[col]

        @pl.when((j >= 6) & (j < 12))
        def _():
            for k in range(4):
                r_ref[k * R : (k + 1) * R, pl.ds(pl.multiple_of((j - 6) * 128, 128), 128)] = values[k]

        @pl.when(j >= 12)
        def _():
            at = pl.multiple_of((j - 12) * 128, 128)
            for k in range(3):
                j_ref[:, pl.ds(pl.multiple_of(k * 768 + at, 128), 128)] = values[k]
            o_ref[:, pl.ds(at, 128)] = values[3]

    return emit


HEADS = 12
VECTORS = (
    "entry_gain", "entry_shift", "joint_bias", "output_bias",
    "middle_gain", "middle_shift", "expand_bias", "reduce_bias",
)
HD = 64
D = 768
FF = 3072
ROWS = 512
EDGE = 128
SPAN = 3 * EDGE
PAIRS = HEADS // 2
NEAR = 112
SLOTS = 12
STREAM = 2
TICK = 512
TICKS = FF // TICK


def nn(left, right):
    return jnp.dot(left, right, preferred_element_type=F32)


def nt(left, right):
    return lax.dot_general(left, right, (((1,), (1,)), ((), ())), preferred_element_type=F32)


def stats(values):
    average = jnp.mean(values, axis=-1, keepdims=True)
    centred = values - average
    spread = jnp.mean(centred * centred, axis=-1, keepdims=True)
    inverse = lax.rsqrt(spread + 1e-06)
    return centred * inverse, inverse


def normal_parts(hidden):
    half = hidden * (0.5**0.5)
    size = jnp.abs(half)
    ratio = 1.0 / (1.0 + 0.3275911 * size)
    bell = jnp.exp(-half * half)
    tail = ((((1.061405429 * ratio - 1.453152027) * ratio + 1.421413741) * ratio - 0.284496736) * ratio + 0.254829592) * ratio
    tail = 0.5 * tail * bell
    share = jnp.where(hidden >= 0, 1.0 - tail, tail)
    return share, hidden * bell * 0.3989422804014327


def column_sum(values):
    return jnp.sum(values, axis=0, keepdims=True)


def layer_kernel(g, names, *refs):
    r = dict(zip(names, refs))
    A, B, R, Y = g.A, g.B, g.R, g.Y
    (patches, cotangent, segments, w_joint, w_output, w_expand, w_reduce) = (
        r[n] for n in ("patches", "cotangent", "segments", "w_joint", "w_output", "w_expand", "w_reduce")
    )
    G, vec = r["G"], r["vec"]
    for name in VECTORS:
        r[name + "_row"][...] = r[name][...].reshape(1, -1)
        r[name] = r[name + "_row"]
    r["oe"], r["oo"] = r["vT"], r["n2"]
    out_rows, dx_rows = r["k"].at[pl.ds(0, ROWS)], r["ml"]
    x, xh, dy = r["x"], r["xh"], r["dy"]
    comm = Comm(g, G, SLOTS, r, emit_to(g, r["j_out"], r["o_out"], r["e_sum"], r["r_sum"]))
    y = comm.y
    has_left, has_right = y > 0, y < Y - 1

    def load(src, dst, k):
        return pltpu.make_async_copy(src, dst, r["load"].at[k])

    load_x = load(patches, x, 0)
    load_wj = load(w_joint, r["wj"], 1)
    load_wo = load(w_output, r["wo"], 2)
    load_dy = load(cotangent, dy, 3)

    def ffn_loads(i):
        s = i % STREAM
        at = pl.ds(pl.multiple_of(i * TICK, TICK), TICK)
        return (
            pltpu.make_async_copy(w_expand.at[:, at], r["we"].at[s], r["stream"].at[0, s]),
            pltpu.make_async_copy(w_reduce.at[at], r["wr"].at[s], r["stream"].at[1, s]),
        )

    load_x.start()
    load_wj.start()
    comm.barrier()

    def edge(k, side, src, dst, sems):
        other = comm.dev(y=(y + Y - 1) % Y) if side == 0 else comm.dev(y=(y + 1) % Y)
        return pltpu.make_async_remote_copy(
            src_ref=src, dst_ref=dst, send_sem=sems.at[(0,) + k + (side,)], recv_sem=sems.at[(1,) + k + (1 - side,)],
            device_id=other, device_id_type=MESH,
        )

    def x_edges():
        return (
            edge((), 0, patches.at[pl.ds(0, NEAR)], xh.at[1, pl.ds(0, NEAR)], r["s_edge"]),
            edge((), 1, patches.at[pl.ds(ROWS - NEAR, NEAR)], xh.at[0, pl.ds(EDGE - NEAR, NEAR)], r["s_edge"]),
        )

    to_left, to_right = x_edges()

    @pl.when(has_left)
    def _():
        to_left.start()

    @pl.when(has_right)
    def _():
        to_right.start()

    xh[0, 0 : EDGE - NEAR, :] = jnp.zeros((EDGE - NEAR, D), BF)
    xh[1, NEAR:EDGE, :] = jnp.zeros((EDGE - NEAR, D), BF)

    first_block = y * (ROWS // EDGE)
    count = segments.shape[0]
    columns = []
    for k in range(6):
        index = first_block + k - 1
        inside = (index >= 0) & (index < count)
        row = segments[pl.ds(jnp.clip(index, 0, count - 1), 1), :]
        row = jnp.where(inside, row, -1)
        columns.append(row)
    for b in range(4):
        for k in range(3):
            keys = jnp.broadcast_to(columns[b + k].astype(F32), (EDGE, EDGE)).T
            own = columns[b + 1].astype(F32)
            r["bias"][b, k * EDGE : (k + 1) * EDGE, :] = jnp.where(keys == own, 0.0, -1e30)

    vec[...] = jnp.zeros_like(vec)
    entry_gain, entry_shift = r["entry_gain"][...], r["entry_shift"][...]
    lanes = lax.broadcasted_iota(jnp.int32, (1, D), 1) % 128
    even = lanes < HD

    def project(rows, at, own, row_at):
        count = rows.shape[0]
        normal, _ = stats(rows.astype(F32))
        low = (normal * entry_gain + entry_shift).astype(BF)
        wj = r["wj"]
        key_rows = nn(low, wj[:, D : 2 * D]).astype(BF)
        r["k"][pl.ds(at, count), :] = key_rows
        value_rows = (nn(low, wj[:, 2 * D :]) + r["joint_bias"][:, D:]).astype(BF)
        r["v"][pl.ds(at, count), :] = value_rows
        r["vT"][:, pl.ds(at, count)] = value_rows.T
        if own:
            r["ml"][pl.ds(row_at, count), :] = low
            queries = (nn(low, wj[:, :D]) + r["joint_bias"][:, :D]).astype(BF) * BF(HD**-0.5)
            r["qe"][pl.ds(row_at, count), :] = jnp.where(even, queries, BF(0))
            r["qo"][pl.ds(row_at, count), :] = jnp.where(even, BF(0), queries)

    load_x.wait()
    load_wj.wait()
    load_wo.start()
    load_dy.start()
    for i in range(STREAM):
        for copy in ffn_loads(i):
            copy.start()

    def own_rows(i, _):
        at = pl.multiple_of(i * 256, 256)
        project(x[pl.ds(at, 256), :], pl.multiple_of(at + EDGE, EDGE), True, at)
        return 0

    lax.fori_loop(0, 2, own_rows, 0)

    @pl.when(has_left)
    def _():
        to_left.wait_send()
        to_right.wait_recv()

    @pl.when(has_right)
    def _():
        to_right.wait_send()
        to_left.wait_recv()

    def edge_rows(i, _):
        at = pl.multiple_of(i * (ROWS + EDGE), EDGE)
        present = jnp.where(i == 0, y, Y - 1 - y) > 0

        @pl.when(present)
        def _():
            project(xh[i], at, False, 0)

        @pl.when(jnp.logical_not(present))
        def _():
            r["k"][pl.ds(at, EDGE), :] = jnp.zeros((EDGE, D), BF)
            r["v"][pl.ds(at, EDGE), :] = jnp.zeros((EDGE, D), BF)
            r["vT"][:, pl.ds(at, EDGE)] = jnp.zeros((D, EDGE), BF)

        return 0

    lax.fori_loop(0, 2, edge_rows, 0)

    top = lax.broadcasted_iota(jnp.int32, (EDGE, 1), 0) < HD

    def scores_of(p, b):
        at = pl.ds(pl.multiple_of(p * 128, 128), 128)
        keys, own = pl.ds(b * EDGE, SPAN), pl.ds(b * EDGE, EDGE)
        both = jnp.concatenate([r["qe"][own, at], r["qo"][own, at]], axis=0)
        return nt(r["k"][keys, at], both)

    def probs_of(b, scores):
        bias = r["bias"][b]
        scores = scores + jnp.concatenate([bias, bias], axis=1)
        powers = jnp.exp(scores - jnp.max(scores, axis=0, keepdims=True))
        return (powers * (1.0 / column_sum(powers))).astype(BF)

    def mix(p, b, probs):
        at = pl.ds(pl.multiple_of(p * 128, 128), 128)
        keys, own = pl.ds(b * EDGE, SPAN), pl.ds(b * EDGE, EDGE)
        r["probs"][p, b] = probs
        mixed = nn(r["vT"][at, keys], probs)
        r["attT"][at, own] = jnp.where(top, mixed[:, :128], mixed[:, 128:]).astype(BF)

    def attend(p, _):
        scores = scores_of(p, 0)
        before = None
        for b in range(4):
            following = scores_of(p, b + 1) if b < 3 else None
            probs = probs_of(b, scores)
            if b > 0:
                mix(p, b - 1, before)
            before, scores = probs, following
        mix(p, 3, before)
        return 0

    lax.fori_loop(0, PAIRS, attend, 0)

    load_wo.wait()
    mid, total, n2, n2T = r["mid"], r["total"], r["n2"], r["n2T"]
    middle_gain, middle_shift = r["middle_gain"][...], r["middle_shift"][...]

    def finish_attention(i, _):
        at = pl.ds(pl.multiple_of(i * 256, 256), 256)
        mixed = r["attT"][:, at].T
        middle = x[at, :].astype(F32) + nn(mixed, r["wo"][...]) + r["output_bias"][...]
        mid[at, :] = middle
        total[at, :] = middle + r["reduce_bias"][...]
        normal, _ = stats(middle)
        low = (normal * middle_gain + middle_shift).astype(BF)
        n2[at, :] = low
        n2T[:, at] = low.T
        r["dn"][at, :] = jnp.zeros((256, D), F32)
        return 0

    lax.fori_loop(0, 2, finish_attention, 0)
    load_dy.wait()

    def feed_forward(i, _):
        s = i % STREAM
        for copy in ffn_loads(i):
            copy.wait()
        we, wr = r["we"].at[s], r["wr"].at[s]
        at = pl.ds(pl.multiple_of(i * TICK, TICK), TICK)
        bias = r["expand_bias"][:, at]
        bias_sum = jnp.zeros((1, TICK), F32)
        rows = [pl.ds(half * 256, 256) for half in range(2)]
        hidden = [nn(n2[part, :], we[...]) + bias for part in rows]
        back = [nt(dy[part, :], wr[...]) for part in rows]
        for half, part in enumerate(rows):
            share, slope = normal_parts(hidden[half])
            active = (hidden[half] * share).astype(BF)
            hidden_gradient = back[half] * (share + slope)
            bias_sum = bias_sum + column_sum(hidden_gradient)
            low = hidden_gradient.astype(BF)
            r["hl"][part, :] = low
            r["actT"][at, part] = active.T
            total[part, :] += nn(active, wr[...])
            r["dn"][part, :] += nt(low, we[...])
        r["eb"][:, at] = bias_sum
        for part in range(2):
            block = nn(n2T[part * 384 : (part + 1) * 384, :], r["hl"][...]).astype(BF)
            store_rows(block, i, part * 2, 2)
        comm.start(i)

        @pl.when(i + STREAM < TICKS)
        def _():
            for copy in ffn_loads(i + STREAM):
                copy.start()

        comm.advance_two(i, 0)
        return 0

    def store_rows(block, chunk, a0, na):
        slot = chunk % SLOTS
        for a in range(na):
            for b in range(B):
                for c in range(2):
                    row = ((a * B + b) * 2 + c) * R
                    for col in range(block.shape[1] // 128):
                        G[slot, c, col, b, a0 + a] = block[row : row + R, col * 128 : (col + 1) * 128]

    lax.fori_loop(0, TICKS, feed_forward, 0)

    def turn(i, _):
        at = pl.ds(pl.multiple_of(i * 256, 256), 256)
        r["kT"][:, at] = r["k"][at, :].T

        @pl.when(i < 2)
        def _():
            r["n1T"][:, at] = r["ml"][at, :].T

        return 0

    lax.fori_loop(0, 3, turn, 0)

    def reduce_gradient(p, _):
        at = pl.ds(pl.multiple_of(p * 256, 256), 256)
        chunk = 6 + 2 * p

        def part(a, _):
            block = nn(r["actT"][pl.ds(pl.multiple_of(a * D, D), D), :], dy[:, at]).astype(BF)
            for h in range(2):
                slot = (chunk + h) % SLOTS
                for b in range(B):
                    for c in range(2):
                        for k in range(4):
                            row = ((b * 2 + c) * 4 + k) * R
                            G[slot, c, k, b, a] = block[row : row + R, h * 128 : (h + 1) * 128]
            return 0

        lax.fori_loop(0, A, part, 0)
        comm.start(chunk)
        comm.start(chunk + 1)
        comm.advance_two(6 + p, 0)
        return 0

    lax.fori_loop(0, 3, reduce_gradient, 0)

    def middle_back(i, _):
        at = pl.ds(pl.multiple_of(i * 256, 256), 256)
        out_rows[at, :] = total[at, :].astype(BF)
        error = r["dn"][at, :]
        normal, inverse = stats(mid[at, :])
        scaled = error * middle_gain
        part = inverse * (
            scaled
            - jnp.mean(scaled, axis=-1, keepdims=True)
            - normal * jnp.mean(scaled * normal, axis=-1, keepdims=True)
        )
        incoming = dy[at, :].astype(F32)
        gradient = incoming + part
        vec[5:6, :] += column_sum(error * normal)
        vec[6:7, :] += column_sum(error)
        vec[4:5, :] += column_sum(gradient)
        vec[11:12, :] += column_sum(incoming)
        mid[at, :] = gradient
        low = gradient.astype(BF)
        r["ml"][at, :] = low
        back = nt(low, r["wo"][...]).astype(BF)
        r["oe"][at, :] = jnp.where(even, back, BF(0))
        r["oo"][at, :] = jnp.where(even, BF(0), back)
        total[at, :] = jnp.zeros((256, D), F32)
        return 0

    lax.fori_loop(0, 2, middle_back, 0)
    save_out = pltpu.make_async_copy(out_rows, r["out"], r["save"].at[0])
    save_out.start()
    for k in range(4):
        vec[7 + k : 8 + k, :] = r["eb"][:, k * D : (k + 1) * D]
    comm.advance(17)
    comm.advance(18)

    place = lax.axis_index("dp")
    n2v, n4v = g.dp // 2, g.dp // 4
    lane = lax.broadcasted_iota(jnp.int32, (1, ROWS), 1)
    want = jnp.where(
        lane < 128,
        lane + place * R,
        jnp.where(lane < 256, lane - 128 + (place % n2v) * (2 * R), lane - 256 + (place % n4v) * (4 * R)),
    )
    spot = lax.broadcasted_iota(jnp.int32, (D, ROWS), 0)
    r["n2T"][...] = jnp.where(spot == want, 1.0, 0.0).astype(BF)

    parts, jq, sent, got, s_part = r["parts"], r["jq"], r["sent"], r["got"], r["s_part"]

    def part_copies(p):
        return (
            edge((p,), 0, sent.at[p % 2, 0], got.at[p, 1], s_part),
            edge((p,), 1, sent.at[p % 2, 1], got.at[p, 0], s_part),
        )

    def attend_back(p):
        at = pl.ds(pl.multiple_of(p * 128, 128), 128)
        slot = p % 2
        own_sum = jnp.zeros((1, 128), F32)
        parts[slot] = jnp.zeros((ROWS + 2 * EDGE, 256), F32)

        def errors_of(b):
            own = pl.ds(b * EDGE, EDGE)
            return jnp.concatenate([r["oe"][own, at], r["oo"][own, at]], axis=0)

        def shares_of(b):
            return nt(r["v"][pl.ds(b * EDGE, SPAN), at], errors_of(b))

        def score_gradient_of(b, shares):
            wide = r["probs"][p, b].astype(F32)
            product = wide * shares
            return (product - wide * column_sum(product)).astype(BF)

        def spread(b, low):
            keys, own = pl.ds(b * EDGE, SPAN), pl.ds(b * EDGE, EDGE)
            queries = jnp.concatenate([r["qe"][own, at], r["qo"][own, at]], axis=0)
            parts[slot, keys, 0:128] += nn(low, queries)
            parts[slot, keys, 128:256] += nn(r["probs"][p, b], errors_of(b))
            turned = nn(r["kT"][at, keys], low)
            mine = (jnp.where(top, turned[:, :128], turned[:, 128:]) * HD**-0.5).T
            jq[slot, own, :] = mine.astype(BF)
            return column_sum(mine)

        to_left, to_right = part_copies(p)

        def send_edges():
            @pl.when(has_left)
            def _():
                sent[slot, 0] = parts[slot, EDGE - NEAR : EDGE, :].astype(BF)
                to_left.start()

            @pl.when(has_right)
            def _():
                sent[slot, 1] = parts[slot, ROWS + EDGE : ROWS + EDGE + NEAR, :].astype(BF)
                to_right.start()

        order = (0, 3, 1, 2)
        shares = shares_of(order[0])
        before = None
        for step, b in enumerate(order):
            following = shares_of(order[step + 1]) if step < 3 else None
            low = score_gradient_of(b, shares)
            if step > 0:
                own_sum = own_sum + spread(order[step - 1], before)
            if step == 2:
                send_edges()
            before, shares = low, following
        own_sum = own_sum + spread(order[3], before)
        vec[2:3, at] = own_sum

    def joint_gradient(p):
        at = pl.ds(pl.multiple_of(p * 128, 128), 128)
        slot = p % 2
        to_left, to_right = part_copies(p)

        @pl.when(has_left)
        def _():
            to_left.wait_send()
            to_right.wait_recv()
            parts[slot, EDGE : EDGE + NEAR, :] += got[p, 0].astype(F32)

        @pl.when(has_right)
        def _():
            to_right.wait_send()
            to_left.wait_recv()
            parts[slot, ROWS + EDGE - NEAR : ROWS + EDGE, :] += got[p, 1].astype(F32)

        sums = parts[slot, EDGE : ROWS + EDGE, :]
        vec[3:4, at] = column_sum(sums[:, 128:])
        low = jnp.concatenate([jq[slot], sums.astype(BF)], axis=1)
        wj = r["wj"]
        weights = jnp.concatenate([wj[:, pl.ds(pl.multiple_of(k * D + p * 128, 128), 128)] for k in range(3)], axis=1)
        total[...] += nt(low, weights)
        low_out = r["ml"][:, at]
        for part in range(2):
            rows = pl.ds(part * 384, 384)
            block = nn(r["n1T"][rows, :], low).astype(BF)
            block_out = nn(r["attT"][rows, :], low_out).astype(BF)
            store_rows(jnp.concatenate([block, block_out], axis=1), 12 + p, part * 2, 2)
        comm.start(12 + p)

    def pair_step(i, _):
        @pl.when(i < PAIRS)
        def _():
            attend_back(i)

        @pl.when(i > 0)
        def _():
            joint_gradient(i - 1)

        comm.advance_two(10 + i, 0)
        return 0

    lax.fori_loop(0, PAIRS + 1, pair_step, 0)

    def entry_back(i, _):
        at = pl.ds(pl.multiple_of(i * 256, 256), 256)
        error = total[at, :]
        normal, inverse = stats(x[at, :].astype(F32))
        scaled = error * entry_gain
        part = inverse * (
            scaled
            - jnp.mean(scaled, axis=-1, keepdims=True)
            - normal * jnp.mean(scaled * normal, axis=-1, keepdims=True)
        )
        vec[0:1, :] += column_sum(error * normal)
        vec[1:2, :] += column_sum(error)
        dx_rows[at, :] = (mid[at, :] + part).astype(BF)
        return 0

    lax.fori_loop(0, 2, entry_back, 0)
    save_dx = pltpu.make_async_copy(dx_rows, r["dx"], r["save"].at[1])
    save_dx.start()

    rv, s_vec = r["rv"], r["s_vec"]

    def vector_copies(step):
        groups = (
            [comm.dev(c=1 - comm.c)],
            [comm.dev(b=(comm.b + k) % B) for k in range(1, B)],
            [comm.dev(a=(comm.a + k) % A) for k in range(1, A)],
            [comm.dev(y=(comm.y + k) % Y) for k in range(1, Y)],
        )
        ids = (comm.c, comm.b, comm.a, comm.y)
        base = (0, 2, 0, A)[step]
        held = rv if step < 2 else r["rvl"]
        here = held.at[base + ids[step]]
        return here, [
            comm.copy(here, here, s_vec, ((0, 2, 2 + B, 2 + B + A)[step] + k,), other) for k, other in enumerate(groups[step])
        ]

    def vector_sum(step):
        base, size = ((0, 2), (2, B), (0, A), (A, Y))[step]
        held = rv if step < 2 else r["rvl"]
        value = held[base].astype(F32)
        for k in range(1, size):
            value = value + held[base + k].astype(F32)
        return value

    def vector_start(step, value):
        here, copies = vector_copies(step)
        here[...] = value.astype(here.dtype)
        for copy in copies:
            copy.start()

    def vector_wait(step):
        for copy in vector_copies(step)[1]:
            copy.wait()

    def pick_vectors():
        summed = vector_sum(3)
        high = summed.astype(BF)
        rest = (summed - high.astype(F32)).astype(BF)
        picked = nn(high, r["n2T"][...]) + nn(rest, r["n2T"][...])
        kind = lax.broadcasted_iota(jnp.int32, (16, 1), 0)
        r["v_out"][...] = picked[:, 0:128]
        r["jb_out"][...] = column_sum(jnp.where(kind == 2 + place // n2v, picked[:, 128:256], 0.0))
        r["eb_out"][...] = column_sum(jnp.where(kind == 7 + place // n4v, picked[:, 256:512], 0.0))

    save_e = pltpu.make_async_copy(r["e_sum"], r["e_out"], r["save"].at[2])
    save_r = pltpu.make_async_copy(r["r_sum"], r["r_out"], r["save"].at[3])
    vector_start(0, vec[...])
    for t in range(34, 2 * CHUNKS + AFTER[4] - 1, 2):
        comm.advance(t)
        if t in VECTOR_STEPS:
            step = VECTOR_STEPS.index(t)
            vector_wait(step)
            if step < 3:
                vector_start(step + 1, vector_sum(step))
            else:
                pick_vectors()
        if t == 2 * 11 + AFTER[4]:
            save_e.start()
            save_r.start()
    save_e.wait()
    save_r.wait()
    save_out.wait()
    save_dx.wait()


def layer(g, patches, segments, vectors, weights, cotangent):
    A, B, R, Y = g.A, g.B, g.R, g.Y
    comm_shapes = comm_scratch(g)
    V = pl.BlockSpec(memory_space=pltpu.VMEM)
    H = pl.BlockSpec(memory_space=pl.ANY)
    inputs = dict(
        patches=(patches, H),
        cotangent=(cotangent, H),
        segments=(segments, V),
        w_joint=(weights[0], H),
        w_output=(weights[1], H),
        w_expand=(weights[2], H),
        w_reduce=(weights[3], H),
        **{name: (value, V) for name, value in vectors.items()},
    )
    outputs = dict(
        out=((ROWS, D), BF),
        dx=((ROWS, D), BF),
        j_out=((R, 3 * D), F32),
        o_out=((R, D), F32),
        e_out=((R, FF), F32),
        r_out=((4 * R, D), F32),
        v_out=((16, 128), F32),
        jb_out=((1, 128), F32),
        eb_out=((1, 256), F32),
    )
    ext = ROWS + 2 * EDGE
    scratch = dict(
        x=pltpu.VMEM((ROWS, D), BF),
        xh=pltpu.VMEM((2, EDGE, D), BF),
        dy=pltpu.VMEM((ROWS, D), BF),
        wj=pltpu.VMEM((D, 3 * D), BF),
        wo=pltpu.VMEM((D, D), BF),
        we=pltpu.VMEM((STREAM, D, TICK), BF),
        wr=pltpu.VMEM((STREAM, TICK, D), BF),
        n1T=pltpu.VMEM((D, ROWS), BF),
        qe=pltpu.VMEM((ROWS, D), BF),
        qo=pltpu.VMEM((ROWS, D), BF),
        k=pltpu.VMEM((ext, D), BF),
        v=pltpu.VMEM((ext, D), BF),
        kT=pltpu.VMEM((D, ext), BF),
        vT=pltpu.VMEM((D, ext), BF),
        bias=pltpu.VMEM((4, SPAN, EDGE), F32),
        probs=pltpu.VMEM((PAIRS, 4, SPAN, 2 * EDGE), BF),
        attT=pltpu.VMEM((D, ROWS), BF),
        mid=pltpu.VMEM((ROWS, D), F32),
        total=pltpu.VMEM((ROWS, D), F32),
        dn=pltpu.VMEM((ROWS, D), F32),
        n2=pltpu.VMEM((ROWS, D), BF),
        n2T=pltpu.VMEM((D, ROWS), BF),
        hl=pltpu.VMEM((ROWS, TICK), BF),
        actT=pltpu.VMEM((FF, ROWS), BF),
        eb=pltpu.VMEM((1, FF), F32),
        ml=pltpu.VMEM((ROWS, D), BF),
        parts=pltpu.VMEM((2, ext, 256), F32),
        jq=pltpu.VMEM((2, ROWS, 128), BF),
        sent=pltpu.VMEM((2, 2, NEAR, 256), BF),
        got=pltpu.VMEM((PAIRS, 2, NEAR, 256), BF),
        vec=pltpu.VMEM((16, D), F32),
        rv=pltpu.VMEM((2 + B, 16, D), F32),
        rvl=pltpu.VMEM((A + Y, 16, D), BF),
        G=pltpu.VMEM((SLOTS, 2, 4, B, A, R, 128), BF),
        load=pltpu.SemaphoreType.DMA((4,)),
        save=pltpu.SemaphoreType.DMA((4,)),
        e_sum=pltpu.VMEM((R, FF), F32),
        r_sum=pltpu.VMEM((4 * R, D), F32),
        stream=pltpu.SemaphoreType.DMA((2, STREAM)),
        s_edge=pltpu.SemaphoreType.DMA((2, 2)),
        s_part=pltpu.SemaphoreType.DMA((2, PAIRS, 2)),
        s_vec=pltpu.SemaphoreType.DMA((2, 2 + B + A + Y)),
        **{name + "_row": pltpu.VMEM((1, value.shape[0]), F32) for name, value in vectors.items()},
        **comm_shapes,
    )
    names = (*inputs, *outputs, *scratch)
    results = pl.pallas_call(
        functools.partial(layer_kernel, g, names),
        out_shape=tuple(jax.ShapeDtypeStruct(*shape) for shape in outputs.values()),
        in_specs=[spec for _, spec in inputs.values()],
        out_specs=[H if name in ("out", "dx", "e_out", "r_out") else V for name in outputs],
        scratch_shapes=list(scratch.values()),
        compiler_params=pltpu.CompilerParams(
            collective_id=0, has_side_effects=True, vmem_limit_bytes=64 << 20
        ),
    )(*(value for value, _ in inputs.values()))
    return hand_over(g, dict(zip(outputs, results)))


def hand_over_kernel(g, out, dx, j, o, e, w, v, jb, eb, *refs):
    outs, held, sems = refs[:14], refs[14:20], refs[20]
    R = g.R
    moves = [(out, 0), (dx, 1), (j, 4), (o, 6), (e, 10), (w, 12)]
    loads = [pltpu.make_async_copy(src, held[i], sems.at[0, i]) for i, (src, _) in enumerate(moves)]
    copies = [pltpu.make_async_copy(held[i], outs[k], sems.at[1, i]) for i, (_, k) in enumerate(moves)]
    for load in loads:
        load.start()
    for load, copy in zip(loads, copies):
        load.wait()
        copy.start()
    for row, k in ((0, 2), (1, 3), (4, 7), (5, 8), (6, 9), (11, 13)):
        outs[k][...] = v[row, :R]
    outs[5][...] = jb[0, : 2 * R]
    outs[11][...] = eb[0, : 4 * R]
    for copy in copies:
        copy.wait()


def hand_over(g, o):
    R = g.R
    V = pl.BlockSpec(memory_space=pltpu.VMEM)
    H = pl.BlockSpec(memory_space=pl.ANY)
    shapes = [
        ((ROWS, D), BF), ((ROWS, D), BF), ((R,), F32), ((R,), F32), ((R, 3 * D), F32), ((2 * R,), F32), ((R, D), F32),
        ((R,), F32), ((R,), F32), ((R,), F32), ((R, FF), F32), ((4 * R,), F32), ((4 * R, D), F32), ((R,), F32),
    ]
    names = ("out", "dx", "j_out", "o_out", "e_out", "r_out", "v_out", "jb_out", "eb_out")
    return pl.pallas_call(
        functools.partial(hand_over_kernel, g),
        out_shape=tuple(jax.ShapeDtypeStruct(*shape) for shape in shapes),
        in_specs=[H] * 6 + [V] * 3,
        out_specs=[V if len(shape) == 1 else H for shape, _ in shapes],
        scratch_shapes=[
            *(pltpu.VMEM(o[name].shape, o[name].dtype) for name in names[:6]),
            pltpu.SemaphoreType.DMA((2, 6)),
        ],
    )(*(o[name] for name in names))


def local(
    patches,
    segments,
    entry_gain,
    entry_shift,
    joint_weight,
    joint_bias,
    output_weight,
    output_bias,
    middle_gain,
    middle_shift,
    expand_weight,
    expand_bias,
    reduce_weight,
    reduce_bias,
    cotangent,
):
    g = Grid(lax.axis_size("dp"), lax.axis_size("blk"), D)
    R = g.R
    vectors = dict(
        entry_gain=entry_gain,
        entry_shift=entry_shift,
        joint_bias=joint_bias,
        output_bias=output_bias,
        middle_gain=middle_gain,
        middle_shift=middle_shift,
        expand_bias=expand_bias,
        reduce_bias=reduce_bias,
    )
    o = layer(
        g,
        patches[0],
        segments.reshape(-1, EDGE),
        vectors,
        (joint_weight, output_weight, expand_weight, reduce_weight),
        cotangent[0],
    )
    return (o[0][None], o[1][None], *o[2:])


def solution(mesh):
    return jax.shard_map(
        local,
        mesh=mesh,
        in_specs=(
            P("dp", "blk", None),
            P("dp", None),
            P(),
            P(),
            P(),
            P(),
            P(),
            P(),
            P(),
            P(),
            P(),
            P(),
            P(),
            P(),
            P("dp", "blk", None),
        ),
        out_specs=(
            P("dp", "blk", None),
            P("dp", "blk", None),
            P("dp"),
            P("dp"),
            P("dp", None),
            P("dp"),
            P("dp", None),
            P("dp"),
            P("dp"),
            P("dp"),
            P("dp", None),
            P("dp"),
            P("dp", None),
            P("dp"),
        ),
        check_vma=False,
    )
```

```python
import functools
import jax
import jax.numpy as jnp
from jax import lax
from jax.experimental import pallas as pl
from jax.experimental.pallas import tpu as pltpu
from jax.sharding import PartitionSpec as P

MESH = pl.DeviceIdType.MESH
CHUNKS = 18
AFTER = (2, 6, 10, 14, 18)
RING = 9
VECTOR_STEPS = (36, 40, 44, 48)
BF = jnp.bfloat16
F32 = jnp.float32


class Grid:
    def __init__(self, dp, blk, width):
        self.A = 4
        self.B = dp // 8
        self.Y = blk
        self.dp = dp
        self.R = width // dp
        self.kinds = 2 if blk == 2 else 1


def comm_scratch(g):
    A, B, Y, R = g.A, g.B, g.Y, g.R
    n = CHUNKS // g.kinds
    shapes = dict(
        r0=pltpu.VMEM((RING, 4, B, A, R, 128), BF),
        rx=pltpu.VMEM((n, B - 1, 4, A, R, 128), BF),
        rz=pltpu.VMEM((n, A - 1, 4, R, 128), BF),
        ryx=pltpu.VMEM((n, Y, 4, R, 128), BF),
        s_core=pltpu.SemaphoreType.DMA((2, CHUNKS)),
        s_x=pltpu.SemaphoreType.DMA((2, CHUNKS, B - 1)),
        s_z=pltpu.SemaphoreType.DMA((2, CHUNKS)),
        s_y=pltpu.SemaphoreType.DMA((2, CHUNKS, Y - 1)),
    )
    if g.kinds == 2:
        shapes.update(
            ry=pltpu.VMEM((n, 2, B, A, R, 128), BF),
            rx2=pltpu.VMEM((n, B - 1, 2, A, R, 128), BF),
            rz2=pltpu.VMEM((n, A - 1, 2, R, 128), BF),
            rag=pltpu.VMEM((n, 2, 2, R, 128), BF),
            s_ag=pltpu.SemaphoreType.DMA((2, CHUNKS)),
        )
    return shapes


class Comm:
    def __init__(self, g, G, slots, refs, emit):
        self.g, self.G, self.slots, self.emit = g, G, slots, emit
        self.__dict__.update(refs)
        dp = lax.axis_index("dp")
        self.y = lax.axis_index("blk")
        self.c = dp % 2
        self.b = (dp // 2) % g.B
        self.a = dp // (2 * g.B)

    def dev(self, a=None, b=None, c=None, y=None):
        a = self.a if a is None else a
        b = self.b if b is None else b
        c = self.c if c is None else c
        y = self.y if y is None else y
        return ((a * self.g.B + b) * 2 + c, y)

    def partners(self):
        g = self.g
        return (
            [self.dev(c=1 - self.c)]
            + [self.dev(b=(self.b + k) % g.B) for k in range(1, g.B)]
            + [self.dev(a=(self.a + k) % g.A) for k in range(1, g.A)]
            + [self.dev(y=(self.y + k) % g.Y) for k in range(1, g.Y)]
        )

    def barrier(self):
        sem = pltpu.get_barrier_semaphore()
        others = self.partners()
        for other in others:
            pl.semaphore_signal(sem, inc=1, device_id=other, device_id_type=MESH)
        pl.semaphore_wait(sem, len(others))

    def copy(self, src, dst, sems, index, device):
        return pltpu.make_async_remote_copy(
            src_ref=src,
            dst_ref=dst,
            send_sem=sems.at[(0,) + index],
            recv_sem=sems.at[(1,) + index],
            device_id=device,
            device_id_type=MESH,
        )

    def core(self, j, kind):
        copy = self.copy(
            self.G.at[j % self.slots, 1 - self.c], self.r0.at[j % RING], self.s_core, (j,), self.dev(c=1 - self.c)
        )
        return [copy], [copy]

    def along_b(self, j, kind):
        g, i = self.g, j // self.g.kinds
        landing = self.rx2 if kind else self.rx
        cols = pl.ds(2 * self.y, 2) if kind else pl.ds(0, 4)
        copies = []
        for k in range(1, g.B):
            other = (self.b + k) % g.B
            source = self.G.at[j % self.slots, self.c, cols, other]
            copies.append(self.copy(source, landing.at[i, k - 1], self.s_x, (j, k - 1), self.dev(b=other)))
        return copies, copies

    def along_a(self, j, kind):
        g, i = self.g, j // self.g.kinds
        landing = self.rz2 if kind else self.rz
        cols = pl.ds(2 * self.y, 2) if kind else pl.ds(0, 4)
        copies = []
        for k in range(1, g.A):
            other = (self.a + k) % g.A
            source = self.G.at[j % self.slots, self.c, cols, self.b, other]
            copies.append(self.copy(source, landing.at[i, k - 1], self.s_z, (j,), self.dev(a=other)))
        return copies, [self.copy(landing.at[i], landing.at[i], self.s_z, (j,), self.dev(a=(self.a + 1) % g.A))]

    def along_blk(self, j, kind):
        g, i = self.g, j // self.g.kinds
        if kind:
            source = self.G.at[j % self.slots, self.c, pl.ds(2 * (1 - self.y), 2)]
            copies = [self.copy(source, self.ry.at[i], self.s_y, (j, 0), self.dev(y=1 - self.y))]
            return copies, copies
        mine = self.ryx.at[i, self.y]
        copies = [
            self.copy(mine, mine, self.s_y, (j, k - 1), self.dev(y=(self.y + k) % g.Y)) for k in range(1, g.Y)
        ]
        return copies, copies

    def share(self, j, kind):
        mine = self.rag.at[j // 2, self.y]
        copies = [self.copy(mine, mine, self.s_ag, (j,), self.dev(y=1 - self.y))]
        return copies, copies

    def add(self, mine, parts):
        if len(parts) == 1:
            mine[...] = mine[...] + parts[0]
        else:
            mine[...] = self.summed(mine, parts)

    def summed(self, mine, parts):
        total = mine[...].astype(F32)
        for part in parts:
            total = total + part.astype(F32)
        return total.astype(BF)

    def after_core(self, j, kind):
        self.add(self.G.at[j % self.slots, self.c], [self.r0[j % RING]])

    def after_b(self, j, kind):
        g, i = self.g, j // self.g.kinds
        landing = self.rx2 if kind else self.rx
        cols = pl.ds(2 * self.y, 2) if kind else pl.ds(0, 4)
        self.add(self.G.at[j % self.slots, self.c, cols, self.b], [landing[i, k] for k in range(g.B - 1)])

    def after_a(self, j, kind):
        g, i = self.g, j // self.g.kinds
        landing = self.rz2 if kind else self.rz
        cols = pl.ds(2 * self.y, 2) if kind else pl.ds(0, 4)
        total = self.summed(
            self.G.at[j % self.slots, self.c, cols, self.b, self.a], [landing[i, k] for k in range(g.A - 1)]
        )
        if kind:
            self.rag[i, self.y] = total
        else:
            self.ryx[i, self.y] = total

    def after_blk(self, j, kind):
        g, i = self.g, j // self.g.kinds
        if kind:
            self.add(self.G.at[j % self.slots, self.c, pl.ds(2 * self.y, 2)], [self.ry[i]])
            return
        total = self.ryx[i, 0].astype(F32)
        for k in range(1, g.Y):
            total = total + self.ryx[i, k].astype(F32)
        self.emit(j, [total[col] for col in range(4)])

    def after_share(self, j, kind):
        i = j // 2
        self.emit(j, [self.rag[i, col // 2, col % 2].astype(F32) for col in range(4)])

    def plan(self, kind):
        core = (self.core, self.after_core)
        b = (self.along_b, self.after_b)
        a = (self.along_a, self.after_a)
        blk = (self.along_blk, self.after_blk)
        share = (self.share, self.after_share)
        return (core, blk, b, a, share) if kind else (core, b, a, blk)

    def start(self, j):
        self.core(j, 0)[0][0].start()

    def finish(self, stage, j):
        for kind in range(self.g.kinds):
            plan = self.plan(kind)
            if stage >= len(plan):
                continue

            def go(kind=kind, plan=plan):
                for copy in plan[stage][0](j, kind)[1]:
                    copy.wait()
                plan[stage][1](j, kind)
                if stage + 1 < len(plan):
                    for copy in plan[stage + 1][0](j, kind)[0]:
                        copy.start()

            if self.g.kinds == 1:
                go()
            elif isinstance(j, int):
                if (j + (j >= CHUNKS - 2)) % 2 == kind:
                    go()
            else:
                pl.when(jnp.where(j >= CHUNKS - 2, j + 1, j) % 2 == kind)(go)

    def advance(self, t):
        for stage in range(5):
            twice = t - AFTER[stage]
            if twice % 2 == 0 and 0 <= twice < 2 * CHUNKS:
                self.finish(stage, twice // 2)

    def advance_two(self, t, odd):
        for stage in range(5):
            if (odd - AFTER[stage]) % 2 == 0:
                j = t + (odd - AFTER[stage]) // 2

                @pl.when((j >= 0) & (j < CHUNKS))
                def _(stage=stage, j=j):
                    self.finish(stage, j)


def emit_to(g, j_ref, o_ref, e_ref, r_ref):
    R = g.R

    def emit(j, values):
        @pl.when(j < 6)
        def _():
            for col in range(4):
                e_ref[:, pl.ds(pl.multiple_of(j * 512 + col * 128, 128), 128)] = values[col]

        @pl.when((j >= 6) & (j < 12))
        def _():
            for k in range(4):
                r_ref[k * R : (k + 1) * R, pl.ds(pl.multiple_of((j - 6) * 128, 128), 128)] = values[k]

        @pl.when(j >= 12)
        def _():
            at = pl.multiple_of((j - 12) * 128, 128)
            for k in range(3):
                j_ref[:, pl.ds(pl.multiple_of(k * 768 + at, 128), 128)] = values[k]
            o_ref[:, pl.ds(at, 128)] = values[3]

    return emit


HEADS = 12
VECTORS = (
    "entry_gain", "entry_shift", "joint_bias", "output_bias",
    "middle_gain", "middle_shift", "expand_bias", "reduce_bias",
)
HD = 64
D = 768
FF = 3072
ROWS = 512
EDGE = 128
SPAN = 3 * EDGE
PAIRS = HEADS // 2
NEAR = 112
SLOTS = 12
STREAM = 2
TICK = 512
TICKS = FF // TICK


def nn(left, right):
    return jnp.dot(left, right, preferred_element_type=F32)


def nt(left, right):
    return lax.dot_general(left, right, (((1,), (1,)), ((), ())), preferred_element_type=F32)


def stats(values):
    average = jnp.mean(values, axis=-1, keepdims=True)
    centred = values - average
    spread = jnp.mean(centred * centred, axis=-1, keepdims=True)
    inverse = lax.rsqrt(spread + 1e-06)
    return centred * inverse, inverse


def normal_parts(hidden):
    half = hidden * (0.5**0.5)
    size = jnp.abs(half)
    ratio = 1.0 / (1.0 + 0.3275911 * size)
    bell = jnp.exp(-half * half)
    tail = ((((1.061405429 * ratio - 1.453152027) * ratio + 1.421413741) * ratio - 0.284496736) * ratio + 0.254829592) * ratio
    tail = 0.5 * tail * bell
    share = jnp.where(hidden >= 0, 1.0 - tail, tail)
    return share, hidden * bell * 0.3989422804014327


def column_sum(values):
    return jnp.sum(values, axis=0, keepdims=True)


def layer_kernel(g, names, *refs):
    r = dict(zip(names, refs))
    A, B, R, Y = g.A, g.B, g.R, g.Y
    (patches, cotangent, segments, w_joint, w_output, w_expand, w_reduce) = (
        r[n] for n in ("patches", "cotangent", "segments", "w_joint", "w_output", "w_expand", "w_reduce")
    )
    G, vec = r["G"], r["vec"]
    for name in VECTORS:
        r[name + "_row"][...] = r[name][...].reshape(1, -1)
        r[name] = r[name + "_row"]
    r["oe"], r["oo"] = r["vT"], r["n2"]
    out_rows, dx_rows = r["k"].at[pl.ds(0, ROWS)], r["ml"]
    x, xh, dy = r["x"], r["xh"], r["dy"]
    comm = Comm(g, G, SLOTS, r, emit_to(g, r["j_out"], r["o_out"], r["e_sum"], r["r_sum"]))
    y = comm.y
    has_left, has_right = y > 0, y < Y - 1

    def load(src, dst, k):
        return pltpu.make_async_copy(src, dst, r["load"].at[k])

    load_x = load(patches, x, 0)
    load_wj = load(w_joint, r["wj"], 1)
    load_wo = load(w_output, r["wo"], 2)
    load_dy = load(cotangent, dy, 3)

    def ffn_loads(i):
        s = i % STREAM
        at = pl.ds(pl.multiple_of(i * TICK, TICK), TICK)
        return (
            pltpu.make_async_copy(w_expand.at[:, at], r["we"].at[s], r["stream"].at[0, s]),
            pltpu.make_async_copy(w_reduce.at[at], r["wr"].at[s], r["stream"].at[1, s]),
        )

    load_x.start()
    load_wj.start()
    comm.barrier()

    def edge(k, side, src, dst, sems):
        other = comm.dev(y=(y + Y - 1) % Y) if side == 0 else comm.dev(y=(y + 1) % Y)
        return pltpu.make_async_remote_copy(
            src_ref=src, dst_ref=dst, send_sem=sems.at[(0,) + k + (side,)], recv_sem=sems.at[(1,) + k + (1 - side,)],
            device_id=other, device_id_type=MESH,
        )

    def x_edges():
        return (
            edge((), 0, patches.at[pl.ds(0, NEAR)], xh.at[1, pl.ds(0, NEAR)], r["s_edge"]),
            edge((), 1, patches.at[pl.ds(ROWS - NEAR, NEAR)], xh.at[0, pl.ds(EDGE - NEAR, NEAR)], r["s_edge"]),
        )

    to_left, to_right = x_edges()

    @pl.when(has_left)
    def _():
        to_left.start()

    @pl.when(has_right)
    def _():
        to_right.start()

    xh[0, 0 : EDGE - NEAR, :] = jnp.zeros((EDGE - NEAR, D), BF)
    xh[1, NEAR:EDGE, :] = jnp.zeros((EDGE - NEAR, D), BF)

    first_block = y * (ROWS // EDGE)
    count = segments.shape[0]
    columns = []
    for k in range(6):
        index = first_block + k - 1
        inside = (index >= 0) & (index < count)
        row = segments[pl.ds(jnp.clip(index, 0, count - 1), 1), :]
        row = jnp.where(inside, row, -1)
        columns.append(row)
    for b in range(4):
        for k in range(3):
            keys = jnp.broadcast_to(columns[b + k].astype(F32), (EDGE, EDGE)).T
            own = columns[b + 1].astype(F32)
            r["bias"][b, k * EDGE : (k + 1) * EDGE, :] = jnp.where(keys == own, 0.0, -1e30)

    vec[...] = jnp.zeros_like(vec)
    entry_gain, entry_shift = r["entry_gain"][...], r["entry_shift"][...]
    lanes = lax.broadcasted_iota(jnp.int32, (1, D), 1) % 128
    even = lanes < HD

    def project(rows, at, own, row_at):
        count = rows.shape[0]
        normal, _ = stats(rows.astype(F32))
        low = (normal * entry_gain + entry_shift).astype(BF)
        wj = r["wj"]
        key_rows = nn(low, wj[:, D : 2 * D]).astype(BF)
        r["k"][pl.ds(at, count), :] = key_rows
        value_rows = (nn(low, wj[:, 2 * D :]) + r["joint_bias"][:, D:]).astype(BF)
        r["v"][pl.ds(at, count), :] = value_rows
        r["vT"][:, pl.ds(at, count)] = value_rows.T
        if own:
            r["ml"][pl.ds(row_at, count), :] = low
            queries = (nn(low, wj[:, :D]) + r["joint_bias"][:, :D]).astype(BF) * BF(HD**-0.5)
            r["qe"][pl.ds(row_at, count), :] = jnp.where(even, queries, BF(0))
            r["qo"][pl.ds(row_at, count), :] = jnp.where(even, BF(0), queries)

    load_x.wait()
    load_wj.wait()
    load_wo.start()
    load_dy.start()
    for i in range(STREAM):
        for copy in ffn_loads(i):
            copy.start()

    def own_rows(i, _):
        at = pl.multiple_of(i * 256, 256)
        project(x[pl.ds(at, 256), :], pl.multiple_of(at + EDGE, EDGE), True, at)
        return 0

    lax.fori_loop(0, 2, own_rows, 0)

    @pl.when(has_left)
    def _():
        to_left.wait_send()
        to_right.wait_recv()

    @pl.when(has_right)
    def _():
        to_right.wait_send()
        to_left.wait_recv()

    def edge_rows(i, _):
        at = pl.multiple_of(i * (ROWS + EDGE), EDGE)
        present = jnp.where(i == 0, y, Y - 1 - y) > 0

        @pl.when(present)
        def _():
            project(xh[i], at, False, 0)

        @pl.when(jnp.logical_not(present))
        def _():
            r["k"][pl.ds(at, EDGE), :] = jnp.zeros((EDGE, D), BF)
            r["v"][pl.ds(at, EDGE), :] = jnp.zeros((EDGE, D), BF)
            r["vT"][:, pl.ds(at, EDGE)] = jnp.zeros((D, EDGE), BF)

        return 0

    lax.fori_loop(0, 2, edge_rows, 0)

    top = lax.broadcasted_iota(jnp.int32, (EDGE, 1), 0) < HD

    def scores_of(p, b):
        at = pl.ds(pl.multiple_of(p * 128, 128), 128)
        keys, own = pl.ds(b * EDGE, SPAN), pl.ds(b * EDGE, EDGE)
        both = jnp.concatenate([r["qe"][own, at], r["qo"][own, at]], axis=0)
        return nt(r["k"][keys, at], both)

    def probs_of(b, scores):
        bias = r["bias"][b]
        scores = scores + jnp.concatenate([bias, bias], axis=1)
        powers = jnp.exp(scores - jnp.max(scores, axis=0, keepdims=True))
        return (powers * (1.0 / column_sum(powers))).astype(BF)

    def mix(p, b, probs):
        at = pl.ds(pl.multiple_of(p * 128, 128), 128)
        keys, own = pl.ds(b * EDGE, SPAN), pl.ds(b * EDGE, EDGE)
        r["probs"][p, b] = probs
        mixed = nn(r["vT"][at, keys], probs)
        r["attT"][at, own] = jnp.where(top, mixed[:, :128], mixed[:, 128:]).astype(BF)

    def attend(i, _):
        blocks = [(2 * i + pair, b) for pair in range(2) for b in range(4)]
        scores = scores_of(*blocks[0])
        before = None
        for k, (p, b) in enumerate(blocks):
            following = scores_of(*blocks[k + 1]) if k + 1 < len(blocks) else None
            probs = probs_of(b, scores)
            if k > 0:
                mix(*blocks[k - 1], before)
            before, scores = probs, following
        mix(*blocks[-1], before)
        return 0

    lax.fori_loop(0, PAIRS // 2, attend, 0)

    load_wo.wait()
    mid, total, n2, n2T = r["mid"], r["total"], r["n2"], r["n2T"]
    middle_gain, middle_shift = r["middle_gain"][...], r["middle_shift"][...]

    halves = [pl.ds(i * 256, 256) for i in range(2)]
    middles = [
        x[at, :].astype(F32) + nn(r["attT"][:, at].T, r["wo"][...]) + r["output_bias"][...] for at in halves
    ]
    for at, middle in zip(halves, middles):
        mid[at, :] = middle
        total[at, :] = middle + r["reduce_bias"][...]
        normal, _ = stats(middle)
        low = (normal * middle_gain + middle_shift).astype(BF)
        n2[at, :] = low
        n2T[:, at] = low.T
        r["dn"][at, :] = jnp.zeros((256, D), F32)
    load_dy.wait()

    def feed_forward(i, _):
        s = i % STREAM
        for copy in ffn_loads(i):
            copy.wait()
        we, wr = r["we"].at[s], r["wr"].at[s]
        at = pl.ds(pl.multiple_of(i * TICK, TICK), TICK)
        bias = r["expand_bias"][:, at]
        bias_sum = jnp.zeros((1, TICK), F32)
        rows = [pl.ds(half * 256, 256) for half in range(2)]
        hidden = [nn(n2[part, :], we[...]) + bias for part in rows]
        back = [nt(dy[part, :], wr[...]) for part in rows]
        for half, part in enumerate(rows):
            share, slope = normal_parts(hidden[half])
            active = (hidden[half] * share).astype(BF)
            hidden_gradient = back[half] * (share + slope)
            bias_sum = bias_sum + column_sum(hidden_gradient)
            low = hidden_gradient.astype(BF)
            r["hl"][part, :] = low
            r["actT"][at, part] = active.T
            total[part, :] += nn(active, wr[...])
            r["dn"][part, :] += nt(low, we[...])
        r["eb"][:, at] = bias_sum
        for part in range(2):
            block = nn(n2T[part * 384 : (part + 1) * 384, :], r["hl"][...]).astype(BF)
            store_rows(block, i, part * 2, 2)
        comm.start(i)

        @pl.when(i + STREAM < TICKS)
        def _():
            for copy in ffn_loads(i + STREAM):
                copy.start()

        comm.advance_two(i, 0)
        return 0

    def store_rows(block, chunk, a0, na):
        slot = chunk % SLOTS
        for a in range(na):
            for b in range(B):
                for c in range(2):
                    row = ((a * B + b) * 2 + c) * R
                    for col in range(block.shape[1] // 128):
                        G[slot, c, col, b, a0 + a] = block[row : row + R, col * 128 : (col + 1) * 128]

    lax.fori_loop(0, TICKS, feed_forward, 0)

    def turn(i, _):
        at = pl.ds(pl.multiple_of(i * 256, 256), 256)
        r["kT"][:, at] = r["k"][at, :].T

        @pl.when(i < 2)
        def _():
            r["n1T"][:, at] = r["ml"][at, :].T

        return 0

    lax.fori_loop(0, 3, turn, 0)

    def reduce_gradient(p, _):
        at = pl.ds(pl.multiple_of(p * 256, 256), 256)
        chunk = 6 + 2 * p

        def part(a, _):
            block = nn(r["actT"][pl.ds(pl.multiple_of(a * D, D), D), :], dy[:, at]).astype(BF)
            for h in range(2):
                slot = (chunk + h) % SLOTS
                for b in range(B):
                    for c in range(2):
                        for k in range(4):
                            row = ((b * 2 + c) * 4 + k) * R
                            G[slot, c, k, b, a] = block[row : row + R, h * 128 : (h + 1) * 128]
            return 0

        lax.fori_loop(0, A, part, 0)
        comm.start(chunk)
        comm.start(chunk + 1)
        comm.advance_two(6 + p, 0)
        return 0

    lax.fori_loop(0, 3, reduce_gradient, 0)

    def middle_back(i, _):
        at = pl.ds(pl.multiple_of(i * 256, 256), 256)
        out_rows[at, :] = total[at, :].astype(BF)
        error = r["dn"][at, :]
        normal, inverse = stats(mid[at, :])
        scaled = error * middle_gain
        part = inverse * (
            scaled
            - jnp.mean(scaled, axis=-1, keepdims=True)
            - normal * jnp.mean(scaled * normal, axis=-1, keepdims=True)
        )
        incoming = dy[at, :].astype(F32)
        gradient = incoming + part
        vec[5:6, :] += column_sum(error * normal)
        vec[6:7, :] += column_sum(error)
        vec[4:5, :] += column_sum(gradient)
        vec[11:12, :] += column_sum(incoming)
        mid[at, :] = gradient
        low = gradient.astype(BF)
        r["ml"][at, :] = low
        back = nt(low, r["wo"][...]).astype(BF)
        r["oe"][at, :] = jnp.where(even, back, BF(0))
        r["oo"][at, :] = jnp.where(even, BF(0), back)
        total[at, :] = jnp.zeros((256, D), F32)
        return 0

    lax.fori_loop(0, 2, middle_back, 0)
    save_out = pltpu.make_async_copy(out_rows, r["out"], r["save"].at[0])
    save_out.start()
    for k in range(4):
        vec[7 + k : 8 + k, :] = r["eb"][:, k * D : (k + 1) * D]
    comm.advance(17)
    comm.advance(18)

    place = lax.axis_index("dp")
    n2v, n4v = g.dp // 2, g.dp // 4
    lane = lax.broadcasted_iota(jnp.int32, (1, ROWS), 1)
    want = jnp.where(
        lane < 128,
        lane + place * R,
        jnp.where(lane < 256, lane - 128 + (place % n2v) * (2 * R), lane - 256 + (place % n4v) * (4 * R)),
    )
    spot = lax.broadcasted_iota(jnp.int32, (D, ROWS), 0)
    r["n2T"][...] = jnp.where(spot == want, 1.0, 0.0).astype(BF)

    parts, jq, sent, got, s_part = r["parts"], r["jq"], r["sent"], r["got"], r["s_part"]

    def part_copies(p):
        return (
            edge((p,), 0, sent.at[p % 2, 0], got.at[p, 1], s_part),
            edge((p,), 1, sent.at[p % 2, 1], got.at[p, 0], s_part),
        )

    def attend_back(p):
        at = pl.ds(pl.multiple_of(p * 128, 128), 128)
        slot = p % 2
        own_sum = jnp.zeros((1, 128), F32)
        parts[slot] = jnp.zeros((ROWS + 2 * EDGE, 256), F32)

        def errors_of(b):
            own = pl.ds(b * EDGE, EDGE)
            return jnp.concatenate([r["oe"][own, at], r["oo"][own, at]], axis=0)

        def shares_of(b):
            return nt(r["v"][pl.ds(b * EDGE, SPAN), at], errors_of(b))

        def score_gradient_of(b, shares):
            wide = r["probs"][p, b].astype(F32)
            product = wide * shares
            return (product - wide * column_sum(product)).astype(BF)

        def spread(b, low):
            keys, own = pl.ds(b * EDGE, SPAN), pl.ds(b * EDGE, EDGE)
            queries = jnp.concatenate([r["qe"][own, at], r["qo"][own, at]], axis=0)
            parts[slot, keys, 0:128] += nn(low, queries)
            parts[slot, keys, 128:256] += nn(r["probs"][p, b], errors_of(b))
            turned = nn(r["kT"][at, keys], low)
            mine = (jnp.where(top, turned[:, :128], turned[:, 128:]) * HD**-0.5).T
            jq[slot, own, :] = mine.astype(BF)
            return column_sum(mine)

        to_left, to_right = part_copies(p)

        def send_edges():
            @pl.when(has_left)
            def _():
                sent[slot, 0] = parts[slot, EDGE - NEAR : EDGE, :].astype(BF)
                to_left.start()

            @pl.when(has_right)
            def _():
                sent[slot, 1] = parts[slot, ROWS + EDGE : ROWS + EDGE + NEAR, :].astype(BF)
                to_right.start()

        order = (0, 3, 1, 2)
        shares = shares_of(order[0])
        before = None
        for step, b in enumerate(order):
            following = shares_of(order[step + 1]) if step < 3 else None
            low = score_gradient_of(b, shares)
            if step > 0:
                own_sum = own_sum + spread(order[step - 1], before)
            if step == 2:
                send_edges()
            before, shares = low, following
        own_sum = own_sum + spread(order[3], before)
        vec[2:3, at] = own_sum

    def joint_gradient(p):
        at = pl.ds(pl.multiple_of(p * 128, 128), 128)
        slot = p % 2
        to_left, to_right = part_copies(p)

        @pl.when(has_left)
        def _():
            to_left.wait_send()
            to_right.wait_recv()
            parts[slot, EDGE : EDGE + NEAR, :] += got[p, 0].astype(F32)

        @pl.when(has_right)
        def _():
            to_right.wait_send()
            to_left.wait_recv()
            parts[slot, ROWS + EDGE - NEAR : ROWS + EDGE, :] += got[p, 1].astype(F32)

        sums = parts[slot, EDGE : ROWS + EDGE, :]
        vec[3:4, at] = column_sum(sums[:, 128:])
        low = jnp.concatenate([jq[slot], sums.astype(BF)], axis=1)
        wj = r["wj"]
        weights = jnp.concatenate([wj[:, pl.ds(pl.multiple_of(k * D + p * 128, 128), 128)] for k in range(3)], axis=1)
        total[...] += nt(low, weights)
        low_out = r["ml"][:, at]
        for part in range(2):
            rows = pl.ds(part * 384, 384)
            block = nn(r["n1T"][rows, :], low).astype(BF)
            block_out = nn(r["attT"][rows, :], low_out).astype(BF)
            store_rows(jnp.concatenate([block, block_out], axis=1), 12 + p, part * 2, 2)
        comm.start(12 + p)

    def pair_step(i, _):
        @pl.when(i < PAIRS)
        def _():
            attend_back(i)

        @pl.when(i > 0)
        def _():
            joint_gradient(i - 1)

        comm.advance_two(10 + i, 0)
        return 0

    lax.fori_loop(0, PAIRS + 1, pair_step, 0)

    def entry_back(i, _):
        at = pl.ds(pl.multiple_of(i * 256, 256), 256)
        error = total[at, :]
        normal, inverse = stats(x[at, :].astype(F32))
        scaled = error * entry_gain
        part = inverse * (
            scaled
            - jnp.mean(scaled, axis=-1, keepdims=True)
            - normal * jnp.mean(scaled * normal, axis=-1, keepdims=True)
        )
        vec[0:1, :] += column_sum(error * normal)
        vec[1:2, :] += column_sum(error)
        dx_rows[at, :] = (mid[at, :] + part).astype(BF)
        return 0

    lax.fori_loop(0, 2, entry_back, 0)
    save_dx = pltpu.make_async_copy(dx_rows, r["dx"], r["save"].at[1])
    save_dx.start()

    rv, s_vec = r["rv"], r["s_vec"]

    def vector_copies(step):
        groups = (
            [comm.dev(c=1 - comm.c)],
            [comm.dev(b=(comm.b + k) % B) for k in range(1, B)],
            [comm.dev(a=(comm.a + k) % A) for k in range(1, A)],
            [comm.dev(y=(comm.y + k) % Y) for k in range(1, Y)],
        )
        ids = (comm.c, comm.b, comm.a, comm.y)
        base = (0, 2, 0, A)[step]
        held = rv if step < 2 else r["rvl"]
        here = held.at[base + ids[step]]
        return here, [
            comm.copy(here, here, s_vec, ((0, 2, 2 + B, 2 + B + A)[step] + k,), other) for k, other in enumerate(groups[step])
        ]

    def vector_sum(step):
        base, size = ((0, 2), (2, B), (0, A), (A, Y))[step]
        held = rv if step < 2 else r["rvl"]
        value = held[base].astype(F32)
        for k in range(1, size):
            value = value + held[base + k].astype(F32)
        return value

    def vector_start(step, value):
        here, copies = vector_copies(step)
        here[...] = value.astype(here.dtype)
        for copy in copies:
            copy.start()

    def vector_wait(step):
        for copy in vector_copies(step)[1]:
            copy.wait()

    def pick_vectors():
        summed = vector_sum(3)
        high = summed.astype(BF)
        rest = (summed - high.astype(F32)).astype(BF)
        picked = nn(high, r["n2T"][...]) + nn(rest, r["n2T"][...])
        kind = lax.broadcasted_iota(jnp.int32, (16, 1), 0)
        r["v_out"][...] = picked[:, 0:128]
        r["jb_out"][...] = column_sum(jnp.where(kind == 2 + place // n2v, picked[:, 128:256], 0.0))
        r["eb_out"][...] = column_sum(jnp.where(kind == 7 + place // n4v, picked[:, 256:512], 0.0))

    save_e = pltpu.make_async_copy(r["e_sum"], r["e_out"], r["save"].at[2])
    save_r = pltpu.make_async_copy(r["r_sum"], r["r_out"], r["save"].at[3])
    vector_start(0, vec[...])
    for t in range(34, 2 * CHUNKS + AFTER[4] - 1, 2):
        comm.advance(t)
        if t in VECTOR_STEPS:
            step = VECTOR_STEPS.index(t)
            vector_wait(step)
            if step < 3:
                vector_start(step + 1, vector_sum(step))
            else:
                pick_vectors()
        if t == 2 * 11 + AFTER[4]:
            save_e.start()
            save_r.start()
    save_e.wait()
    save_r.wait()
    save_out.wait()
    save_dx.wait()


def layer(g, patches, segments, vectors, weights, cotangent):
    A, B, R, Y = g.A, g.B, g.R, g.Y
    comm_shapes = comm_scratch(g)
    V = pl.BlockSpec(memory_space=pltpu.VMEM)
    H = pl.BlockSpec(memory_space=pl.ANY)
    inputs = dict(
        patches=(patches, H),
        cotangent=(cotangent, H),
        segments=(segments, V),
        w_joint=(weights[0], H),
        w_output=(weights[1], H),
        w_expand=(weights[2], H),
        w_reduce=(weights[3], H),
        **{name: (value, V) for name, value in vectors.items()},
    )
    outputs = dict(
        out=((ROWS, D), BF),
        dx=((ROWS, D), BF),
        j_out=((R, 3 * D), F32),
        o_out=((R, D), F32),
        e_out=((R, FF), F32),
        r_out=((4 * R, D), F32),
        v_out=((16, 128), F32),
        jb_out=((1, 128), F32),
        eb_out=((1, 256), F32),
    )
    ext = ROWS + 2 * EDGE
    scratch = dict(
        x=pltpu.VMEM((ROWS, D), BF),
        xh=pltpu.VMEM((2, EDGE, D), BF),
        dy=pltpu.VMEM((ROWS, D), BF),
        wj=pltpu.VMEM((D, 3 * D), BF),
        wo=pltpu.VMEM((D, D), BF),
        we=pltpu.VMEM((STREAM, D, TICK), BF),
        wr=pltpu.VMEM((STREAM, TICK, D), BF),
        n1T=pltpu.VMEM((D, ROWS), BF),
        qe=pltpu.VMEM((ROWS, D), BF),
        qo=pltpu.VMEM((ROWS, D), BF),
        k=pltpu.VMEM((ext, D), BF),
        v=pltpu.VMEM((ext, D), BF),
        kT=pltpu.VMEM((D, ext), BF),
        vT=pltpu.VMEM((D, ext), BF),
        bias=pltpu.VMEM((4, SPAN, EDGE), F32),
        probs=pltpu.VMEM((PAIRS, 4, SPAN, 2 * EDGE), BF),
        attT=pltpu.VMEM((D, ROWS), BF),
        mid=pltpu.VMEM((ROWS, D), F32),
        total=pltpu.VMEM((ROWS, D), F32),
        dn=pltpu.VMEM((ROWS, D), F32),
        n2=pltpu.VMEM((ROWS, D), BF),
        n2T=pltpu.VMEM((D, ROWS), BF),
        hl=pltpu.VMEM((ROWS, TICK), BF),
        actT=pltpu.VMEM((FF, ROWS), BF),
        eb=pltpu.VMEM((1, FF), F32),
        ml=pltpu.VMEM((ROWS, D), BF),
        parts=pltpu.VMEM((2, ext, 256), F32),
        jq=pltpu.VMEM((2, ROWS, 128), BF),
        sent=pltpu.VMEM((2, 2, NEAR, 256), BF),
        got=pltpu.VMEM((PAIRS, 2, NEAR, 256), BF),
        vec=pltpu.VMEM((16, D), F32),
        rv=pltpu.VMEM((2 + B, 16, D), F32),
        rvl=pltpu.VMEM((A + Y, 16, D), BF),
        G=pltpu.VMEM((SLOTS, 2, 4, B, A, R, 128), BF),
        load=pltpu.SemaphoreType.DMA((4,)),
        save=pltpu.SemaphoreType.DMA((4,)),
        e_sum=pltpu.VMEM((R, FF), F32),
        r_sum=pltpu.VMEM((4 * R, D), F32),
        stream=pltpu.SemaphoreType.DMA((2, STREAM)),
        s_edge=pltpu.SemaphoreType.DMA((2, 2)),
        s_part=pltpu.SemaphoreType.DMA((2, PAIRS, 2)),
        s_vec=pltpu.SemaphoreType.DMA((2, 2 + B + A + Y)),
        **{name + "_row": pltpu.VMEM((1, value.shape[0]), F32) for name, value in vectors.items()},
        **comm_shapes,
    )
    names = (*inputs, *outputs, *scratch)
    results = pl.pallas_call(
        functools.partial(layer_kernel, g, names),
        out_shape=tuple(jax.ShapeDtypeStruct(*shape) for shape in outputs.values()),
        in_specs=[spec for _, spec in inputs.values()],
        out_specs=[H if name in ("out", "dx", "e_out", "r_out") else V for name in outputs],
        scratch_shapes=list(scratch.values()),
        compiler_params=pltpu.CompilerParams(
            collective_id=0, has_side_effects=True, vmem_limit_bytes=64 << 20
        ),
    )(*(value for value, _ in inputs.values()))
    return hand_over(g, dict(zip(outputs, results)))


def hand_over_kernel(g, out, dx, j, o, e, w, v, jb, eb, *refs):
    outs, held, sems = refs[:14], refs[14:20], refs[20]
    R = g.R
    moves = [(out, 0), (dx, 1), (j, 4), (o, 6), (e, 10), (w, 12)]
    loads = [pltpu.make_async_copy(src, held[i], sems.at[0, i]) for i, (src, _) in enumerate(moves)]
    copies = [pltpu.make_async_copy(held[i], outs[k], sems.at[1, i]) for i, (_, k) in enumerate(moves)]
    for load in loads:
        load.start()
    for load, copy in zip(loads, copies):
        load.wait()
        copy.start()
    for row, k in ((0, 2), (1, 3), (4, 7), (5, 8), (6, 9), (11, 13)):
        outs[k][...] = v[row, :R]
    outs[5][...] = jb[0, : 2 * R]
    outs[11][...] = eb[0, : 4 * R]
    for copy in copies:
        copy.wait()


def hand_over(g, o):
    R = g.R
    V = pl.BlockSpec(memory_space=pltpu.VMEM)
    H = pl.BlockSpec(memory_space=pl.ANY)
    shapes = [
        ((ROWS, D), BF), ((ROWS, D), BF), ((R,), F32), ((R,), F32), ((R, 3 * D), F32), ((2 * R,), F32), ((R, D), F32),
        ((R,), F32), ((R,), F32), ((R,), F32), ((R, FF), F32), ((4 * R,), F32), ((4 * R, D), F32), ((R,), F32),
    ]
    names = ("out", "dx", "j_out", "o_out", "e_out", "r_out", "v_out", "jb_out", "eb_out")
    return pl.pallas_call(
        functools.partial(hand_over_kernel, g),
        out_shape=tuple(jax.ShapeDtypeStruct(*shape) for shape in shapes),
        in_specs=[H] * 6 + [V] * 3,
        out_specs=[V if len(shape) == 1 else H for shape, _ in shapes],
        scratch_shapes=[
            *(pltpu.VMEM(o[name].shape, o[name].dtype) for name in names[:6]),
            pltpu.SemaphoreType.DMA((2, 6)),
        ],
    )(*(o[name] for name in names))


def local(
    patches,
    segments,
    entry_gain,
    entry_shift,
    joint_weight,
    joint_bias,
    output_weight,
    output_bias,
    middle_gain,
    middle_shift,
    expand_weight,
    expand_bias,
    reduce_weight,
    reduce_bias,
    cotangent,
):
    g = Grid(lax.axis_size("dp"), lax.axis_size("blk"), D)
    R = g.R
    vectors = dict(
        entry_gain=entry_gain,
        entry_shift=entry_shift,
        joint_bias=joint_bias,
        output_bias=output_bias,
        middle_gain=middle_gain,
        middle_shift=middle_shift,
        expand_bias=expand_bias,
        reduce_bias=reduce_bias,
    )
    o = layer(
        g,
        patches[0],
        segments.reshape(-1, EDGE),
        vectors,
        (joint_weight, output_weight, expand_weight, reduce_weight),
        cotangent[0],
    )
    return (o[0][None], o[1][None], *o[2:])


def solution(mesh):
    return jax.shard_map(
        local,
        mesh=mesh,
        in_specs=(
            P("dp", "blk", None),
            P("dp", None),
            P(),
            P(),
            P(),
            P(),
            P(),
            P(),
            P(),
            P(),
            P(),
            P(),
            P(),
            P(),
            P("dp", "blk", None),
        ),
        out_specs=(
            P("dp", "blk", None),
            P("dp", "blk", None),
            P("dp"),
            P("dp"),
            P("dp", None),
            P("dp"),
            P("dp", None),
            P("dp"),
            P("dp"),
            P("dp"),
            P("dp", None),
            P("dp"),
            P("dp", None),
            P("dp"),
        ),
        check_vma=False,
    )
```

```python
import functools
import jax
import jax.numpy as jnp
from jax import lax
from jax.experimental import pallas as pl
from jax.experimental.pallas import tpu as pltpu
from jax.sharding import PartitionSpec as P

MESH = pl.DeviceIdType.MESH
CHUNKS = 18
AFTER = (2, 6, 10, 14, 18)
RING = 9
VECTOR_STEPS = (36, 40, 44, 48)
BF = jnp.bfloat16
F32 = jnp.float32


class Grid:
    def __init__(self, dp, blk, width):
        self.A = 4
        self.B = dp // 8
        self.Y = blk
        self.dp = dp
        self.R = width // dp
        self.kinds = 2 if blk == 2 else 1


def comm_scratch(g):
    A, B, Y, R = g.A, g.B, g.Y, g.R
    n = CHUNKS // g.kinds
    shapes = dict(
        r0=pltpu.VMEM((RING, 4, B, A, R, 128), BF),
        rx=pltpu.VMEM((n, B - 1, 4, A, R, 128), BF),
        rz=pltpu.VMEM((n, A - 1, 4, R, 128), BF),
        ryx=pltpu.VMEM((n, Y, 4, R, 128), BF),
        s_core=pltpu.SemaphoreType.DMA((2, CHUNKS)),
        s_x=pltpu.SemaphoreType.DMA((2, CHUNKS, B - 1)),
        s_z=pltpu.SemaphoreType.DMA((2, CHUNKS)),
        s_y=pltpu.SemaphoreType.DMA((2, CHUNKS, Y - 1)),
    )
    if g.kinds == 2:
        shapes.update(
            ry=pltpu.VMEM((n, 2, B, A, R, 128), BF),
            rx2=pltpu.VMEM((n, B - 1, 2, A, R, 128), BF),
            rz2=pltpu.VMEM((n, A - 1, 2, R, 128), BF),
            rag=pltpu.VMEM((n, 2, 2, R, 128), BF),
            s_ag=pltpu.SemaphoreType.DMA((2, CHUNKS)),
        )
    return shapes


class Comm:
    def __init__(self, g, G, slots, refs, emit):
        self.g, self.G, self.slots, self.emit = g, G, slots, emit
        self.__dict__.update(refs)
        dp = lax.axis_index("dp")
        self.y = lax.axis_index("blk")
        self.c = dp % 2
        self.b = (dp // 2) % g.B
        self.a = dp // (2 * g.B)

    def dev(self, a=None, b=None, c=None, y=None):
        a = self.a if a is None else a
        b = self.b if b is None else b
        c = self.c if c is None else c
        y = self.y if y is None else y
        return ((a * self.g.B + b) * 2 + c, y)

    def partners(self):
        g = self.g
        return (
            [self.dev(c=1 - self.c)]
            + [self.dev(b=(self.b + k) % g.B) for k in range(1, g.B)]
            + [self.dev(a=(self.a + k) % g.A) for k in range(1, g.A)]
            + [self.dev(y=(self.y + k) % g.Y) for k in range(1, g.Y)]
        )

    def barrier(self):
        sem = pltpu.get_barrier_semaphore()
        others = self.partners()
        for other in others:
            pl.semaphore_signal(sem, inc=1, device_id=other, device_id_type=MESH)
        pl.semaphore_wait(sem, len(others))

    def copy(self, src, dst, sems, index, device):
        return pltpu.make_async_remote_copy(
            src_ref=src,
            dst_ref=dst,
            send_sem=sems.at[(0,) + index],
            recv_sem=sems.at[(1,) + index],
            device_id=device,
            device_id_type=MESH,
        )

    def core(self, j, kind):
        copy = self.copy(
            self.G.at[j % self.slots, 1 - self.c], self.r0.at[j % RING], self.s_core, (j,), self.dev(c=1 - self.c)
        )
        return [copy], [copy]

    def along_b(self, j, kind):
        g, i = self.g, j // self.g.kinds
        landing = self.rx2 if kind else self.rx
        cols = pl.ds(2 * self.y, 2) if kind else pl.ds(0, 4)
        copies = []
        for k in range(1, g.B):
            other = (self.b + k) % g.B
            source = self.G.at[j % self.slots, self.c, cols, other]
            copies.append(self.copy(source, landing.at[i, k - 1], self.s_x, (j, k - 1), self.dev(b=other)))
        return copies, copies

    def along_a(self, j, kind):
        g, i = self.g, j // self.g.kinds
        landing = self.rz2 if kind else self.rz
        cols = pl.ds(2 * self.y, 2) if kind else pl.ds(0, 4)
        copies = []
        for k in range(1, g.A):
            other = (self.a + k) % g.A
            source = self.G.at[j % self.slots, self.c, cols, self.b, other]
            copies.append(self.copy(source, landing.at[i, k - 1], self.s_z, (j,), self.dev(a=other)))
        return copies, [self.copy(landing.at[i], landing.at[i], self.s_z, (j,), self.dev(a=(self.a + 1) % g.A))]

    def along_blk(self, j, kind):
        g, i = self.g, j // self.g.kinds
        if kind:
            source = self.G.at[j % self.slots, self.c, pl.ds(2 * (1 - self.y), 2)]
            copies = [self.copy(source, self.ry.at[i], self.s_y, (j, 0), self.dev(y=1 - self.y))]
            return copies, copies
        mine = self.ryx.at[i, self.y]
        copies = [
            self.copy(mine, mine, self.s_y, (j, k - 1), self.dev(y=(self.y + k) % g.Y)) for k in range(1, g.Y)
        ]
        return copies, copies

    def share(self, j, kind):
        mine = self.rag.at[j // 2, self.y]
        copies = [self.copy(mine, mine, self.s_ag, (j,), self.dev(y=1 - self.y))]
        return copies, copies

    def add(self, mine, parts):
        if len(parts) == 1:
            mine[...] = mine[...] + parts[0]
        else:
            mine[...] = self.summed(mine, parts)

    def summed(self, mine, parts):
        total = mine[...].astype(F32)
        for part in parts:
            total = total + part.astype(F32)
        return total.astype(BF)

    def after_core(self, j, kind):
        self.add(self.G.at[j % self.slots, self.c], [self.r0[j % RING]])

    def after_b(self, j, kind):
        g, i = self.g, j // self.g.kinds
        landing = self.rx2 if kind else self.rx
        cols = pl.ds(2 * self.y, 2) if kind else pl.ds(0, 4)
        self.add(self.G.at[j % self.slots, self.c, cols, self.b], [landing[i, k] for k in range(g.B - 1)])

    def after_a(self, j, kind):
        g, i = self.g, j // self.g.kinds
        landing = self.rz2 if kind else self.rz
        cols = pl.ds(2 * self.y, 2) if kind else pl.ds(0, 4)
        total = self.summed(
            self.G.at[j % self.slots, self.c, cols, self.b, self.a], [landing[i, k] for k in range(g.A - 1)]
        )
        if kind:
            self.rag[i, self.y] = total
        else:
            self.ryx[i, self.y] = total

    def after_blk(self, j, kind):
        g, i = self.g, j // self.g.kinds
        if kind:
            self.add(self.G.at[j % self.slots, self.c, pl.ds(2 * self.y, 2)], [self.ry[i]])
            return
        total = self.ryx[i, 0].astype(F32)
        for k in range(1, g.Y):
            total = total + self.ryx[i, k].astype(F32)
        self.emit(j, [total[col] for col in range(4)])

    def after_share(self, j, kind):
        i = j // 2
        self.emit(j, [self.rag[i, col // 2, col % 2].astype(F32) for col in range(4)])

    def plan(self, kind):
        core = (self.core, self.after_core)
        b = (self.along_b, self.after_b)
        a = (self.along_a, self.after_a)
        blk = (self.along_blk, self.after_blk)
        share = (self.share, self.after_share)
        return (core, blk, b, a, share) if kind else (core, b, a, blk)

    def start(self, j):
        self.core(j, 0)[0][0].start()

    def finish(self, stage, j):
        for kind in range(self.g.kinds):
            plan = self.plan(kind)
            if stage >= len(plan):
                continue

            def go(kind=kind, plan=plan):
                for copy in plan[stage][0](j, kind)[1]:
                    copy.wait()
                plan[stage][1](j, kind)
                if stage + 1 < len(plan):
                    for copy in plan[stage + 1][0](j, kind)[0]:
                        copy.start()

            if self.g.kinds == 1:
                go()
            elif isinstance(j, int):
                if (j + (j >= CHUNKS - 2)) % 2 == kind:
                    go()
            else:
                pl.when(jnp.where(j >= CHUNKS - 2, j + 1, j) % 2 == kind)(go)

    def advance(self, t):
        for stage in range(5):
            twice = t - AFTER[stage]
            if twice % 2 == 0 and 0 <= twice < 2 * CHUNKS:
                self.finish(stage, twice // 2)

    def advance_two(self, t, odd):
        for stage in range(5):
            if (odd - AFTER[stage]) % 2 == 0:
                j = t + (odd - AFTER[stage]) // 2

                @pl.when((j >= 0) & (j < CHUNKS))
                def _(stage=stage, j=j):
                    self.finish(stage, j)


def emit_to(g, j_ref, o_ref, e_ref, r_ref):
    R = g.R

    def emit(j, values):
        @pl.when(j < 6)
        def _():
            for col in range(4):
                e_ref[:, pl.ds(pl.multiple_of(j * 512 + col * 128, 128), 128)] = values[col]

        @pl.when((j >= 6) & (j < 12))
        def _():
            for k in range(4):
                r_ref[k * R : (k + 1) * R, pl.ds(pl.multiple_of((j - 6) * 128, 128), 128)] = values[k]

        @pl.when(j >= 12)
        def _():
            at = pl.multiple_of((j - 12) * 128, 128)
            for k in range(3):
                j_ref[:, pl.ds(pl.multiple_of(k * 768 + at, 128), 128)] = values[k]
            o_ref[:, pl.ds(at, 128)] = values[3]

    return emit


HEADS = 12
VECTORS = (
    "entry_gain", "entry_shift", "joint_bias", "output_bias",
    "middle_gain", "middle_shift", "expand_bias", "reduce_bias",
)
HD = 64
D = 768
FF = 3072
ROWS = 512
EDGE = 128
SPAN = 3 * EDGE
PAIRS = HEADS // 2
NEAR = 112
SLOTS = 12
STREAM = 2
TICK = 512
TICKS = FF // TICK


def nn(left, right):
    return jnp.dot(left, right, preferred_element_type=F32)


def nt(left, right):
    return lax.dot_general(left, right, (((1,), (1,)), ((), ())), preferred_element_type=F32)


def stats(values):
    average = jnp.mean(values, axis=-1, keepdims=True)
    centred = values - average
    spread = jnp.mean(centred * centred, axis=-1, keepdims=True)
    inverse = lax.rsqrt(spread + 1e-06)
    return centred * inverse, inverse


def normal_parts(hidden):
    half = hidden * (0.5**0.5)
    size = jnp.abs(half)
    ratio = 1.0 / (1.0 + 0.3275911 * size)
    bell = jnp.exp(-half * half)
    tail = ((((1.061405429 * ratio - 1.453152027) * ratio + 1.421413741) * ratio - 0.284496736) * ratio + 0.254829592) * ratio
    tail = 0.5 * tail * bell
    share = jnp.where(hidden >= 0, 1.0 - tail, tail)
    return share, hidden * bell * 0.3989422804014327


def column_sum(values):
    return jnp.sum(values, axis=0, keepdims=True)


def layer_kernel(g, names, *refs):
    r = dict(zip(names, refs))
    A, B, R, Y = g.A, g.B, g.R, g.Y
    (patches, cotangent, segments, w_joint, w_output, w_expand, w_reduce) = (
        r[n] for n in ("patches", "cotangent", "segments", "w_joint", "w_output", "w_expand", "w_reduce")
    )
    G, vec = r["G"], r["vec"]
    for name in VECTORS:
        r[name + "_row"][...] = r[name][...].reshape(1, -1)
        r[name] = r[name + "_row"]
    r["oe"], r["oo"] = r["vT"], r["n2"]
    out_rows, dx_rows = r["k"].at[pl.ds(0, ROWS)], r["ml"]
    x, xh, dy = r["x"], r["xh"], r["dy"]
    comm = Comm(g, G, SLOTS, r, emit_to(g, r["j_out"], r["o_out"], r["e_sum"], r["r_sum"]))
    y = comm.y
    has_left, has_right = y > 0, y < Y - 1

    def load(src, dst, k):
        return pltpu.make_async_copy(src, dst, r["load"].at[k])

    load_x = load(patches, x, 0)
    load_wj = load(w_joint, r["wj"], 1)
    load_wo = load(w_output, r["wo"], 2)
    load_dy = load(cotangent, dy, 3)

    def ffn_loads(i):
        s = i % STREAM
        at = pl.ds(pl.multiple_of(i * TICK, TICK), TICK)
        return (
            pltpu.make_async_copy(w_expand.at[:, at], r["we"].at[s], r["stream"].at[0, s]),
            pltpu.make_async_copy(w_reduce.at[at], r["wr"].at[s], r["stream"].at[1, s]),
        )

    load_x.start()
    load_wj.start()
    comm.barrier()

    def edge(k, side, src, dst, sems):
        other = comm.dev(y=(y + Y - 1) % Y) if side == 0 else comm.dev(y=(y + 1) % Y)
        return pltpu.make_async_remote_copy(
            src_ref=src, dst_ref=dst, send_sem=sems.at[(0,) + k + (side,)], recv_sem=sems.at[(1,) + k + (1 - side,)],
            device_id=other, device_id_type=MESH,
        )

    def x_edges():
        return (
            edge((), 0, patches.at[pl.ds(0, NEAR)], xh.at[1, pl.ds(0, NEAR)], r["s_edge"]),
            edge((), 1, patches.at[pl.ds(ROWS - NEAR, NEAR)], xh.at[0, pl.ds(EDGE - NEAR, NEAR)], r["s_edge"]),
        )

    to_left, to_right = x_edges()

    @pl.when(has_left)
    def _():
        to_left.start()

    @pl.when(has_right)
    def _():
        to_right.start()

    xh[0, 0 : EDGE - NEAR, :] = jnp.zeros((EDGE - NEAR, D), BF)
    xh[1, NEAR:EDGE, :] = jnp.zeros((EDGE - NEAR, D), BF)

    first_block = y * (ROWS // EDGE)
    count = segments.shape[0]
    columns = []
    for k in range(6):
        index = first_block + k - 1
        inside = (index >= 0) & (index < count)
        row = segments[pl.ds(jnp.clip(index, 0, count - 1), 1), :]
        row = jnp.where(inside, row, -1)
        columns.append(row)
    for b in range(4):
        for k in range(3):
            keys = jnp.broadcast_to(columns[b + k].astype(F32), (EDGE, EDGE)).T
            own = columns[b + 1].astype(F32)
            r["bias"][b, k * EDGE : (k + 1) * EDGE, :] = jnp.where(keys == own, 0.0, -1e30)

    vec[...] = jnp.zeros_like(vec)
    r["dn"][...] = jnp.zeros((ROWS, D), F32)
    entry_gain, entry_shift = r["entry_gain"][...], r["entry_shift"][...]
    lanes = lax.broadcasted_iota(jnp.int32, (1, D), 1) % 128
    even = lanes < HD

    def project(rows, at, own, row_at):
        count = rows.shape[0]
        normal, _ = stats(rows.astype(F32))
        low = (normal * entry_gain + entry_shift).astype(BF)
        wj = r["wj"]
        key_rows = nn(low, wj[:, D : 2 * D]).astype(BF)
        r["k"][pl.ds(at, count), :] = key_rows
        value_rows = (nn(low, wj[:, 2 * D :]) + r["joint_bias"][:, D:]).astype(BF)
        r["v"][pl.ds(at, count), :] = value_rows
        r["vT"][:, pl.ds(at, count)] = value_rows.T
        if own:
            r["ml"][pl.ds(row_at, count), :] = low
            queries = (nn(low, wj[:, :D]) + r["joint_bias"][:, :D]).astype(BF) * BF(HD**-0.5)
            r["qe"][pl.ds(row_at, count), :] = jnp.where(even, queries, BF(0))
            r["qo"][pl.ds(row_at, count), :] = jnp.where(even, BF(0), queries)

    load_x.wait()
    load_wj.wait()
    load_wo.start()
    load_dy.start()
    for i in range(STREAM):
        for copy in ffn_loads(i):
            copy.start()

    def own_rows(i, _):
        at = pl.multiple_of(i * 256, 256)
        project(x[pl.ds(at, 256), :], pl.multiple_of(at + EDGE, EDGE), True, at)
        return 0

    lax.fori_loop(0, 2, own_rows, 0)

    @pl.when(has_left)
    def _():
        to_left.wait_send()
        to_right.wait_recv()

    @pl.when(has_right)
    def _():
        to_right.wait_send()
        to_left.wait_recv()

    def edge_rows(i, _):
        at = pl.multiple_of(i * (ROWS + EDGE), EDGE)
        present = jnp.where(i == 0, y, Y - 1 - y) > 0

        @pl.when(present)
        def _():
            project(xh[i], at, False, 0)

        @pl.when(jnp.logical_not(present))
        def _():
            r["k"][pl.ds(at, EDGE), :] = jnp.zeros((EDGE, D), BF)
            r["v"][pl.ds(at, EDGE), :] = jnp.zeros((EDGE, D), BF)
            r["vT"][:, pl.ds(at, EDGE)] = jnp.zeros((D, EDGE), BF)

        return 0

    lax.fori_loop(0, 2, edge_rows, 0)

    top = lax.broadcasted_iota(jnp.int32, (EDGE, 1), 0) < HD

    def scores_of(p, b):
        at = pl.ds(pl.multiple_of(p * 128, 128), 128)
        keys, own = pl.ds(b * EDGE, SPAN), pl.ds(b * EDGE, EDGE)
        both = jnp.concatenate([r["qe"][own, at], r["qo"][own, at]], axis=0)
        return nt(r["k"][keys, at], both)

    def probs_of(b, scores):
        bias = r["bias"][b]
        scores = scores + jnp.concatenate([bias, bias], axis=1)
        powers = jnp.exp(scores - jnp.max(scores, axis=0, keepdims=True))
        return (powers * (1.0 / column_sum(powers))).astype(BF)

    def mix(p, b, probs):
        at = pl.ds(pl.multiple_of(p * 128, 128), 128)
        keys, own = pl.ds(b * EDGE, SPAN), pl.ds(b * EDGE, EDGE)
        r["probs"][p, b] = probs
        mixed = nn(r["vT"][at, keys], probs)
        r["attT"][at, own] = jnp.where(top, mixed[:, :128], mixed[:, 128:]).astype(BF)

    def attend(i, _):
        blocks = [(2 * i + pair, b) for pair in range(2) for b in range(4)]
        scores = scores_of(*blocks[0])
        before = None
        for k, (p, b) in enumerate(blocks):
            following = scores_of(*blocks[k + 1]) if k + 1 < len(blocks) else None
            probs = probs_of(b, scores)
            if k > 0:
                mix(*blocks[k - 1], before)
            before, scores = probs, following
        mix(*blocks[-1], before)
        return 0

    lax.fori_loop(0, PAIRS // 2, attend, 0)

    load_wo.wait()
    mid, total, n2, n2T = r["mid"], r["total"], r["n2"], r["n2T"]
    middle_gain, middle_shift = r["middle_gain"][...], r["middle_shift"][...]

    halves = [pl.ds(i * 256, 256) for i in range(2)]
    middles = [
        x[at, :].astype(F32) + nn(r["attT"][:, at].T, r["wo"][...]) + r["output_bias"][...] for at in halves
    ]
    for at, middle in zip(halves, middles):
        mid[at, :] = middle
        total[at, :] = middle + r["reduce_bias"][...]
        normal, _ = stats(middle)
        low = (normal * middle_gain + middle_shift).astype(BF)
        n2[at, :] = low
        n2T[:, at] = low.T
    load_dy.wait()

    def feed_forward(i, _):
        s = i % STREAM
        for copy in ffn_loads(i):
            copy.wait()
        we, wr = r["we"].at[s], r["wr"].at[s]
        at = pl.ds(pl.multiple_of(i * TICK, TICK), TICK)
        bias = r["expand_bias"][:, at]
        bias_sum = jnp.zeros((1, TICK), F32)
        rows = [pl.ds(half * 256, 256) for half in range(2)]
        hidden = [nn(n2[part, :], we[...]) + bias for part in rows]
        back = [nt(dy[part, :], wr[...]) for part in rows]
        for half, part in enumerate(rows):
            share, slope = normal_parts(hidden[half])
            active = (hidden[half] * share).astype(BF)
            hidden_gradient = back[half] * (share + slope)
            bias_sum = bias_sum + column_sum(hidden_gradient)
            low = hidden_gradient.astype(BF)
            r["hl"][part, :] = low
            r["actT"][at, part] = active.T
            total[part, :] += nn(active, wr[...])
            r["dn"][part, :] += nt(low, we[...])
        r["eb"][:, at] = bias_sum
        for part in range(2):
            block = nn(n2T[part * 384 : (part + 1) * 384, :], r["hl"][...]).astype(BF)
            store_rows(block, i, part * 2, 2)
        comm.start(i)

        @pl.when(i + STREAM < TICKS)
        def _():
            for copy in ffn_loads(i + STREAM):
                copy.start()

        comm.advance_two(i, 0)
        return 0

    def store_rows(block, chunk, a0, na):
        slot = chunk % SLOTS
        for a in range(na):
            for b in range(B):
                for c in range(2):
                    row = ((a * B + b) * 2 + c) * R
                    for col in range(block.shape[1] // 128):
                        G[slot, c, col, b, a0 + a] = block[row : row + R, col * 128 : (col + 1) * 128]

    lax.fori_loop(0, TICKS, feed_forward, 0)

    def turn(i, _):
        at = pl.ds(pl.multiple_of(i * 256, 256), 256)
        r["kT"][:, at] = r["k"][at, :].T

        @pl.when(i < 2)
        def _():
            r["n1T"][:, at] = r["ml"][at, :].T

        return 0

    lax.fori_loop(0, 3, turn, 0)

    def reduce_gradient(p, _):
        at = pl.ds(pl.multiple_of(p * 256, 256), 256)
        chunk = 6 + 2 * p

        def part(a, _):
            block = nn(r["actT"][pl.ds(pl.multiple_of(a * D, D), D), :], dy[:, at]).astype(BF)
            for h in range(2):
                slot = (chunk + h) % SLOTS
                for b in range(B):
                    for c in range(2):
                        for k in range(4):
                            row = ((b * 2 + c) * 4 + k) * R
                            G[slot, c, k, b, a] = block[row : row + R, h * 128 : (h + 1) * 128]
            return 0

        lax.fori_loop(0, A, part, 0)
        comm.start(chunk)
        comm.start(chunk + 1)
        comm.advance_two(6 + p, 0)
        return 0

    lax.fori_loop(0, 3, reduce_gradient, 0)

    def middle_back(i, _):
        at = pl.ds(pl.multiple_of(i * 256, 256), 256)
        out_rows[at, :] = total[at, :].astype(BF)
        error = r["dn"][at, :]
        normal, inverse = stats(mid[at, :])
        scaled = error * middle_gain
        part = inverse * (
            scaled
            - jnp.mean(scaled, axis=-1, keepdims=True)
            - normal * jnp.mean(scaled * normal, axis=-1, keepdims=True)
        )
        incoming = dy[at, :].astype(F32)
        gradient = incoming + part
        vec[5:6, :] += column_sum(error * normal)
        vec[6:7, :] += column_sum(error)
        vec[4:5, :] += column_sum(gradient)
        vec[11:12, :] += column_sum(incoming)
        mid[at, :] = gradient
        low = gradient.astype(BF)
        r["ml"][at, :] = low
        back = nt(low, r["wo"][...]).astype(BF)
        r["oe"][at, :] = jnp.where(even, back, BF(0))
        r["oo"][at, :] = jnp.where(even, BF(0), back)
        total[at, :] = jnp.zeros((256, D), F32)
        return 0

    lax.fori_loop(0, 2, middle_back, 0)
    save_out = pltpu.make_async_copy(out_rows, r["out"], r["save"].at[0])
    save_out.start()
    for k in range(4):
        vec[7 + k : 8 + k, :] = r["eb"][:, k * D : (k + 1) * D]
    comm.advance(17)
    comm.advance(18)

    place = lax.axis_index("dp")
    n2v, n4v = g.dp // 2, g.dp // 4
    lane = lax.broadcasted_iota(jnp.int32, (1, ROWS), 1)
    want = jnp.where(
        lane < 128,
        lane + place * R,
        jnp.where(lane < 256, lane - 128 + (place % n2v) * (2 * R), lane - 256 + (place % n4v) * (4 * R)),
    )
    spot = lax.broadcasted_iota(jnp.int32, (D, ROWS), 0)
    r["n2T"][...] = jnp.where(spot == want, 1.0, 0.0).astype(BF)

    parts, jq, sent, got, s_part = r["parts"], r["jq"], r["sent"], r["got"], r["s_part"]

    def part_copies(p):
        return (
            edge((p,), 0, sent.at[p % 2, 0], got.at[p, 1], s_part),
            edge((p,), 1, sent.at[p % 2, 1], got.at[p, 0], s_part),
        )

    def attend_back(p):
        at = pl.ds(pl.multiple_of(p * 128, 128), 128)
        slot = p % 2
        own_sum = jnp.zeros((1, 128), F32)
        parts[slot] = jnp.zeros((ROWS + 2 * EDGE, 256), F32)

        def errors_of(b):
            own = pl.ds(b * EDGE, EDGE)
            return jnp.concatenate([r["oe"][own, at], r["oo"][own, at]], axis=0)

        def shares_of(b):
            return nt(r["v"][pl.ds(b * EDGE, SPAN), at], errors_of(b))

        def score_gradient_of(b, shares):
            wide = r["probs"][p, b].astype(F32)
            product = wide * shares
            return (product - wide * column_sum(product)).astype(BF)

        def spread(b, low):
            keys, own = pl.ds(b * EDGE, SPAN), pl.ds(b * EDGE, EDGE)
            queries = jnp.concatenate([r["qe"][own, at], r["qo"][own, at]], axis=0)
            parts[slot, keys, 0:128] += nn(low, queries)
            parts[slot, keys, 128:256] += nn(r["probs"][p, b], errors_of(b))
            turned = nn(r["kT"][at, keys], low)
            mine = (jnp.where(top, turned[:, :128], turned[:, 128:]) * HD**-0.5).T
            jq[slot, own, :] = mine.astype(BF)
            return column_sum(mine)

        to_left, to_right = part_copies(p)

        def send_edges():
            @pl.when(has_left)
            def _():
                sent[slot, 0] = parts[slot, EDGE - NEAR : EDGE, :].astype(BF)
                to_left.start()

            @pl.when(has_right)
            def _():
                sent[slot, 1] = parts[slot, ROWS + EDGE : ROWS + EDGE + NEAR, :].astype(BF)
                to_right.start()

        order = (0, 3, 1, 2)
        shares = shares_of(order[0])
        before = None
        for step, b in enumerate(order):
            following = shares_of(order[step + 1]) if step < 3 else None
            low = score_gradient_of(b, shares)
            if step > 0:
                own_sum = own_sum + spread(order[step - 1], before)
            if step == 2:
                send_edges()
            before, shares = low, following
        own_sum = own_sum + spread(order[3], before)
        vec[2:3, at] = own_sum

    def joint_gradient(p):
        at = pl.ds(pl.multiple_of(p * 128, 128), 128)
        slot = p % 2
        to_left, to_right = part_copies(p)

        @pl.when(has_left)
        def _():
            to_left.wait_send()
            to_right.wait_recv()
            parts[slot, EDGE : EDGE + NEAR, :] += got[p, 0].astype(F32)

        @pl.when(has_right)
        def _():
            to_right.wait_send()
            to_left.wait_recv()
            parts[slot, ROWS + EDGE - NEAR : ROWS + EDGE, :] += got[p, 1].astype(F32)

        sums = parts[slot, EDGE : ROWS + EDGE, :]
        vec[3:4, at] = column_sum(sums[:, 128:])
        low = jnp.concatenate([jq[slot], sums.astype(BF)], axis=1)
        wj = r["wj"]
        weights = jnp.concatenate([wj[:, pl.ds(pl.multiple_of(k * D + p * 128, 128), 128)] for k in range(3)], axis=1)
        total[...] += nt(low, weights)
        low_out = r["ml"][:, at]
        for part in range(2):
            rows = pl.ds(part * 384, 384)
            block = nn(r["n1T"][rows, :], low).astype(BF)
            block_out = nn(r["attT"][rows, :], low_out).astype(BF)
            store_rows(jnp.concatenate([block, block_out], axis=1), 12 + p, part * 2, 2)
        comm.start(12 + p)

    def pair_step(i, _):
        @pl.when(i < PAIRS)
        def _():
            attend_back(i)

        @pl.when(i > 0)
        def _():
            joint_gradient(i - 1)

        comm.advance_two(10 + i, 0)
        return 0

    lax.fori_loop(0, PAIRS + 1, pair_step, 0)

    def entry_back(i, _):
        at = pl.ds(pl.multiple_of(i * 256, 256), 256)
        error = total[at, :]
        normal, inverse = stats(x[at, :].astype(F32))
        scaled = error * entry_gain
        part = inverse * (
            scaled
            - jnp.mean(scaled, axis=-1, keepdims=True)
            - normal * jnp.mean(scaled * normal, axis=-1, keepdims=True)
        )
        vec[0:1, :] += column_sum(error * normal)
        vec[1:2, :] += column_sum(error)
        dx_rows[at, :] = (mid[at, :] + part).astype(BF)
        return 0

    lax.fori_loop(0, 2, entry_back, 0)
    save_dx = pltpu.make_async_copy(dx_rows, r["dx"], r["save"].at[1])
    save_dx.start()

    rv, s_vec = r["rv"], r["s_vec"]

    def vector_copies(step):
        groups = (
            [comm.dev(c=1 - comm.c)],
            [comm.dev(b=(comm.b + k) % B) for k in range(1, B)],
            [comm.dev(a=(comm.a + k) % A) for k in range(1, A)],
            [comm.dev(y=(comm.y + k) % Y) for k in range(1, Y)],
        )
        ids = (comm.c, comm.b, comm.a, comm.y)
        base = (0, 2, 0, A)[step]
        held = rv if step < 2 else r["rvl"]
        here = held.at[base + ids[step]]
        return here, [
            comm.copy(here, here, s_vec, ((0, 2, 2 + B, 2 + B + A)[step] + k,), other) for k, other in enumerate(groups[step])
        ]

    def vector_sum(step):
        base, size = ((0, 2), (2, B), (0, A), (A, Y))[step]
        held = rv if step < 2 else r["rvl"]
        value = held[base].astype(F32)
        for k in range(1, size):
            value = value + held[base + k].astype(F32)
        return value

    def vector_start(step, value):
        here, copies = vector_copies(step)
        here[...] = value.astype(here.dtype)
        for copy in copies:
            copy.start()

    def vector_wait(step):
        for copy in vector_copies(step)[1]:
            copy.wait()

    def pick_vectors():
        summed = vector_sum(3)
        high = summed.astype(BF)
        rest = (summed - high.astype(F32)).astype(BF)
        picked = nn(high, r["n2T"][...]) + nn(rest, r["n2T"][...])
        kind = lax.broadcasted_iota(jnp.int32, (16, 1), 0)
        r["v_out"][...] = picked[:, 0:128]
        r["jb_out"][...] = column_sum(jnp.where(kind == 2 + place // n2v, picked[:, 128:256], 0.0))
        r["eb_out"][...] = column_sum(jnp.where(kind == 7 + place // n4v, picked[:, 256:512], 0.0))

    save_e = pltpu.make_async_copy(r["e_sum"], r["e_out"], r["save"].at[2])
    save_r = pltpu.make_async_copy(r["r_sum"], r["r_out"], r["save"].at[3])
    vector_start(0, vec[...])
    for t in range(34, 2 * CHUNKS + AFTER[4] - 1, 2):
        comm.advance(t)
        if t in VECTOR_STEPS:
            step = VECTOR_STEPS.index(t)
            vector_wait(step)
            if step < 3:
                vector_start(step + 1, vector_sum(step))
            else:
                pick_vectors()
        if t == 2 * 11 + AFTER[4]:
            save_e.start()
            save_r.start()
    save_e.wait()
    save_r.wait()
    save_out.wait()
    save_dx.wait()


def layer(g, patches, segments, vectors, weights, cotangent):
    A, B, R, Y = g.A, g.B, g.R, g.Y
    comm_shapes = comm_scratch(g)
    V = pl.BlockSpec(memory_space=pltpu.VMEM)
    H = pl.BlockSpec(memory_space=pl.ANY)
    inputs = dict(
        patches=(patches, H),
        cotangent=(cotangent, H),
        segments=(segments, V),
        w_joint=(weights[0], H),
        w_output=(weights[1], H),
        w_expand=(weights[2], H),
        w_reduce=(weights[3], H),
        **{name: (value, V) for name, value in vectors.items()},
    )
    outputs = dict(
        out=((ROWS, D), BF),
        dx=((ROWS, D), BF),
        j_out=((R, 3 * D), F32),
        o_out=((R, D), F32),
        e_out=((R, FF), F32),
        r_out=((4 * R, D), F32),
        v_out=((16, 128), F32),
        jb_out=((1, 128), F32),
        eb_out=((1, 256), F32),
    )
    ext = ROWS + 2 * EDGE
    scratch = dict(
        x=pltpu.VMEM((ROWS, D), BF),
        xh=pltpu.VMEM((2, EDGE, D), BF),
        dy=pltpu.VMEM((ROWS, D), BF),
        wj=pltpu.VMEM((D, 3 * D), BF),
        wo=pltpu.VMEM((D, D), BF),
        we=pltpu.VMEM((STREAM, D, TICK), BF),
        wr=pltpu.VMEM((STREAM, TICK, D), BF),
        n1T=pltpu.VMEM((D, ROWS), BF),
        qe=pltpu.VMEM((ROWS, D), BF),
        qo=pltpu.VMEM((ROWS, D), BF),
        k=pltpu.VMEM((ext, D), BF),
        v=pltpu.VMEM((ext, D), BF),
        kT=pltpu.VMEM((D, ext), BF),
        vT=pltpu.VMEM((D, ext), BF),
        bias=pltpu.VMEM((4, SPAN, EDGE), F32),
        probs=pltpu.VMEM((PAIRS, 4, SPAN, 2 * EDGE), BF),
        attT=pltpu.VMEM((D, ROWS), BF),
        mid=pltpu.VMEM((ROWS, D), F32),
        total=pltpu.VMEM((ROWS, D), F32),
        dn=pltpu.VMEM((ROWS, D), F32),
        n2=pltpu.VMEM((ROWS, D), BF),
        n2T=pltpu.VMEM((D, ROWS), BF),
        hl=pltpu.VMEM((ROWS, TICK), BF),
        actT=pltpu.VMEM((FF, ROWS), BF),
        eb=pltpu.VMEM((1, FF), F32),
        ml=pltpu.VMEM((ROWS, D), BF),
        parts=pltpu.VMEM((2, ext, 256), F32),
        jq=pltpu.VMEM((2, ROWS, 128), BF),
        sent=pltpu.VMEM((2, 2, NEAR, 256), BF),
        got=pltpu.VMEM((PAIRS, 2, NEAR, 256), BF),
        vec=pltpu.VMEM((16, D), F32),
        rv=pltpu.VMEM((2 + B, 16, D), F32),
        rvl=pltpu.VMEM((A + Y, 16, D), BF),
        G=pltpu.VMEM((SLOTS, 2, 4, B, A, R, 128), BF),
        load=pltpu.SemaphoreType.DMA((4,)),
        save=pltpu.SemaphoreType.DMA((4,)),
        e_sum=pltpu.VMEM((R, FF), F32),
        r_sum=pltpu.VMEM((4 * R, D), F32),
        stream=pltpu.SemaphoreType.DMA((2, STREAM)),
        s_edge=pltpu.SemaphoreType.DMA((2, 2)),
        s_part=pltpu.SemaphoreType.DMA((2, PAIRS, 2)),
        s_vec=pltpu.SemaphoreType.DMA((2, 2 + B + A + Y)),
        **{name + "_row": pltpu.VMEM((1, value.shape[0]), F32) for name, value in vectors.items()},
        **comm_shapes,
    )
    names = (*inputs, *outputs, *scratch)
    results = pl.pallas_call(
        functools.partial(layer_kernel, g, names),
        out_shape=tuple(jax.ShapeDtypeStruct(*shape) for shape in outputs.values()),
        in_specs=[spec for _, spec in inputs.values()],
        out_specs=[H if name in ("out", "dx", "e_out", "r_out") else V for name in outputs],
        scratch_shapes=list(scratch.values()),
        compiler_params=pltpu.CompilerParams(
            collective_id=0, has_side_effects=True, vmem_limit_bytes=64 << 20
        ),
    )(*(value for value, _ in inputs.values()))
    return hand_over(g, dict(zip(outputs, results)))


def hand_over_kernel(g, out, dx, j, o, e, w, v, jb, eb, *refs):
    outs, held, sems = refs[:14], refs[14:20], refs[20]
    R = g.R
    moves = [(out, 0), (dx, 1), (j, 4), (o, 6), (e, 10), (w, 12)]
    loads = [pltpu.make_async_copy(src, held[i], sems.at[0, i]) for i, (src, _) in enumerate(moves)]
    copies = [pltpu.make_async_copy(held[i], outs[k], sems.at[1, i]) for i, (_, k) in enumerate(moves)]
    for load in loads:
        load.start()
    for load, copy in zip(loads, copies):
        load.wait()
        copy.start()
    for row, k in ((0, 2), (1, 3), (4, 7), (5, 8), (6, 9), (11, 13)):
        outs[k][...] = v[row, :R]
    outs[5][...] = jb[0, : 2 * R]
    outs[11][...] = eb[0, : 4 * R]
    for copy in copies:
        copy.wait()


def hand_over(g, o):
    R = g.R
    V = pl.BlockSpec(memory_space=pltpu.VMEM)
    H = pl.BlockSpec(memory_space=pl.ANY)
    shapes = [
        ((ROWS, D), BF), ((ROWS, D), BF), ((R,), F32), ((R,), F32), ((R, 3 * D), F32), ((2 * R,), F32), ((R, D), F32),
        ((R,), F32), ((R,), F32), ((R,), F32), ((R, FF), F32), ((4 * R,), F32), ((4 * R, D), F32), ((R,), F32),
    ]
    names = ("out", "dx", "j_out", "o_out", "e_out", "r_out", "v_out", "jb_out", "eb_out")
    return pl.pallas_call(
        functools.partial(hand_over_kernel, g),
        out_shape=tuple(jax.ShapeDtypeStruct(*shape) for shape in shapes),
        in_specs=[H] * 6 + [V] * 3,
        out_specs=[V if len(shape) == 1 else H for shape, _ in shapes],
        scratch_shapes=[
            *(pltpu.VMEM(o[name].shape, o[name].dtype) for name in names[:6]),
            pltpu.SemaphoreType.DMA((2, 6)),
        ],
    )(*(o[name] for name in names))


def local(
    patches,
    segments,
    entry_gain,
    entry_shift,
    joint_weight,
    joint_bias,
    output_weight,
    output_bias,
    middle_gain,
    middle_shift,
    expand_weight,
    expand_bias,
    reduce_weight,
    reduce_bias,
    cotangent,
):
    g = Grid(lax.axis_size("dp"), lax.axis_size("blk"), D)
    R = g.R
    vectors = dict(
        entry_gain=entry_gain,
        entry_shift=entry_shift,
        joint_bias=joint_bias,
        output_bias=output_bias,
        middle_gain=middle_gain,
        middle_shift=middle_shift,
        expand_bias=expand_bias,
        reduce_bias=reduce_bias,
    )
    o = layer(
        g,
        patches[0],
        segments.reshape(-1, EDGE),
        vectors,
        (joint_weight, output_weight, expand_weight, reduce_weight),
        cotangent[0],
    )
    return (o[0][None], o[1][None], *o[2:])


def solution(mesh):
    return jax.shard_map(
        local,
        mesh=mesh,
        in_specs=(
            P("dp", "blk", None),
            P("dp", None),
            P(),
            P(),
            P(),
            P(),
            P(),
            P(),
            P(),
            P(),
            P(),
            P(),
            P(),
            P(),
            P("dp", "blk", None),
        ),
        out_specs=(
            P("dp", "blk", None),
            P("dp", "blk", None),
            P("dp"),
            P("dp"),
            P("dp", None),
            P("dp"),
            P("dp", None),
            P("dp"),
            P("dp"),
            P("dp"),
            P("dp", None),
            P("dp"),
            P("dp", None),
            P("dp"),
        ),
        check_vma=False,
    )
```
